32 devices in a mesh: batch: 8 (over y, x, core), rows: 4 (over z).
Axes of the slice: x: 2, y: 2, z: 4, core: 2. Of those that a mesh axis runs over, the one named last changes fastest.
Arguments:
- images: bfloat16 [32, 32, 32, 192], P('batch', 'rows'), may hold values from -6 to 6
- w_qkv: bfloat16 [192, 576], P('batch'), may hold values from -0.4375 to 0.4375
- w_proj: bfloat16 [192, 192], P('batch'), may hold values from -0.4375 to 0.4375
- w_up: bfloat16 [192, 768], P('batch'), may hold values from -0.4375 to 0.4375
- w_down: bfloat16 [768, 192], P('batch'), may hold values from -0.21875 to 0.21875
- gains_main: bfloat16 [2, 192], replicated, may hold values from 0.5 to 1.5
- shifts_main: bfloat16 [11, 192], replicated, may hold values from -1.25 to 1.25
- pool_kernels: bfloat16 [3, 9, 96], replicated, may hold values from -2 to 2
- pool_gains: bfloat16 [3, 96], replicated, may hold values from 0.5 to 1.5
- pool_shifts: bfloat16 [2, 96], replicated, may hold values from -1.75 to 1.75
- rel_height: bfloat16 [63, 96], replicated, may hold values from -0.625 to 0.625
- rel_width: bfloat16 [63, 96], replicated, may hold values from -0.625 to 0.625
- cotangent: bfloat16 [32, 32, 32, 192], P('batch', 'rows'), may hold values from -6 to 6
Outputs:
- output: bfloat16 [32, 32, 32, 192], P('batch', 'rows')
- grad_images: float32 [32, 32, 32, 192], P('batch', 'rows')
- grad_w_qkv: float32 [192, 576], P('batch')
- grad_w_proj: float32 [192, 192], P('batch')
- grad_w_up: float32 [192, 768], P('batch')
- grad_w_down: float32 [768, 192], P('batch')
- grad_gains_main: float32 [2, 192], replicated
- grad_shifts_main: float32 [11, 192], replicated
- grad_pool_kernels: float32 [3, 9, 96], replicated
- grad_pool_gains: float32 [3, 96], replicated
- grad_pool_shifts: float32 [2, 96], replicated
- grad_rel_height: float32 [63, 96], replicated
- grad_rel_width: float32 [63, 96], replicated
The draws below stay inside these ranges and needn't reach their ends.
All inputs are finite; a program needn't handle non-finite values.
Results may differ from the reference program's by a relative error of at most 0.017.
Values may be sent and summed in bfloat16 or wider, within the bound.
No kernel may reach another device: no remote copies, remote signals or barrier semaphores. Data moves between devices by JAX's collectives and lax.ppermute only.
A program may use at most 128 MiB of HBM per device.

```python
import jax
import jax.numpy as jnp
from jax import lax

D = 192
HEAD_DIM = 96
FF = 768
IMG_W = 32
IMG_H = 32
REL_H = 63
REL_W = 63
IMAGES = 32
SHIFT_ROWS = 11


def level_of(key, extent, cuts, low, largest):
    gain, own = 1.0, jax.random.fold_in(key, 6)
    for dim, parts in cuts:
        heights = jnp.exp(jax.random.uniform(jax.random.fold_in(own, dim), (parts,), jnp.float32, low / len(cuts), largest / len(cuts)))
        gain = gain * jnp.repeat(heights, extent[dim] // parts).reshape([-1 if axis == dim else 1 for axis in range(len(extent))])
    return gain


def noise(rng, extent, deviation, bound, cuts=(), held_as=jnp.bfloat16):
    loudness = level_of(rng, extent, cuts, -0.22, 0.18) if cuts else 1.0
    drawn = jax.random.normal(rng, extent, jnp.float32) * deviation * loudness
    return jnp.minimum(jnp.maximum(drawn, -bound), bound).astype(held_as)


def setup_inputs(seed: int = 0) -> dict:
    splits = jax.random.split(jax.random.key(seed), 14)
    return {
        "images": noise(splits[0], (IMAGES, IMG_H, IMG_W, D), 1.0, 6.0, ((0, 8), (1, 4))),
        "w_qkv": noise(splits[1], (D, 3 * D), D ** -0.5, 0.4375, ((0, 8),)),
        "w_proj": noise(splits[2], (D, D), D ** -0.5, 0.4375, ((0, 8),)),
        "w_up": noise(splits[3], (D, FF), D ** -0.5, 0.4375, ((0, 8),)),
        "w_down": noise(splits[4], (FF, D), FF ** -0.5, 0.21875, ((0, 8),)),
        "gains_main": jnp.clip(1.0 + 0.1 * jax.random.normal(splits[5], (2, D), jnp.float32), 0.5, 1.5).astype(jnp.bfloat16),
        "shifts_main": noise(splits[6], (SHIFT_ROWS, D), 0.2, 1.25),
        "pool_kernels": noise(splits[7], (3, 9, HEAD_DIM), 9 ** -0.5, 2.0),
        "pool_gains": jnp.clip(1.0 + 0.1 * jax.random.normal(splits[8], (3, HEAD_DIM), jnp.float32), 0.5, 1.5).astype(jnp.bfloat16),
        "pool_shifts": noise(splits[9], (2, HEAD_DIM), 0.3, 1.75),
        "rel_height": noise(splits[10], (REL_H, HEAD_DIM), 0.1, 0.625),
        "rel_width": noise(splits[11], (REL_W, HEAD_DIM), 0.1, 0.625),
        "cotangent": noise(splits[12], (IMAGES, IMG_H, IMG_W, D), 1.0, 6.0, ((0, 8), (1, 4))),
    }


norm_eps = 1e-06
highest = lax.Precision.HIGHEST

@jax.custom_vjp
def low(v):
    return lax.optimization_barrier(v.astype(jnp.bfloat16)).astype(jnp.float32)

@jax.custom_vjp
def low_back(v):
    return v

def low_keep(v):
    return (low(v), None)

def low_pass(kept, grad):
    return (grad,)

def back_keep(v):
    return (v, None)

def back_low(kept, grad):
    return (low(grad),)
low.defvjp(low_keep, low_pass)
low_back.defvjp(back_keep, back_low)

def layer_norm(values, gains, shifts):
    centre = lax.optimization_barrier(jnp.mean(values, -1, keepdims=True))
    centred = values - centre
    spread = lax.optimization_barrier(jnp.mean(centred * centred, -1, keepdims=True))
    return centred * lax.rsqrt(spread + norm_eps) * gains + shifts

def depthwise(padded, kernel, stride, out_rows, out_cols):
    summed = jnp.zeros(padded.shape[:-3] + (out_rows, out_cols, padded.shape[-1]), jnp.float32)
    for offset_row in range(3):
        for offset_col in range(3):
            window = padded[..., offset_row:offset_row + stride * (out_rows - 1) + 1:stride, offset_col:offset_col + stride * (out_cols - 1) + 1:stride, :]
            summed = summed + window * kernel[3 * offset_row + offset_col]
    return summed

def pool_heads(padded, kernels, gains, shifts):
    features = padded.shape[-1] // 3
    out_rows = padded.shape[-3] - 2
    out_cols = padded.shape[-2] - 2
    head_count = features // kernels.shape[-1]
    results = []
    for member, stride in ((0, 1), (1, 2), (2, 2)):
        section = padded[..., member * features:(member + 1) * features]
        pooled = depthwise(section, jnp.tile(kernels[member], (1, head_count)), stride, out_rows // stride, out_cols // stride)
        pooled = pooled.reshape(pooled.shape[:-1] + (head_count, kernels.shape[-1]))
        offset = shifts[0] if member == 0 else shifts[1] if member == 2 else jnp.zeros_like(shifts[0])
        results.append(layer_norm(pooled, gains[member], offset))
    return tuple(results)

def gelu_tanh(values):
    return jax.nn.gelu(values, approximate=True)

def rel_lookup(table, query_len, key_len):
    distance = jnp.arange(query_len)[:, None] - 2 * jnp.arange(key_len)[None, :] + 2 * (key_len - 1)
    return table[distance]

def block_forward(params, picture):
    w_qkv, w_proj, w_up, w_down, gains_main, shifts_main, pool_kernels, pool_gains, pool_shifts, rel_height, rel_width = params
    height, breadth, features = picture.shape
    head_dim = pool_kernels.shape[-1]
    head_count = features // head_dim
    key_rows = height // 2
    key_cols = breadth // 2
    tokens_flat = picture.reshape(height * breadth, features)
    normed_one = low(layer_norm(tokens_flat, gains_main[0], shifts_main[0]))
    mixed = jnp.dot(normed_one, w_qkv, precision=highest) + shifts_main[2:5].reshape(3 * features)
    mixed = low(low_back(mixed)).reshape(height, breadth, 3 * features)
    padded = jnp.pad(mixed, ((1, 1), (1, 1), (0, 0)))
    queries, keys_pooled, values_pooled = pool_heads(padded, pool_kernels, pool_gains, pool_shifts)
    queries = low(queries)
    keys_pooled = low(keys_pooled)
    values_pooled = low(values_pooled)
    term_height = jnp.einsum('xyhc,xjc->hxyj', queries, rel_lookup(rel_height, height, key_rows), precision=highest)
    term_width = jnp.einsum('xyhc,yjc->hxyj', queries, rel_lookup(rel_width, breadth, key_cols), precision=highest)
    scores = jnp.einsum('xyhc,ujhc->hxyuj', queries, keys_pooled, precision=highest) * head_dim ** (-0.5)
    scores = scores + term_height[..., :, None] + term_width[..., None, :]
    scores = low_back(scores).reshape(head_count, height * breadth, key_rows * key_cols)
    weights_soft = jax.nn.softmax(scores, axis=-1)
    attended = jnp.einsum('hqk,khc->qhc', weights_soft, values_pooled.reshape(key_rows * key_cols, head_count, head_dim), precision=highest)
    attended = attended + queries.reshape(height * breadth, head_count, head_dim)
    attended = low(low_back(attended.reshape(height * breadth, features)))
    branch = low_back(jnp.dot(attended, w_proj, precision=highest) + shifts_main[5])
    middle = tokens_flat + branch
    normed_two = low(layer_norm(middle, gains_main[1], shifts_main[1]))
    hidden = low_back(jnp.dot(normed_two, w_up, precision=highest) + shifts_main[6:-1].reshape(-1))
    activated = low(gelu_tanh(hidden))
    output = middle + jnp.dot(activated, w_down, precision=highest) + shifts_main[-1]
    return output.reshape(height, breadth, features)

def reference(images, w_qkv, w_proj, w_up, w_down, gains_main, shifts_main, pool_kernels, pool_gains, pool_shifts, rel_height, rel_width, cotangent):
    params = tuple((argument.astype(jnp.float32) for argument in (w_qkv, w_proj, w_up, w_down, gains_main, shifts_main, pool_kernels, pool_gains, pool_shifts, rel_height, rel_width)))
    pictures = images.astype(jnp.float32)
    cotangents = cotangent.astype(jnp.float32)
    initial = jax.tree.map(jnp.zeros_like, params)

    def per_picture(running, inputs):
        picture, upstream = inputs
        output, pullback = jax.vjp(block_forward, params, picture)
        grad_params, grad_picture = pullback(upstream)
        running = jax.tree.map(jnp.add, running, grad_params)
        return (running, (output.astype(jnp.bfloat16), grad_picture))
    totals, (outputs, grad_images) = lax.scan(per_picture, initial, (pictures, cotangents))
    return (outputs, grad_images, totals[0], totals[1], totals[2], totals[3], totals[4], totals[5], totals[6], totals[7], totals[8], totals[9], totals[10])
```

```python
import functools

import jax
import jax.numpy as jnp
from jax import lax
from jax.experimental import pallas as pl
from jax.experimental.pallas import tpu as pltpu
from jax.sharding import PartitionSpec as P

HEADS = 2
HEAD_DIM = 96


norm_eps = 1e-06
highest = lax.Precision.HIGHEST


def padded(cells, sides, width):
    for axis, dim in sides:
        count = lax.axis_size(axis)
        ends = count - 1
        head = lax.slice_in_dim(cells, 0, width, axis=dim)
        tail = lax.slice_in_dim(cells, cells.shape[dim] - width, cells.shape[dim], axis=dim)
        cells = jnp.concatenate(
            [
                lax.ppermute(tail, axis, [(i, (i + 1) % count) for i in range(ends)]),
                cells,
                lax.ppermute(head, axis, [((i + 1) % count, i) for i in range(ends)]),
            ],
            axis=dim,
        )
    return cells


def layer_norm(values, gains, shifts):
    centre = jnp.mean(values, -1, keepdims=True)
    centred = values - centre
    spread = jnp.mean(centred * centred, -1, keepdims=True)
    return centred * lax.rsqrt(spread + norm_eps) * gains + shifts


def gelu_tanh(values):
    return jax.nn.gelu(values, approximate=True)


def pool_section(section, kernel, stride):
    image_count, ext_rows, col_count, features = section.shape
    out_rows = (ext_rows - 2) // stride
    out_cols = col_count // stride
    col_out = jnp.arange(out_cols)[:, None] * stride
    col_in = jnp.arange(col_count)[None, :]
    shifted = []
    for offset_col in range(3):
        picker = (col_out + offset_col - 1 == col_in).astype(jnp.float32)
        shifted.append(jnp.einsum("jy,bxyc->bxjc", picker, section, precision=highest))
    summed = jnp.zeros((image_count, out_rows, out_cols, features), jnp.float32)
    for offset_row in range(3):
        for offset_col in range(3):
            window = shifted[offset_col][:, offset_row : offset_row + ext_rows - 2]
            if stride == 2:
                window = window.reshape(image_count, out_rows, 2, out_cols, features)[:, :, 0]
            summed = summed + window * kernel[3 * offset_row + offset_col]
    return summed


def pooled_local(extended_f, kernels, gains, shifts):
    features = extended_f.shape[-1]
    head_dim = kernels.shape[-1]
    head_count = features // head_dim
    results = []
    for member, stride in ((0, 1), (1, 2), (2, 2)):
        pooled = pool_section(
            extended_f[member], jnp.tile(kernels[member], (1, head_count)), stride
        )
        pooled = pooled.reshape(pooled.shape[:-1] + (head_count, head_dim))
        offset = (
            shifts[0] if member == 0 else shifts[1] if member == 2 else jnp.zeros_like(shifts[0])
        )
        results.append(layer_norm(pooled, gains[member], offset))
    return tuple(results)


def row_sharded(
    images,
    w_qkv,
    w_proj,
    w_up,
    w_down,
    gains_main,
    shifts_main,
    pool_kernels,
    pool_gains,
    pool_shifts,
    rel_height,
    rel_width,
    cotangent,
):
    image_count, row_count, col_count, features = images.shape
    head_dim = HEAD_DIM
    head_count = HEADS
    scale_factor = head_dim ** (-0.5)
    cycle_size = lax.axis_size("rows")
    key_rows_all = row_count * cycle_size // 2
    key_cols = col_count // 2
    key_total = key_rows_all * key_cols
    query_count = row_count * col_count
    key_local = row_count // 2 * key_cols
    gain_rows = gains_main.astype(jnp.float32)
    shift_rows = shifts_main.astype(jnp.float32)
    full_qkv, full_proj, full_up, full_down = (
        lax.all_gather(w_qkv, "batch", axis=0, tiled=True),
        lax.all_gather(w_proj, "batch", axis=0, tiled=True),
        lax.all_gather(w_up, "batch", axis=0, tiled=True),
        lax.all_gather(w_down, "batch", axis=0, tiled=True),
    )
    qkv_split = full_qkv.reshape(features, 3, features)
    inputs_f = images.astype(jnp.float32)
    normed_one, norm_one_pullback = jax.vjp(layer_norm, inputs_f, gain_rows[0], shift_rows[0])
    normed_low = normed_one.astype(jnp.bfloat16)
    mixed = (
        jnp.einsum("bxyd,dme->mbxye", normed_low, qkv_split, preferred_element_type=jnp.float32)
        + shift_rows[2:5][:, None, None, None, :]
    )
    mixed_low = mixed.astype(jnp.bfloat16)
    extended = padded(mixed_low, (("rows", 2),), 1)
    (queries, keys_pooled, values_pooled), pool_pullback = jax.vjp(
        pooled_local,
        extended.astype(jnp.float32),
        pool_kernels.astype(jnp.float32),
        pool_gains.astype(jnp.float32),
        pool_shifts.astype(jnp.float32),
    )
    queries_low = queries.astype(jnp.bfloat16)
    query_flat = queries_low.reshape(image_count, query_count, head_count, head_dim)
    keys_low = keys_pooled.astype(jnp.bfloat16).reshape(image_count, key_local, features)
    values_low = values_pooled.astype(jnp.bfloat16).reshape(image_count, key_local, features)
    key_value = jnp.concatenate([keys_low, values_low], -1)
    first_row = lax.axis_index("rows") * row_count

    def rel_terms(query_vals, table_height, table_width):
        row_place = first_row + jnp.arange(row_count)
        dist_height = (
            row_place[:, None] - 2 * jnp.arange(key_rows_all)[None, :] + 2 * (key_rows_all - 1)
        )
        pick_height = (
            dist_height[:, :, None] == jnp.arange(table_height.shape[0])[None, None, :]
        ).astype(jnp.float32)
        lookup_height = jnp.einsum("xjt,tc->xjc", pick_height, table_height, precision=highest)
        dist_width = (
            jnp.arange(col_count)[:, None] - 2 * jnp.arange(key_cols)[None, :] + 2 * (key_cols - 1)
        )
        pick_width = (
            dist_width[:, :, None] == jnp.arange(table_width.shape[0])[None, None, :]
        ).astype(jnp.float32)
        lookup_width = jnp.einsum("yjt,tc->yjc", pick_width, table_width, precision=highest)
        term_height = jnp.einsum("bxyhc,xjc->bhxyj", query_vals, lookup_height, precision=highest)
        term_width = jnp.einsum("bxyhc,yjc->bhxyj", query_vals, lookup_width, precision=highest)
        return (term_height, term_width)

    (term_height, term_width), rel_pullback = jax.vjp(
        rel_terms,
        queries_low.astype(jnp.float32),
        rel_height.astype(jnp.float32),
        rel_width.astype(jnp.float32),
    )
    rel_full = (term_height[..., :, None] + term_width[..., None, :]).reshape(
        image_count, head_count, query_count, key_total
    )

    def key_scores(key_piece):
        piece_rows = key_piece.shape[1]
        keys_part = key_piece[..., :features].reshape(image_count, piece_rows, head_count, head_dim)
        products = jnp.einsum(
            "bqhc,bkhc->bhqk", query_flat, keys_part, preferred_element_type=jnp.float32
        )
        return products * scale_factor + lax.slice_in_dim(rel_full, 0, piece_rows, axis=3)

    key_piece = lax.all_gather(key_value, "rows", axis=1, tiled=True)
    run_max = jnp.full((image_count, head_count, query_count), -1e30, jnp.float32)
    run_sum = jnp.zeros((image_count, head_count, query_count), jnp.float32)
    run_acc = jnp.zeros((image_count, head_count, query_count, head_dim), jnp.float32)
    piece_rows = key_piece.shape[1]
    values_part = key_piece[..., features:].reshape(image_count, piece_rows, head_count, head_dim)
    scores = key_scores(key_piece)
    new_max = jnp.maximum(run_max, jnp.max(scores, -1))
    weights_exp = jnp.exp(scores - new_max[..., None])
    factor = jnp.exp(run_max - new_max)
    run_sum = run_sum * factor + jnp.sum(weights_exp, -1)
    run_acc = run_acc * factor[..., None] + jnp.einsum(
        "bhqk,bkhc->bhqc", weights_exp, values_part.astype(jnp.float32), precision=highest
    )
    run_max, run_sum, run_acc = (new_max, run_sum, run_acc)
    log_total = run_max + jnp.log(run_sum)
    attended = (run_acc / run_sum[..., None]).transpose(0, 2, 1, 3) + query_flat.astype(jnp.float32)
    attended_low = attended.reshape(image_count, row_count, col_count, features).astype(
        jnp.bfloat16
    )
    branch = (
        jnp.einsum("bxyd,de->bxye", attended_low, full_proj, preferred_element_type=jnp.float32)
        + shift_rows[5]
    )
    middle = inputs_f + branch
    normed_two, norm_two_pullback = jax.vjp(layer_norm, middle, gain_rows[1], shift_rows[1])
    normed_two_low = normed_two.astype(jnp.bfloat16)
    hidden = jnp.einsum(
        "bxyd,df->bxyf", normed_two_low, full_up, preferred_element_type=jnp.float32
    ) + shift_rows[6:-1].reshape(-1)
    activated, gelu_pullback = jax.vjp(gelu_tanh, hidden)
    activated_low = activated.astype(jnp.bfloat16)
    output = (
        middle
        + jnp.einsum("bxyf,fd->bxyd", activated_low, full_down, preferred_element_type=jnp.float32)
        + shift_rows[-1]
    )
    output_low = output.astype(jnp.bfloat16)
    upstream = cotangent.astype(jnp.float32)
    grad_down = jnp.einsum(
        "bxyf,bxyd->fd", activated_low, cotangent, preferred_element_type=jnp.float32
    )
    grad_shift_down = jnp.sum(upstream, (0, 1, 2))
    grad_activated = jnp.einsum(
        "bxyd,fd->bxyf", cotangent, full_down, preferred_element_type=jnp.float32
    )
    (grad_hidden,) = gelu_pullback(grad_activated)
    grad_hidden_low = grad_hidden.astype(jnp.bfloat16)
    grad_up = jnp.einsum(
        "bxyd,bxyf->df", normed_two_low, grad_hidden_low, preferred_element_type=jnp.float32
    )
    grad_shift_up = jnp.sum(grad_hidden_low.astype(jnp.float32), (0, 1, 2))
    grad_normed_two = jnp.einsum(
        "bxyf,df->bxyd", grad_hidden_low, full_up, preferred_element_type=jnp.float32
    )
    grad_middle_norm, grad_gain_two, grad_shift_two = norm_two_pullback(grad_normed_two)
    grad_middle = upstream + grad_middle_norm
    grad_branch_low = grad_middle.astype(jnp.bfloat16)
    grad_proj = jnp.einsum(
        "bxyd,bxye->de", attended_low, grad_branch_low, preferred_element_type=jnp.float32
    )
    grad_shift_proj = jnp.sum(grad_branch_low.astype(jnp.float32), (0, 1, 2))
    grad_attended = jnp.einsum(
        "bxye,de->bxyd", grad_branch_low, full_proj, preferred_element_type=jnp.float32
    )
    grad_flat = grad_attended.astype(jnp.bfloat16).reshape(
        image_count, query_count, head_count, head_dim
    )
    grad_flat_f = grad_flat.astype(jnp.float32)
    key_value_all = lax.all_gather(key_value, "rows", axis=1, tiled=True)
    scores = key_scores(key_value_all)
    soft = jnp.exp(scores - log_total[..., None])
    keys_all = key_value_all[..., :features].reshape(image_count, key_total, head_count, head_dim)
    values_all = key_value_all[..., features:].reshape(image_count, key_total, head_count, head_dim)
    grad_soft = jnp.einsum(
        "bqhc,bkhc->bhqk", grad_flat, values_all, preferred_element_type=jnp.float32
    )
    row_dot = jnp.sum(soft * grad_soft, -1, keepdims=True)
    grad_scores = (soft * (grad_soft - row_dot)).astype(jnp.bfloat16)
    grad_queries = (
        scale_factor
        * jnp.einsum("bhqk,bkhc->bqhc", grad_scores, keys_all, preferred_element_type=jnp.float32)
        + grad_flat_f
    )
    grad_scores_f = grad_scores.astype(jnp.float32).reshape(
        image_count, head_count, row_count, col_count, key_rows_all, key_cols
    )
    grad_query_rel, grad_rel_h, grad_rel_w = rel_pullback(
        (jnp.sum(grad_scores_f, -1), jnp.sum(grad_scores_f, -2))
    )
    grad_queries = (
        grad_queries.reshape(image_count, row_count, col_count, head_count, head_dim)
        + grad_query_rel
    )
    key_span = key_local * lax.axis_size("rows")
    part_scores = lax.slice_in_dim(grad_scores, 0, key_span, axis=3)
    part_soft = lax.slice_in_dim(soft, 0, key_span, axis=3)
    grad_keys_part = scale_factor * jnp.einsum(
        "bhqk,bqhc->kbhc", part_scores, query_flat, preferred_element_type=jnp.float32
    )
    grad_values_part = jnp.einsum("bhqk,bqhc->kbhc", part_soft, grad_flat_f, precision=highest)
    key_grads = (
        lax.psum_scatter(
            jnp.concatenate(
                [
                    grad_keys_part.reshape(key_span, image_count, features),
                    grad_values_part.reshape(key_span, image_count, features),
                ],
                -1,
            ).astype(jnp.bfloat16),
            "rows",
            scatter_dimension=0,
            tiled=True,
        )
        .astype(jnp.float32)
        .transpose(1, 0, 2)
    )
    grad_keys = key_grads[..., :features].reshape(
        image_count, row_count // 2, key_cols, head_count, head_dim
    )
    grad_values = key_grads[..., features:].reshape(
        image_count, row_count // 2, key_cols, head_count, head_dim
    )
    grad_extended, grad_kernels, grad_pool_gain, grad_pool_shift = pool_pullback(
        (grad_queries, grad_keys, grad_values)
    )
    rims = jnp.concatenate([grad_extended[:, :, :1], grad_extended[:, :, -1:]], 2)
    rims_all = padded(rims.astype(jnp.bfloat16), (("rows", 2),), 1).astype(rims.dtype)
    grad_mixed = grad_extended[:, :, 1:-1]
    grad_mixed = grad_mixed.at[:, :, 0].add(rims_all[:, :, 0]).at[:, :, -1].add(rims_all[:, :, 3])
    grad_mixed_low = grad_mixed.astype(jnp.bfloat16)
    grad_qkv = jnp.einsum(
        "bxyd,mbxye->dme", normed_low, grad_mixed_low, preferred_element_type=jnp.float32
    ).reshape(features, 3 * features)
    grad_shift_qkv = jnp.sum(grad_mixed_low.astype(jnp.float32), (1, 2, 3))
    grad_normed_one = jnp.einsum(
        "mbxye,dme->bxyd", grad_mixed_low, qkv_split, preferred_element_type=jnp.float32
    )
    grad_inputs_norm, grad_gain_one, grad_shift_one = norm_one_pullback(grad_normed_one)
    grad_images = grad_middle + grad_inputs_norm
    grad_gains = jnp.stack([grad_gain_one, grad_gain_two])
    grad_shifts = jnp.concatenate(
        [
            grad_shift_one[None],
            grad_shift_two[None],
            grad_shift_qkv,
            grad_shift_proj[None],
            grad_shift_up.reshape(-1, features),
            grad_shift_down[None],
        ],
        0,
    )
    small_summed = lax.psum(
        (
            grad_gains,
            grad_shifts,
            grad_kernels,
            grad_pool_gain,
            grad_pool_shift,
            grad_rel_h,
            grad_rel_w,
        ),
        ("batch", "rows"),
    )
    matrix_grads = (grad_qkv, grad_proj, grad_up, grad_down)
    summed_rows = (
        lax.psum(matrix_grads[0].astype(jnp.bfloat16), "rows").astype(jnp.float32),
        lax.psum(matrix_grads[1].astype(jnp.bfloat16), "rows").astype(jnp.float32),
        lax.psum(matrix_grads[2].astype(jnp.bfloat16), "rows").astype(jnp.float32),
        lax.psum(matrix_grads[3].astype(jnp.bfloat16), "rows").astype(jnp.float32),
    )
    owned = (
        lax.psum_scatter(
            summed_rows[0].astype(jnp.bfloat16), "batch", scatter_dimension=0, tiled=True
        ).astype(jnp.float32),
        lax.psum_scatter(
            summed_rows[1].astype(jnp.bfloat16), "batch", scatter_dimension=0, tiled=True
        ).astype(jnp.float32),
        lax.psum_scatter(
            summed_rows[2].astype(jnp.bfloat16), "batch", scatter_dimension=0, tiled=True
        ).astype(jnp.float32),
        lax.psum_scatter(
            summed_rows[3].astype(jnp.bfloat16), "batch", scatter_dimension=0, tiled=True
        ).astype(jnp.float32),
    )
    return (
        output_low,
        grad_images,
        owned[0],
        owned[1],
        owned[2],
        owned[3],
        small_summed[0],
        small_summed[1],
        small_summed[2],
        small_summed[3],
        small_summed[4],
        small_summed[5],
        small_summed[6],
    )


LANES = 128
NT = (((1,), (1,)), ((), ()))
TN = (((0,), (0,)), ((), ()))
NN = (((1,), (0,)), ((), ()))
f32 = jnp.float32
bf16 = jnp.bfloat16


def dot(a, b, dims=NN):
    return lax.dot_general(a, b, dims, preferred_element_type=f32)


def lane_ids(shape):
    return lax.broadcasted_iota(jnp.int32, shape, len(shape) - 1)


def head_mask(rows):
    return (lane_ids((rows, LANES)) < HEAD_DIM).astype(f32)


def head_piece(values, start):
    base = start // LANES * LANES
    move = start - base
    if move == 0:
        piece = values[:, base : base + LANES]
    else:
        piece = pltpu.roll(values[:, base : base + 2 * LANES], 2 * LANES - move, 1)[:, :LANES]
    return piece * head_mask(values.shape[0])


def norm_parts(values, count):
    centre = jnp.sum(values, -1, keepdims=True) * (1.0 / count)
    centred = values - centre
    spread = jnp.sum(centred * centred, -1, keepdims=True) * (1.0 / count)
    scale = lax.rsqrt(spread + norm_eps)
    return centred * scale, scale


def head_norm_parts(values, mask):
    centre = jnp.sum(values, -1, keepdims=True) * (1.0 / HEAD_DIM)
    centred = (values - centre) * mask
    spread = jnp.sum(centred * centred, -1, keepdims=True) * (1.0 / HEAD_DIM)
    scale = lax.rsqrt(spread + norm_eps)
    return centred * scale, scale


def norm_back(grad, unit, scale, count):
    first = jnp.sum(grad, -1, keepdims=True) * (1.0 / count)
    second = jnp.sum(grad * unit, -1, keepdims=True) * (1.0 / count)
    return scale * (grad - first - unit * second)


def fold_rows(values):
    rows, lanes = values.shape
    return jnp.sum(values.reshape(rows // 8, 8, lanes), 0)


def fold_block(values):
    rows = values.shape[0]
    tail = values[:, LANES : LANES + 64]
    tail = jnp.concatenate([tail, jnp.zeros_like(tail)], 1)
    side = tail[: rows // 2] + pltpu.roll(tail[rows // 2 :], 64, 1)
    return jnp.concatenate([values[:, :LANES], side], 0)


def unfold_block(folded):
    rows = folded.shape[0] * 2 // 3
    side = folded[rows:]
    tail = jnp.concatenate([side, pltpu.roll(side, 64, 1)], 0)
    return jnp.concatenate([folded[:rows], tail[:, :64]], 1)


def turned(shift):
    return lax.rem(lax.axis_index("rows") + shift, 4)


def copy_all(pairs, sems):
    copies = []
    for near, far in pairs:
        copies.append(pltpu.make_async_copy(near, far, sems.at[len(copies)]))
        copies[-1].start()
    return copies


def wait_all(copies):
    for copy in copies:
        copy.wait()


def pack_kernel(qkv_ref, proj_ref, up_ref, down_ref, packed_ref, qkv_in, proj_in, up_in, down_in, sems):
    wait_all(
        copy_all(
            [(qkv_ref, qkv_in), (proj_ref, proj_in), (up_ref, up_in), (down_ref, down_in)], sems
        )
    )
    share = qkv_in.shape[0]
    packed_ref[...] = jnp.concatenate(
        [qkv_in[...].astype(f32), proj_in[...].astype(f32), up_in[...].astype(f32)]
        + [
            down_in[...].astype(f32)[share * i : share * (i + 1)]
            for i in range(down_in.shape[0] // share)
        ],
        1,
    ).astype(bf16)


def fold_images_kernel(img_ref, out_ref, img_in, sems):
    loads = copy_all([(img_ref.at[k], img_in.at[k]) for k in range(4)], sems)
    for block in range(4):
        loads[block].wait()
        out_ref[block] = fold_block(img_in[block].astype(f32)).astype(bf16)


def fold_kernel(cot_ref, cot_0, cot_1, cot_2, cot_3, cot_in, cot_scr, in_sems, sems):
    loads = copy_all([(cot_ref.at[turned(k)], cot_in.at[k]) for k in range(4)], in_sems)
    copies = []
    for shift, far in enumerate((cot_0, cot_1, cot_2, cot_3)):
        loads[shift].wait()
        cot_scr[shift] = fold_block(cot_in[shift].astype(f32)).astype(bf16)
        copies.append(pltpu.make_async_copy(cot_scr.at[shift], far, sems.at[shift]))
        copies[-1].start()
    wait_all(copies)


def flipped(flip):
    place = lax.axis_index("batch")
    owner = place
    for bit in (1, 2, 4):
        if flip & bit:
            owner = owner + bit - 2 * bit * lax.rem(place // bit, 2)
    return owner


def gather_rows(own_ref, other_ref, first, last, full_scr):
    share = own_ref.shape[1]
    for flip in range(8):
        source = other_ref if flip & 1 else own_ref
        rows = pl.ds(pl.multiple_of(flipped(flip) * share, 8), share)
        full_scr[rows, :] = source[flip // 2, :, first:last].astype(f32)


def load_taps(kernel_ref, kernel_scr):
    kernel_scr[...] = jnp.zeros_like(kernel_scr)
    for tap in range(9):
        kernel_scr[tap, 0:3, 0:HEAD_DIM] = kernel_ref[tap].astype(f32)


def load_gains(gain_ref, shift_ref, gain_scr):
    gain_scr[...] = jnp.zeros_like(gain_scr)
    gain_scr[0:3, 0:HEAD_DIM] = gain_ref[...].astype(f32)
    gain_scr[3:5, 0:HEAD_DIM] = shift_ref[...].astype(f32)


def clear_rim(padded_scr):
    rows, cols, lanes = padded_scr.shape[-3:]
    for place in range(padded_scr.shape[0] if len(padded_scr.shape) == 4 else 1):
        cells = padded_scr.at[place] if len(padded_scr.shape) == 4 else padded_scr
        cells[0:1] = jnp.zeros((1, cols, lanes), f32)
        cells[rows - 1 : rows] = jnp.zeros((1, cols, lanes), f32)
        cells[:, 0:8, :] = jnp.zeros((rows, 8, lanes), f32)
        cells[:, cols - 8 : cols, :] = jnp.zeros((rows, 8, lanes), f32)


CHUNK_ROWS = 8
MIX_ROWS = 32
ATTEND_ROWS = 32
BACK_ROWS = 32
WEIGH_TILE = 1024
IMAGE_TILE = 1024
LOG2_E = 1.4426950408889634


def stride_windows(padded, place, side, key_rows, key_cols):
    columns = pl.ds(7 + side, key_cols, stride=2)
    even = padded[place, pl.ds(0, key_rows + 1, stride=2), columns, :]
    odd = padded[place, pl.ds(1, key_rows, stride=2), columns, :]
    return even[:key_rows], odd, even[1:]


def attend_kernel(
    stage, weight_scr, bias_ref, rows_ref, kern_scr, gain_scr, table_ref,
    img_ref, padded, qraw_out, kvraw_out, soft_out, att_out, key_out, val_out,
    query_scr, keyaug_scr,
):
    cols = padded.shape[2] - 16
    rows = padded.shape[1] - 2
    tile = CHUNK_ROWS * cols
    chunks = rows // CHUNK_ROWS
    key_cols = cols // 2
    key_rows = rows // 2
    key_total = key_rows * key_cols
    features = img_ref.shape[1]
    clear_rim(padded)
    gain_one = rows_ref[16:17, 0:features]
    shift_one = rows_ref[0:1, 0:features]
    table = table_ref[...]

    mix_tile = MIX_ROWS * cols

    img_ref[...] = jnp.concatenate(
        [unfold_block(stage[place].astype(f32)) for place in range(4)], 0
    ).astype(bf16)

    def mix(step, carry):
        span = pl.ds(pl.multiple_of(step * mix_tile, mix_tile), mix_tile)
        unit, _ = norm_parts(img_ref[span, :].astype(f32), features)
        normed = (unit * gain_one + shift_one).astype(bf16)
        mixed = dot(normed, weight_scr[...]) + bias_ref[0:1, :]
        for place in range(3 * HEADS):
            low = mixed[:, place * LANES : (place + 1) * LANES].astype(bf16)
            padded[place, pl.ds(1 + step * MIX_ROWS, MIX_ROWS), 8 : 8 + cols, :] = low.astype(
                f32
            ).reshape(MIX_ROWS, cols, LANES)
        return carry

    lax.fori_loop(0, rows // MIX_ROWS, mix, 0, unroll=True)

    tile_mask = head_mask(tile)

    def pool_queries(step, carry):
        span = pl.ds(pl.multiple_of(step * tile, tile), tile)
        for head in range(HEADS):
            total = jnp.zeros((CHUNK_ROWS, cols, LANES), f32)
            for side in range(3):
                window = padded[
                    head, pl.ds(step * CHUNK_ROWS, CHUNK_ROWS + 2), 7 + side : 7 + side + cols, :
                ]
                for up in range(3):
                    total = total + window[up : up + CHUNK_ROWS] * kern_scr[3 * up + side, 0:1, :]
            raw = total.reshape(tile, LANES)
            qraw_out[head, span, :] = raw
            unit, _ = head_norm_parts(raw, tile_mask)
            query_scr[head, span, :] = (unit * gain_scr[0:1, :] + gain_scr[3:4, :]).astype(bf16)
        return carry

    lax.fori_loop(0, chunks, pool_queries, 0, unroll=True)

    for place in range(2 * HEADS):
        member = 1 + place // HEADS
        total = jnp.zeros((key_rows, key_cols, LANES), f32)
        for side in range(3):
            for up, window in enumerate(stride_windows(padded, HEADS + place, side, key_rows, key_cols)):
                total = total + window * kern_scr[3 * up + side, member : member + 1, :]
        kvraw_out[place] = total.reshape(key_total, LANES)

    key_mask = head_mask(key_total)
    key_place = lax.broadcasted_iota(jnp.int32, (key_total, LANES), 0)
    lanes = lane_ids((key_total, LANES))
    from_row = 30 - 2 * (key_place // key_cols)
    from_col = 96 + 2 * (key_place % key_cols)
    hot = (
        (lanes == from_row)
        | (lanes == from_row + 64)
        | (lanes == from_col)
        | (lanes == from_col - 64)
    ).astype(bf16)
    for head in range(HEADS):
        unit, _ = head_norm_parts(kvraw_out[head], key_mask)
        low = (unit * gain_scr[1:2, :]).astype(bf16)
        key_out[head] = low
        keyaug_scr[head, :, 0:LANES] = low
        keyaug_scr[head, :, LANES : 2 * LANES] = hot
        unit, _ = head_norm_parts(kvraw_out[HEADS + head], key_mask)
        val_out[head] = (unit * gain_scr[2:3, :] + gain_scr[4:5, :]).astype(bf16)

    scale_factor = HEAD_DIM ** (-0.5)
    row_lanes = lane_ids((cols, LANES))
    part_tile = ATTEND_ROWS * cols
    part_lanes = lane_ids((part_tile, LANES))

    def attend(step, carry):
        span = pl.ds(pl.multiple_of(step * part_tile, part_tile), part_tile)
        for head in range(HEADS):
            query = query_scr[head, span, :]
            looked = dot(query, table, NT) * (1.0 / scale_factor)
            pieces = []
            for row in range(ATTEND_ROWS):
                part = looked[row * cols : (row + 1) * cols, :]
                place = step * ATTEND_ROWS + row
                by_row = pltpu.roll(part, LANES - place, 1)
                by_col = pltpu.roll(part, 0, 1, stride=1, stride_axis=0)
                pieces.append(jnp.where(row_lanes < 64, by_row, by_col))
            terms = jnp.concatenate(pieces, 0)
            high = terms.astype(bf16).astype(f32)
            rest = pltpu.roll(terms - high, 64, 1)
            both = jnp.where((part_lanes < 32) | (part_lanes >= 96), high, rest).astype(bf16)
            scores = dot(jnp.concatenate([query, both], 1), keyaug_scr[head], NT)
            top = jnp.max(scores, -1, keepdims=True)
            powers = jnp.exp2((scores - top) * (scale_factor * LOG2_E))
            soft = (powers * (1.0 / jnp.sum(powers, -1, keepdims=True))).astype(bf16)
            soft_out[head, span, :] = soft
            att = dot(soft, val_out[head]) + query.astype(f32)
            att_out[span, head * LANES : (head + 1) * LANES] = att.astype(bf16)
        return carry

    lax.fori_loop(0, rows // ATTEND_ROWS, attend, 0, unroll=True)


def stack_blocks(values, block_scr):
    owners = block_scr.shape[0]
    share = values.shape[0] // owners
    for block in range(values.shape[1] // LANES):
        for owner in range(owners):
            block_scr[owner, share * block : share * (block + 1), :] = values[
                share * owner : share * (owner + 1), block * LANES : (block + 1) * LANES
            ]


def split_owners(block_scr, mine_ref, theirs_ref, order):
    count = block_scr.shape[1]
    for place, flip in enumerate(order):
        span = pl.ds(place * count, count)
        mine_ref[span, :] = block_scr[flipped(flip)].astype(bf16)
        theirs_ref[span, :] = block_scr[flipped(flip + 1)].astype(bf16)


def weights_kernel(
    owners, own_ref, other_ref, gains_far, shifts_far, kern_far, pgain_far, pshift_far, relh_far, relw_far,
    wide_ref, proj_ref, up_ref, down_ref, bias_ref, rows_ref, columns_ref, taps_ref, pool_ref, ahead_ref, behind_ref,
    full_scr, down_scr, gains_in, shifts_in, kern_in, pgain_in, pshift_in, relh_in, relw_in, table_scr, sems,
):
    loads = copy_all(
        [
            (gains_far, gains_in), (shifts_far, shifts_in), (kern_far, kern_in), (pgain_far, pgain_in),
            (pshift_far, pshift_in), (relh_far, relh_in), (relw_far, relw_in),
        ],
        sems,
    )
    gather_rows(own_ref, other_ref, 0, own_ref.shape[2], full_scr)
    for place in range(3 * HEADS):
        wide_ref[:, place * LANES : (place + 1) * LANES] = head_piece(
            full_scr[:, 0 : 5 * LANES], place * HEAD_DIM
        ).astype(bf16)
    features, hidden_count = up_ref.shape
    proj = pltpu.roll(full_scr[:, 4 * LANES : 6 * LANES], 192, 1)[:, 0:features]
    gap = jnp.zeros((LANES - HEAD_DIM, features), f32)
    proj_ref[...] = jnp.concatenate(
        [proj[0:HEAD_DIM, :], gap, proj[HEAD_DIM : 2 * HEAD_DIM, :], gap], 0
    ).astype(bf16)
    up_ref[...] = full_scr[:, 4 * features : 4 * features + hidden_count].astype(bf16)
    columns = full_scr[:, 4 * features + hidden_count :]
    share = features // owners
    pieces = hidden_count // features
    for piece in range(pieces):
        start = piece * features
        base = start // LANES * LANES
        window = columns[:, base : base + 2 * LANES]
        if start != base:
            window = pltpu.roll(window, 2 * LANES - (start - base), 1)
        for owner in range(owners):
            place = owner * share * pieces + piece * share
            down_scr[place : place + share, :] = window[
                owner * share : (owner + 1) * share, 0:features
            ]
    down_ref[...] = down_scr[...].astype(bf16)
    wait_all(loads)
    rows_ref[...] = jnp.zeros_like(rows_ref)
    rows_ref[0 : shifts_in.shape[0], 0:features] = shifts_in[...].astype(f32)
    rows_ref[16:18, 0:features] = gains_in[...].astype(f32)
    columns_ref[...] = jnp.concatenate(
        [rows_ref[...], jnp.zeros((LANES - rows_ref.shape[0], 2 * LANES), f32)], 0
    ).T
    bias_ref[...] = jnp.zeros_like(bias_ref)
    for section in range(3):
        for head in range(HEADS):
            place = (section * HEADS + head) * LANES
            bias_ref[0:1, place : place + LANES] = head_piece(
                rows_ref[2 + section : 3 + section, :], head * HEAD_DIM
            )
    for piece in range(pieces):
        bias_ref[1:2, piece * features : (piece + 1) * features] = rows_ref[
            6 + piece : 7 + piece, 0:features
        ]
    load_taps(kern_in, taps_ref)
    load_gains(pgain_in, pshift_in, pool_ref)
    count = relw_in.shape[0]
    table_scr[...] = jnp.zeros_like(table_scr)
    table_scr[0:count, 0:HEAD_DIM] = relh_in[...].astype(f32)
    table_scr[64 : 64 + count, 0:HEAD_DIM] = relw_in[...].astype(f32)
    behind_ref[...] = table_scr[...].astype(bf16)
    flip = (
        lax.broadcasted_iota(jnp.int32, (64, count), 0) + lax.broadcasted_iota(jnp.int32, (64, count), 1)
        == count - 1
    ).astype(bf16)
    table_scr[64:128, 0:HEAD_DIM] = dot(flip, relw_in[...])
    ahead_ref[...] = table_scr[...].astype(bf16)


def send_turned(near, fars, sems):
    sends = []
    for shift, far in enumerate(fars):
        sends.append(pltpu.make_async_copy(near.at[turned(shift)], far, sems.at[shift]))
        sends[-1].start()
    return sends


GELU_A = 0.7978845608028654
GELU_B = 0.044715


def feed_ahead_kernel(
    img_ref, att_ref, proj_ref, up_ref, down_ref, bias_ref, rows_ref,
    out_0, out_1, out_2, out_3, normed_ref, unit_ref, scale_ref, active_ref, slope_ref,
    out_stage, turn_sems,
):
    tokens, features = img_ref.shape
    pieces = up_ref.shape[1] // features
    block = tokens // 4
    middle = img_ref[...].astype(f32) + (dot(att_ref[...], proj_ref[...]) + rows_ref[5:6, 0:features])
    unit, scale = norm_parts(middle, features)
    normed = (unit * rows_ref[17:18, 0:features] + rows_ref[1:2, 0:features]).astype(bf16)
    unit_ref[...] = unit
    scale_ref[...] = jnp.broadcast_to(scale, scale_ref.shape)
    normed_ref[...] = normed
    hidden = dot(normed, up_ref[...]) + bias_ref[1:2, :]
    square = hidden * hidden
    wave = jnp.tanh(hidden * (GELU_A + (GELU_A * GELU_B) * square))
    half = 0.5 + 0.5 * wave
    active = (hidden * half).astype(bf16)
    active_ref[...] = active
    slope_ref[...] = half * (
        1.0 + (1.0 - half) * (hidden * (2.0 * GELU_A + (6.0 * GELU_A * GELU_B) * square))
    )
    out = middle + dot(active, down_ref[...]) + rows_ref[6 + pieces : 7 + pieces, 0:features]
    for place in range(4):
        out_stage[place] = fold_block(out[place * block : (place + 1) * block, :]).astype(bf16)
    wait_all(send_turned(out_stage, (out_0, out_1, out_2, out_3), turn_sems))


def feed_back_kernel(
    owners,
    att_ref, cot_0, cot_1, cot_2, cot_3, normed_ref, unit_ref, scale_ref, active_ref, slope_ref,
    proj_ref, up_ref, down_ref, rows_ref,
    mid_ref, gatt_ref, mine_ref, theirs_ref,
    gdown, gup, gproj, gbias, gsmall, block_scr, cot_stage, cot_sems,
):
    cot_loads = copy_all(
        [(piece, cot_stage.at[turned(4 - k)]) for k, piece in enumerate((cot_0, cot_1, cot_2, cot_3))],
        cot_sems,
    )
    tokens, features = unit_ref.shape
    hidden_count = up_ref.shape[1]
    pieces = hidden_count // features
    unit = unit_ref[...]
    att = att_ref[...]
    wait_all(cot_loads)
    cot = jnp.concatenate([unfold_block(cot_stage[place].astype(f32)) for place in range(4)], 0)
    cot_low = cot.astype(bf16)
    gdown[...] = dot(cot_low, active_ref[...], TN)
    gact = dot(cot_low, down_ref[...], NT)
    ghid = (gact * slope_ref[...]).astype(bf16)
    gup[...] = dot(normed_ref[...], ghid, TN)
    gbias[...] = fold_rows(ghid.astype(f32))
    gnorm = dot(ghid, up_ref[...], NT)
    gsmall[0:8, :] = fold_rows(gnorm * unit)
    gsmall[8:16, :] = fold_rows(gnorm)
    gmid = cot + norm_back(gnorm * rows_ref[17:18, 0:features], unit, scale_ref[:, 0:1], features)
    gbranch = gmid.astype(bf16)
    mid_ref[...] = gbranch
    gsmall[16:24, :] = fold_rows(gbranch.astype(f32))
    gsmall[24:32, :] = fold_rows(cot)
    gproj[...] = dot(att, gbranch, TN)
    gatt_ref[...] = dot(gbranch, proj_ref[...], NT).astype(bf16)

    share = features // owners
    proj = jnp.concatenate(
        [gproj[head * LANES : head * LANES + HEAD_DIM, :] for head in range(HEADS)], 0
    )
    down = gdown[...].T
    down_pieces = []
    for piece in range(pieces):
        down_pieces.append(
            jnp.concatenate(
                [
                    down[
                        owner * share * pieces + piece * share : owner * share * pieces
                        + (piece + 1) * share,
                        :,
                    ]
                    for owner in range(owners)
                ],
                0,
            )
        )
    sums = [jnp.sum(gsmall[8 * i : 8 * i + 8, :], 0, keepdims=True) for i in range(4)]
    bias_row = jnp.sum(gbias[...], 0, keepdims=True)
    block = jnp.concatenate(
        sums + [bias_row[:, i * features : (i + 1) * features] for i in range(pieces)], 0
    )
    block = jnp.concatenate([block, jnp.zeros((share - 8, features), f32)], 0)
    small = jnp.concatenate([block] * owners, 0)
    block_scr[...] = jnp.zeros_like(block_scr)
    stack_blocks(jnp.concatenate([proj, gup[...]] + down_pieces + [small], 1), block_scr)
    split_owners(block_scr, mine_ref, theirs_ref, (0, 4, 2, 6))


SMALL_ROWS = 168
DENSE_ROWS = 128
LATE_ROWS = 128


def back_attend_kernel(
    head, qraw_ref, kvraw_ref, soft_ref, gatt_ref, key_ref, val_ref,
    gain_scr, table_ref,
    gpadded, gkeypad, sums_ref,
    keyaug_scr, gtable, gkey, gval, gsums,
):
    cols = gpadded.shape[1] - 16
    rows = gpadded.shape[0] - 2
    tile = BACK_ROWS * cols
    chunks = rows // BACK_ROWS
    key_cols = cols // 2
    key_rows = rows // 2
    key_total = kvraw_ref.shape[1]
    clear_rim(gpadded)
    gkeypad[...] = jnp.zeros_like(gkeypad)
    table = table_ref[...]
    gsums[...] = jnp.zeros_like(gsums)

    key_place = lax.broadcasted_iota(jnp.int32, (key_total, LANES), 0)
    lanes = lane_ids((key_total, LANES))
    hot = (
        (lanes == 30 - 2 * (key_place // key_cols)) | (lanes == 94 - 2 * (key_place % key_cols))
    ).astype(bf16)
    keyaug_scr[:, 0:LANES] = key_ref[head]
    keyaug_scr[:, LANES : 2 * LANES] = hot

    scale_factor = HEAD_DIM ** (-0.5)
    tile_mask = head_mask(tile)
    row_lanes = lane_ids((cols, LANES))

    def attend(step, carry):
        span = pl.ds(pl.multiple_of(step * tile, tile), tile)
        unit, scale = head_norm_parts(qraw_ref[head, span, :], tile_mask)
        query = (unit * gain_scr[0:1, :] + gain_scr[3:4, :]).astype(bf16)
        gatt = gatt_ref[span, head * LANES : (head + 1) * LANES]
        soft_low = soft_ref[head, span, :]
        soft = soft_low.astype(f32)
        gsoft = dot(gatt, val_ref[head], NT)
        inner = jnp.sum(soft * gsoft, -1, keepdims=True)
        gscore = (soft * (gsoft - inner)).astype(bf16)
        gkey[...] = dot(query, gscore, TN)
        gval[...] = dot(gatt, soft_low, TN)
        wide = dot(gscore, keyaug_scr[...])
        gterm = wide[:, LANES : 2 * LANES]
        pieces = []
        for row in range(BACK_ROWS):
            part = gterm[row * cols : (row + 1) * cols, :]
            place = step * BACK_ROWS + row
            by_row = pltpu.roll(part, place, 1)
            by_col = pltpu.roll(part, 0, 1, stride=1, stride_axis=0)
            pieces.append(jnp.where(row_lanes < 64, by_row, by_col))
        glook = jnp.concatenate(pieces, 0).astype(bf16)
        gtable[...] = dot(glook, query, TN)
        gquery = scale_factor * wide[:, 0:LANES] + gatt.astype(f32) + dot(glook, table)
        gsums[0:8, :] = fold_rows(gquery * unit)
        gsums[8:16, :] = fold_rows(gquery)
        graw = norm_back(gquery * gain_scr[0:1, :], unit, scale, HEAD_DIM) * tile_mask
        gpadded[pl.ds(1 + step * BACK_ROWS, BACK_ROWS), 8 : 8 + cols, :] = graw.reshape(
            BACK_ROWS, cols, LANES
        )
        return carry

    lax.fori_loop(0, chunks, attend, 0, unroll=True)

    key_mask = head_mask(key_total)
    for member, grad in ((1, gkey[...].T * scale_factor), (2, gval[...].T)):
        unit, scale = head_norm_parts(kvraw_ref[(member - 1) * HEADS + head], key_mask)
        base = 16 if member == 1 else 24
        gsums[base : base + 8, :] += fold_rows(grad * unit)
        if member == 2:
            gsums[32:40, :] += fold_rows(grad)
        graw = norm_back(grad * gain_scr[member : member + 1, :], unit, scale, HEAD_DIM) * key_mask
        gkeypad[member - 1, 0:key_rows, 0:key_cols, :] = graw.reshape(key_rows, key_cols, LANES)

    sums_ref[...] = jnp.zeros_like(sums_ref)
    sums_ref[0:63, :] = gtable[0:63, :]
    sums_ref[63:126, :] = gtable[64:127, :]
    for place, base in enumerate((0, 16, 24, 8, 32)):
        sums_ref[126 + place : 127 + place, :] = jnp.sum(gsums[base : base + 8, :], 0, keepdims=True)


def back_weights_kernel(
    img_ref, padded, gpadded_0, gpadded_1, gkeypad_0, gkeypad_1, sums_0, sums_1, weight_ref, columns_ref, kern_scr,
    gmix_scr, mine_ref, theirs_ref,
    gmixrow, gkern, gweight, gbias, small_scr, dense_scr, block_scr,
):
    tokens, features = img_ref.shape
    cols = padded.shape[2] - 16
    rows = padded.shape[1] - 2
    tile = CHUNK_ROWS * cols
    chunks = rows // CHUNK_ROWS
    key_cols = cols // 2
    key_rows = rows // 2
    gkern[...] = jnp.zeros_like(gkern)

    def spread_queries(step, carry):
        span = pl.ds(pl.multiple_of(step * tile, tile), tile)
        around = pl.ds(step * CHUNK_ROWS, CHUNK_ROWS + 2)
        for head, gpadded in enumerate((gpadded_0, gpadded_1)):
            total = jnp.zeros((CHUNK_ROWS, cols, LANES), f32)
            own = gpadded[pl.ds(1 + step * CHUNK_ROWS, CHUNK_ROWS), 8 : 8 + cols, :]
            for side in range(3):
                window = gpadded[around, 9 - side : 9 - side + cols, :]
                cells = padded[head, around, 7 + side : 7 + side + cols, :]
                for up in range(3):
                    tap = 3 * up + side
                    total = total + window[2 - up : 2 - up + CHUNK_ROWS] * kern_scr[tap, 0:1, :]
                    gkern[tap] += fold_rows((own * cells[up : up + CHUNK_ROWS]).reshape(tile, LANES))
            flat = total.reshape(tile, LANES).astype(bf16)
            gmix_scr[span, head * LANES : (head + 1) * LANES] = flat
        return carry

    lax.fori_loop(0, chunks, spread_queries, 0, unroll=True)

    evens = pl.ds(0, key_cols, stride=2)
    odds = pl.ds(1, key_cols, stride=2)
    for place in range(2 * HEADS):
        member = 1 + place // HEADS
        taps = [kern_scr[tap, member : member + 1, :] for tap in range(9)]
        gkeypad = (gkeypad_0, gkeypad_1)[place % HEADS].at[place // HEADS]
        left = gkeypad[0 : key_rows + 1, 0:key_cols, :]
        right = gkeypad[0 : key_rows + 1, 1 : 1 + key_cols, :]
        here, below, beside, cross = left[:key_rows], left[1:], right[:key_rows], right[1:]
        gmixrow[:, 0, evens, :] = here * taps[4]
        gmixrow[:, 0, odds, :] = beside * taps[3] + here * taps[5]
        gmixrow[:, 1, evens, :] = below * taps[1] + here * taps[7]
        gmixrow[:, 1, odds, :] = (
            cross * taps[0] + below * taps[2] + beside * taps[6] + here * taps[8]
        )
        lane = (HEADS + place) * LANES
        gmix_scr[:, lane : lane + LANES] = gmixrow[...].reshape(rows * cols, LANES).astype(bf16)
        for side in range(3):
            for up, cells in enumerate(stride_windows(padded, HEADS + place, side, key_rows, key_cols)):
                gkern[9 * member + 3 * up + side] += fold_rows(
                    (here * cells).reshape(key_rows * key_cols, LANES)
                )

    def weigh(step, carry):
        span = pl.ds(pl.multiple_of(step * WEIGH_TILE, WEIGH_TILE), WEIGH_TILE)
        unit, _ = norm_parts(img_ref[span, :].astype(f32), features)
        gmix = gmix_scr[span, :]
        gweight[...] = dot(unit.astype(bf16), gmix, TN)
        gbias[...] = fold_rows(gmix.astype(f32))
        return carry

    lax.fori_loop(0, tokens // WEIGH_TILE, weigh, 0, unroll=True)

    bias_row = jnp.sum(gbias[...], 0, keepdims=True)
    weight = weight_ref[...].astype(f32)
    raw = gweight[...]
    lanes = lane_ids((features, LANES))
    norm_sums = jnp.where(
        lanes == 0,
        jnp.sum(weight * raw, 1, keepdims=True),
        jnp.where(lanes == 1, jnp.sum(weight * bias_row, 1, keepdims=True), 0.0),
    )
    norm_rows = jnp.concatenate([norm_sums, jnp.zeros((2 * LANES - features, LANES), f32)], 0).T
    gweight[...] = raw * columns_ref[0:features, 16:17] + columns_ref[0:features, 0:1] * bias_row

    for tap in range(27):
        row = 3 * (tap % 9) + tap // 9
        small_scr[row : row + 1, :] = jnp.sum(gkern[tap], 0, keepdims=True)
    small_scr[27:158, :] = sums_0[0:131, :] + sums_1[0:131, :]
    for place in range(3 * HEADS):
        small_scr[158 + place : 159 + place, :] = bias_row[:, place * LANES : (place + 1) * LANES]
    for place in range(2):
        for head in range(HEADS):
            at = 164 + HEADS * place + head
            small_scr[at : at + 1, :] = head_piece(norm_rows[place : place + 1, :], head * HEAD_DIM)
    weights = jnp.concatenate(
        [gweight[:, place * LANES : place * LANES + HEAD_DIM] for place in range(3 * HEADS)]
        + [jnp.zeros((features, 64), f32)],
        1,
    )
    block_scr[...] = jnp.zeros_like(block_scr)
    stack_blocks(weights, block_scr)
    split_owners(block_scr, mine_ref, theirs_ref, (0, 2, 4, 6))
    count = block_scr.shape[1]
    dense_scr[...] = jnp.zeros_like(dense_scr)
    dense_scr[0:126, :] = small_scr[0:126, :] * head_mask(126)
    beside = lane_ids((42, LANES)) >= HEAD_DIM
    for piece in range(3):
        moved = small_scr[126:168, :]
        moved = pltpu.roll(moved, HEAD_DIM - 32 * piece, 1)
        dense_scr[42 * piece : 42 * (piece + 1), :] += jnp.where(beside, moved, 0.0)
    small = dense_scr[...].astype(bf16)
    mine_ref[4 * count :, :] = small
    theirs_ref[4 * count :, :] = small


def back_images_kernel(img_ref, gmix_ref, gmid_ref, weight_ref, rows_ref, gimg_ref):
    tokens, features = img_ref.shape
    tile = IMAGE_TILE
    block = tokens // 4
    gain_one = rows_ref[16:17, 0:features]

    def finish(step, carry):
        span = pl.ds(pl.multiple_of(step * tile, tile), tile)
        unit, scale = norm_parts(img_ref[span, :].astype(f32), features)
        gnorm = dot(gmix_ref[span, :], weight_ref[...], NT)
        gimg = gmid_ref[span, :].astype(f32) + norm_back(gnorm * gain_one, unit, scale, features)
        for place in range(tile // block):
            gimg_ref[step * (tile // block) + place] = fold_block(
                gimg[place * block : (place + 1) * block, :]
            ).astype(bf16)
        return carry

    lax.fori_loop(0, tokens // tile, finish, 0, unroll=True)


def halve_kernel(mine_ref, got_ref, keep_ref, send_ref):
    half = keep_ref.shape[0]
    total = (mine_ref[...].astype(f32) + got_ref[...].astype(f32)).astype(bf16)
    keep_ref[...] = total[:half]
    send_ref[...] = total[half:]


def pair_kernel(shared, mine_ref, got_ref, own_ref, msg_1, msg_2, msg_3):
    total = (mine_ref[...].astype(f32) + got_ref[...].astype(f32)).astype(bf16)
    count = (total.shape[0] - shared) // 4
    for place, out in enumerate((own_ref, msg_1, msg_2, msg_3)):
        out[0:count, :] = total[place * count : (place + 1) * count]
        if shared:
            out[count:, :] = total[4 * count :]


def chips_sum(own_ref, got_1, got_2, got_3):
    return (own_ref[...].astype(f32) + got_1[...].astype(f32)) + (
        got_2[...].astype(f32) + got_3[...].astype(f32)
    )


def two_kernel(own_ref, got_ref, out_ref):
    out_ref[...] = (own_ref[...].astype(f32) + got_ref[...].astype(f32)).astype(bf16)


def four_kernel(own_ref, got_1, got_2, got_3, out_ref):
    out_ref[...] = chips_sum(own_ref, got_1, got_2, got_3).astype(bf16)


def pictures_kernel(out_0, out_1, out_2, out_3, gimg_low, out_ref, gimg_ref):
    for shift in range(4):
        gimg_ref[shift] = unfold_block(gimg_low[shift].astype(f32))
        block = (out_0, out_1, out_2, out_3)[shift][...]
        out_ref[turned(4 - shift)] = unfold_block(block.astype(f32)).astype(bf16)


def finish_kernel(
    early_0, early_1, late_0, late_1,
    gqkv_ref, gproj_ref, gup_ref, gdown_ref, ggain_ref, gshift_ref, gkern_ref,
    gpgain_ref, gpshift_ref, grelh_ref, grelw_ref,
    small_scr, dense_scr,
):
    share, features = gproj_ref.shape
    hidden = gup_ref.shape[1]
    pieces = hidden // features
    early = early_0[...].astype(f32) + early_1[...].astype(f32)
    early = jnp.concatenate(
        [early[share * i : share * (i + 1), :] for i in range((2 * features + 2 * hidden) // LANES)], 1
    )
    gproj_ref[...] = early[:, 0:features]
    gup_ref[...] = early[:, features : features + hidden]
    for piece in range(pieces):
        start = features + hidden + piece * features
        gdown_ref[piece * share : (piece + 1) * share, :] = early[:, start : start + features]
    start = features + 2 * hidden
    block = early[0:8, start : start + features]
    late = late_0[...].astype(f32) + late_1[...].astype(f32)
    gqkv_ref[...] = jnp.concatenate([late[share * i : share * (i + 1), :] for i in range(5)], 1)[
        :, 0 : 3 * features
    ]
    dense = late[LATE_ROWS : LATE_ROWS + DENSE_ROWS, :]
    small_scr[0:126, :] = dense[0:126, :]
    dense_scr[...] = dense
    lanes = lane_ids((42, LANES))
    rest = jnp.zeros((42, LANES), f32)
    for piece in range(3):
        moved = pltpu.roll(dense_scr[42 * piece : 42 * (piece + 1), :], 32 + 32 * piece, 1)
        rest = jnp.where((lanes >= 32 * piece) & (lanes < 32 * piece + 32), moved, rest)
    small_scr[126:168, :] = rest
    for tap in range(9):
        gkern_ref[tap] = small_scr[3 * tap : 3 * tap + 3, 0:HEAD_DIM]
    gpgain_ref[...] = small_scr[153:156, 0:HEAD_DIM]
    gpshift_ref[...] = small_scr[156:158, 0:HEAD_DIM]
    grelh_ref[...] = small_scr[27:90, 0:HEAD_DIM]
    grelw_ref[...] = small_scr[90:153, 0:HEAD_DIM]
    ggain_ref[1:2, :] = block[0:1, :]
    gshift_ref[1:2, :] = block[1:2, :]
    for head in range(HEADS):
        lanes = slice(head * HEAD_DIM, (head + 1) * HEAD_DIM)
        ggain_ref[0:1, lanes] = small_scr[164 + head : 165 + head, 0:HEAD_DIM]
        gshift_ref[0:1, lanes] = small_scr[166 + head : 167 + head, 0:HEAD_DIM]
        for section in range(3):
            row = 158 + section * HEADS + head
            gshift_ref[2 + section : 3 + section, lanes] = small_scr[row : row + 1, 0:HEAD_DIM]
    gshift_ref[5:6, :] = block[2:3, :]
    gshift_ref[6 : 6 + pieces, :] = block[4 : 4 + pieces, :]
    gshift_ref[6 + pieces : 7 + pieces, :] = block[3:4, :]


LONG = {"back_attend_1": 2 * 10**10}


def call(kernel, name, outs, scratch, flops, limit, spaces, out_spaces, *args):
    place = {"v": pltpu.VMEM, "p": pltpu.VMEM, "h": pltpu.HBM, "a": pl.ANY}
    keep = {"p": pltpu.VMEM, "h": pltpu.HBM}
    args = [
        pltpu.with_memory_space_constraint(a, keep[c]) if c in keep else a for c, a in zip(spaces, args)
    ]
    outs = [keep[c](o.shape, o.dtype) if c in keep else o for c, o in zip(out_spaces, outs)]
    return pl.pallas_call(
        kernel,
        name=name,
        out_shape=outs,
        in_specs=[pl.BlockSpec(memory_space=place[c]) for c in spaces],
        out_specs=[pl.BlockSpec(memory_space=place[c]) for c in out_spaces],
        scratch_shapes=scratch,
        cost_estimate=pl.CostEstimate(flops=LONG.get(name, 1), bytes_accessed=LONG.get(name, 1) // 500, transcendentals=0),
        compiler_params=pltpu.CompilerParams(vmem_limit_bytes=limit * 2**20),
    )(*args)


KA_LIMIT = 36


def whole_image(
    images,
    w_qkv,
    w_proj,
    w_up,
    w_down,
    gains_main,
    shifts_main,
    pool_kernels,
    pool_gains,
    pool_shifts,
    rel_height,
    rel_width,
    cotangent,
):
    owners = lax.axis_size("batch")
    cycle = lax.axis_size("rows")
    image_count, row_count, cols, features = images.shape
    rows = row_count * cycle
    tokens = rows * cols
    hidden = w_up.shape[1]
    share = w_proj.shape[0]
    pieces = hidden // features
    key_total = tokens // 4
    early_used = (2 * features + 2 * hidden) // LANES * share
    early_rows = -(-early_used // 16) * 16
    def shaped(shape, dtype):
        return jax.ShapeDtypeStruct(shape, dtype)

    block = tokens // cycle
    folded = (block * features // LANES, LANES)
    width = 4 * features + 2 * hidden

    def send_on(pieces):
        return list(pieces[:1]) + [
            lax.ppermute(pieces[k], "rows", [(i, (i + k) % cycle) for i in range(cycle)])
            for k in range(1, cycle)
        ]

    def trade(cells, flip):
        return lax.ppermute(cells, "batch", [(i, i ^ flip) for i in range(owners)])

    img = call(
        fold_images_kernel,
        "fold_images",
        [shaped((cycle,) + folded, bf16)],
        [pltpu.VMEM((cycle, block, features), bf16), pltpu.SemaphoreType.DMA((4,))],
        1,
        4,
        "h",
        "v",
        images.reshape(cycle, block, features),
    )[0]
    img, w_qkv = lax.optimization_barrier((img, w_qkv))
    img = lax.all_to_all(img, "rows", 0, 0, tiled=True)
    packed = call(
        pack_kernel,
        "pack",
        [shaped((share, width), bf16)],
        [pltpu.VMEM(w.shape, bf16) for w in (w_qkv, w_proj, w_up, w_down)]
        + [pltpu.SemaphoreType.DMA((4,))],
        10**6,
        4,
        "hhhh",
        "v",
        w_qkv, w_proj, w_up, w_down,
    )[0]
    packed, cotangent = lax.optimization_barrier((packed, cotangent))
    cot_pieces = call(
        fold_kernel,
        "fold",
        [shaped(folded, bf16)] * cycle,
        [
            pltpu.VMEM((cycle, block, features), bf16),
            pltpu.VMEM((cycle,) + folded, bf16),
            pltpu.SemaphoreType.DMA((4,)),
            pltpu.SemaphoreType.DMA((4,)),
        ],
        10**6,
        8,
        "h",
        "a" * 4,
        cotangent.reshape(cycle, block, features),
    )
    img, cot_pieces, *shards = lax.optimization_barrier(
        (img, cot_pieces, *[trade(packed, flip) for flip in (2, 4, 6)])
    )
    own = jnp.stack([packed, *shards])
    other = trade(own, 1)
    taps = pool_kernels.transpose(1, 0, 2)
    small = (gains_main, shifts_main, taps, pool_gains, pool_shifts, rel_height, rel_width)
    wide, full_proj, full_up, full_down, biases, lines, columns, taps_wide, pool_lines, ahead, behind = call(
        functools.partial(weights_kernel, owners),
        "weights",
        [
            shaped((features, 3 * HEADS * LANES), bf16),
            shaped((HEADS * LANES, features), bf16),
            shaped((features, hidden), bf16),
            shaped((hidden, features), bf16),
            shaped((8, hidden), f32),
            shaped((24, 2 * LANES), f32),
            shaped((2 * LANES, LANES), f32),
            shaped((9, 8, LANES), f32),
            shaped((8, LANES), f32),
            shaped((LANES, LANES), bf16),
            shaped((LANES, LANES), bf16),
        ],
        [pltpu.VMEM((features, width), f32), pltpu.VMEM((hidden, features), f32)]
        + [pltpu.VMEM(a.shape, bf16) for a in small]
        + [pltpu.VMEM((LANES, LANES), f32), pltpu.SemaphoreType.DMA((7,))],
        10**6,
        12,
        "vv" + "h" * 7,
        "v" * 11,
        own, other, *small,
    )
    cot_pieces = send_on(cot_pieces)
    whole = [
        shaped((3 * HEADS, rows + 2, cols + 16, LANES), f32),
        shaped((HEADS, tokens, LANES), f32),
        shaped((2 * HEADS, key_total, LANES), f32),
        shaped((HEADS, tokens, key_total), bf16),
        shaped((tokens, HEADS * LANES), bf16),
    ]
    img, padded, qraw, kvraw, soft, att, keys, values = call(
        attend_kernel,
        "attend",
        [shaped((tokens, features), bf16)] + whole + [shaped((HEADS, key_total, LANES), bf16)] * 2,
        [
            pltpu.VMEM((HEADS, tokens, LANES), bf16),
            pltpu.VMEM((HEADS, key_total, 2 * LANES), bf16),
        ],
        10**10,
        KA_LIMIT,
        "v" * 7,
        "p" * 8,
        img, wide, biases, lines, taps_wide, pool_lines, ahead,
    )
    *out_pieces, normed, unit, scale, active, slope = call(
        feed_ahead_kernel,
        "feed_ahead",
        [shaped(folded, bf16)] * cycle
        + [
            shaped((tokens, features), bf16),
            shaped((tokens, features), f32),
            shaped((tokens, LANES), f32),
            shaped((tokens, hidden), bf16),
            shaped((tokens, hidden), f32),
        ],
        [pltpu.VMEM((cycle,) + folded, bf16), pltpu.SemaphoreType.DMA((4,))],
        1,
        36,
        "pp" + "v" * 5,
        "a" * cycle + "p" * 5,
        img, att, full_proj, full_up, full_down, biases, lines,
    )
    gmid, gatt, mine, theirs = call(
        functools.partial(feed_back_kernel, owners),
        "feed_back",
        [shaped((tokens, features), bf16), shaped((tokens, HEADS * LANES), bf16)]
        + [shaped((4 * early_rows, LANES), bf16)] * 2,
        [
            pltpu.VMEM((features, hidden), f32),
            pltpu.VMEM((features, hidden), f32),
            pltpu.VMEM((HEADS * LANES, features), f32),
            pltpu.VMEM((8, hidden), f32),
            pltpu.VMEM((32, features), f32),
            pltpu.VMEM((owners, early_rows, LANES), f32),
            pltpu.VMEM((cycle,) + folded, bf16),
            pltpu.SemaphoreType.DMA((4,)),
        ],
        1,
        36,
        "p" + "a" * 4 + "p" * 5 + "v" * 4,
        "pp" + "vv",
        att, *cot_pieces, normed, unit, scale, active, slope, full_proj, full_up, full_down, lines,
    )

    def halved(mine, got):
        return call(
            halve_kernel,
            "halve",
            [shaped((mine.shape[0] // 2, LANES), bf16)] * 2,
            [],
            10**6,
            4,
            "vv",
            "vv",
            mine, got,
        )

    got = trade(theirs, 1)

    def back_attend(head, behind):
        return call(
            functools.partial(back_attend_kernel, head),
            f"back_attend_{head}",
            [
                shaped((rows + 2, cols + 16, LANES), f32),
                shaped((2, rows // 2 + 1, cols // 2 + 8, LANES), f32),
                shaped((136, LANES), f32),
            ],
            [
                pltpu.VMEM((key_total, 2 * LANES), bf16),
                pltpu.VMEM((LANES, LANES), f32),
                pltpu.VMEM((LANES, key_total), f32),
                pltpu.VMEM((LANES, key_total), f32),
                pltpu.VMEM((40, LANES), f32),
            ],
            10**10,
            30,
            "p" * 6 + "vv",
            "ppp",
            qraw, kvraw, soft, gatt, keys, values, pool_lines, behind,
        )

    gpadded_0, gkeypad_0, sums_0 = back_attend(0, behind)
    got, gkeypad_0, behind = lax.optimization_barrier((got, gkeypad_0, behind))
    early, away = halved(mine, got)
    away = trade(away, 2)
    out_pieces = send_on(out_pieces)
    gpadded_1, gkeypad_1, sums_1 = back_attend(1, behind)
    gmix, mine, theirs = call(
        back_weights_kernel,
        "back_weights",
        [shaped((tokens, 3 * HEADS * LANES), bf16)]
        + [shaped((4 * LATE_ROWS + DENSE_ROWS, LANES), bf16)] * 2,
        [
            pltpu.VMEM((rows // 2, 2, cols, LANES), f32),
            pltpu.VMEM((27, 8, LANES), f32),
            pltpu.VMEM((features, 3 * HEADS * LANES), f32),
            pltpu.VMEM((8, 3 * HEADS * LANES), f32),
            pltpu.VMEM((SMALL_ROWS, LANES), f32),
            pltpu.VMEM((DENSE_ROWS, LANES), f32),
            pltpu.VMEM((owners, LATE_ROWS, LANES), f32),
        ],
        10**10,
        30,
        "p" + "p" * 7 + "v" * 3,
        "pvv",
        img, padded, gpadded_0, gpadded_1, gkeypad_0, gkeypad_1, sums_0, sums_1, wide, columns, taps_wide,
    )

    def summed(kernel, *pieces):
        return call(
            kernel,
            "sum_four" if len(pieces) == 4 else "sum_two",
            [shaped(pieces[0].shape, bf16)],
            [],
            1,
            4,
            "v" * len(pieces),
            "v",
            *pieces,
        )[0]

    def ring_trade(cells, flip):
        return lax.ppermute(cells, "rows", [(i, i ^ flip) for i in range(cycle)])

    away, out_pieces, gmix, mine, theirs = lax.optimization_barrier(
        (away, out_pieces, gmix, mine, theirs)
    )
    early, away = halved(early, away)
    away = trade(away, 4)
    got = trade(theirs, 1)
    gimg = call(
        back_images_kernel,
        "back_images",
        [shaped((cycle,) + folded, bf16)],
        [],
        10**10,
        24,
        "pppvv",
        "v",
        img, gmix, gmid, wide, lines,
    )[0]
    got, gimg = lax.optimization_barrier((got, gimg))
    gimg = lax.all_to_all(gimg, "rows", 0, 0, tiled=True)
    early = summed(two_kernel, early, away)
    early = summed(two_kernel, early, ring_trade(early, 1))
    away = ring_trade(early, 2)
    own, *apart = call(
        functools.partial(pair_kernel, DENSE_ROWS),
        "pair",
        [shaped((LATE_ROWS + DENSE_ROWS, LANES), bf16)] * 4,
        [],
        10**6,
        4,
        "vv",
        "vvvv",
        mine, got,
    )
    late = summed(four_kernel, own, *[trade(apart[k], 2 * k + 2) for k in range(3)])
    late = summed(two_kernel, late, ring_trade(late, 1))
    late_away = ring_trade(late, 2)
    output, grad_images = call(
        pictures_kernel,
        "pictures",
        [shaped((cycle, block, features), bf16), shaped((cycle, block, features), f32)],
        [],
        1,
        16,
        "v" * 5,
        "v" * 2,
        *out_pieces, gimg,
    )
    late, output, grad_images = lax.optimization_barrier((late, output, grad_images))
    grads = call(
        finish_kernel,
        "finish",
        [
            shaped((share, 3 * features), f32),
            shaped((share, features), f32),
            shaped((share, hidden), f32),
            shaped((share * pieces, features), f32),
            shaped(gains_main.shape, f32),
            shaped(shifts_main.shape, f32),
            shaped(taps.shape, f32),
            shaped(pool_gains.shape, f32),
            shaped(pool_shifts.shape, f32),
            shaped(rel_height.shape, f32),
            shaped(rel_width.shape, f32),
        ],
        [pltpu.VMEM((SMALL_ROWS, LANES), f32), pltpu.VMEM((DENSE_ROWS, LANES), f32)],
        10**8,
        16,
        "v" * 4,
        "v" * 11,
        early, away, late, late_away,
    )
    grads = list(grads)
    grads[6] = grads[6].transpose(1, 0, 2)
    return (output.reshape(images.shape), grad_images.reshape(images.shape), *grads)

def per_device(images, *rest):
    cycle = lax.axis_size("rows")
    image_count, row_count, cols, _ = images.shape
    fits = image_count == cycle and row_count * cycle == 32 and cols == 32
    return whole_image(images, *rest) if fits else row_sharded(images, *rest)


def solution(mesh):
    return jax.shard_map(
        per_device,
        mesh=mesh,
        in_specs=(
            P("batch", "rows", None, None),
            P("batch", None),
            P("batch", None),
            P("batch", None),
            P("batch", None),
            P(),
            P(),
            P(),
            P(),
            P(),
            P(),
            P(),
            P("batch", "rows", None, None),
        ),
        out_specs=(
            P("batch", "rows", None, None),
            P("batch", "rows", None, None),
            P("batch", None),
            P("batch", None),
            P("batch", None),
            P("batch", None),
            P(),
            P(),
            P(),
            P(),
            P(),
            P(),
            P(),
        ),
        check_vma=False,
    )
```

```python
import functools

import jax
import jax.numpy as jnp
from jax import lax
from jax.experimental import pallas as pl
from jax.experimental.pallas import tpu as pltpu
from jax.sharding import PartitionSpec as P

HEADS = 2
HEAD_DIM = 96


norm_eps = 1e-06
highest = lax.Precision.HIGHEST


def padded(cells, sides, width):
    for axis, dim in sides:
        count = lax.axis_size(axis)
        ends = count - 1
        head = lax.slice_in_dim(cells, 0, width, axis=dim)
        tail = lax.slice_in_dim(cells, cells.shape[dim] - width, cells.shape[dim], axis=dim)
        cells = jnp.concatenate(
            [
                lax.ppermute(tail, axis, [(i, (i + 1) % count) for i in range(ends)]),
                cells,
                lax.ppermute(head, axis, [((i + 1) % count, i) for i in range(ends)]),
            ],
            axis=dim,
        )
    return cells


def layer_norm(values, gains, shifts):
    centre = jnp.mean(values, -1, keepdims=True)
    centred = values - centre
    spread = jnp.mean(centred * centred, -1, keepdims=True)
    return centred * lax.rsqrt(spread + norm_eps) * gains + shifts


def gelu_tanh(values):
    return jax.nn.gelu(values, approximate=True)


def pool_section(section, kernel, stride):
    image_count, ext_rows, col_count, features = section.shape
    out_rows = (ext_rows - 2) // stride
    out_cols = col_count // stride
    col_out = jnp.arange(out_cols)[:, None] * stride
    col_in = jnp.arange(col_count)[None, :]
    shifted = []
    for offset_col in range(3):
        picker = (col_out + offset_col - 1 == col_in).astype(jnp.float32)
        shifted.append(jnp.einsum("jy,bxyc->bxjc", picker, section, precision=highest))
    summed = jnp.zeros((image_count, out_rows, out_cols, features), jnp.float32)
    for offset_row in range(3):
        for offset_col in range(3):
            window = shifted[offset_col][:, offset_row : offset_row + ext_rows - 2]
            if stride == 2:
                window = window.reshape(image_count, out_rows, 2, out_cols, features)[:, :, 0]
            summed = summed + window * kernel[3 * offset_row + offset_col]
    return summed


def pooled_local(extended_f, kernels, gains, shifts):
    features = extended_f.shape[-1]
    head_dim = kernels.shape[-1]
    head_count = features // head_dim
    results = []
    for member, stride in ((0, 1), (1, 2), (2, 2)):
        pooled = pool_section(
            extended_f[member], jnp.tile(kernels[member], (1, head_count)), stride
        )
        pooled = pooled.reshape(pooled.shape[:-1] + (head_count, head_dim))
        offset = (
            shifts[0] if member == 0 else shifts[1] if member == 2 else jnp.zeros_like(shifts[0])
        )
        results.append(layer_norm(pooled, gains[member], offset))
    return tuple(results)


def row_sharded(
    images,
    w_qkv,
    w_proj,
    w_up,
    w_down,
    gains_main,
    shifts_main,
    pool_kernels,
    pool_gains,
    pool_shifts,
    rel_height,
    rel_width,
    cotangent,
):
    image_count, row_count, col_count, features = images.shape
    head_dim = HEAD_DIM
    head_count = HEADS
    scale_factor = head_dim ** (-0.5)
    cycle_size = lax.axis_size("rows")
    key_rows_all = row_count * cycle_size // 2
    key_cols = col_count // 2
    key_total = key_rows_all * key_cols
    query_count = row_count * col_count
    key_local = row_count // 2 * key_cols
    gain_rows = gains_main.astype(jnp.float32)
    shift_rows = shifts_main.astype(jnp.float32)
    full_qkv, full_proj, full_up, full_down = (
        lax.all_gather(w_qkv, "batch", axis=0, tiled=True),
        lax.all_gather(w_proj, "batch", axis=0, tiled=True),
        lax.all_gather(w_up, "batch", axis=0, tiled=True),
        lax.all_gather(w_down, "batch", axis=0, tiled=True),
    )
    qkv_split = full_qkv.reshape(features, 3, features)
    inputs_f = images.astype(jnp.float32)
    normed_one, norm_one_pullback = jax.vjp(layer_norm, inputs_f, gain_rows[0], shift_rows[0])
    normed_low = normed_one.astype(jnp.bfloat16)
    mixed = (
        jnp.einsum("bxyd,dme->mbxye", normed_low, qkv_split, preferred_element_type=jnp.float32)
        + shift_rows[2:5][:, None, None, None, :]
    )
    mixed_low = mixed.astype(jnp.bfloat16)
    extended = padded(mixed_low, (("rows", 2),), 1)
    (queries, keys_pooled, values_pooled), pool_pullback = jax.vjp(
        pooled_local,
        extended.astype(jnp.float32),
        pool_kernels.astype(jnp.float32),
        pool_gains.astype(jnp.float32),
        pool_shifts.astype(jnp.float32),
    )
    queries_low = queries.astype(jnp.bfloat16)
    query_flat = queries_low.reshape(image_count, query_count, head_count, head_dim)
    keys_low = keys_pooled.astype(jnp.bfloat16).reshape(image_count, key_local, features)
    values_low = values_pooled.astype(jnp.bfloat16).reshape(image_count, key_local, features)
    key_value = jnp.concatenate([keys_low, values_low], -1)
    first_row = lax.axis_index("rows") * row_count

    def rel_terms(query_vals, table_height, table_width):
        row_place = first_row + jnp.arange(row_count)
        dist_height = (
            row_place[:, None] - 2 * jnp.arange(key_rows_all)[None, :] + 2 * (key_rows_all - 1)
        )
        pick_height = (
            dist_height[:, :, None] == jnp.arange(table_height.shape[0])[None, None, :]
        ).astype(jnp.float32)
        lookup_height = jnp.einsum("xjt,tc->xjc", pick_height, table_height, precision=highest)
        dist_width = (
            jnp.arange(col_count)[:, None] - 2 * jnp.arange(key_cols)[None, :] + 2 * (key_cols - 1)
        )
        pick_width = (
            dist_width[:, :, None] == jnp.arange(table_width.shape[0])[None, None, :]
        ).astype(jnp.float32)
        lookup_width = jnp.einsum("yjt,tc->yjc", pick_width, table_width, precision=highest)
        term_height = jnp.einsum("bxyhc,xjc->bhxyj", query_vals, lookup_height, precision=highest)
        term_width = jnp.einsum("bxyhc,yjc->bhxyj", query_vals, lookup_width, precision=highest)
        return (term_height, term_width)

    (term_height, term_width), rel_pullback = jax.vjp(
        rel_terms,
        queries_low.astype(jnp.float32),
        rel_height.astype(jnp.float32),
        rel_width.astype(jnp.float32),
    )
    rel_full = (term_height[..., :, None] + term_width[..., None, :]).reshape(
        image_count, head_count, query_count, key_total
    )

    def key_scores(key_piece):
        piece_rows = key_piece.shape[1]
        keys_part = key_piece[..., :features].reshape(image_count, piece_rows, head_count, head_dim)
        products = jnp.einsum(
            "bqhc,bkhc->bhqk", query_flat, keys_part, preferred_element_type=jnp.float32
        )
        return products * scale_factor + lax.slice_in_dim(rel_full, 0, piece_rows, axis=3)

    key_piece = lax.all_gather(key_value, "rows", axis=1, tiled=True)
    run_max = jnp.full((image_count, head_count, query_count), -1e30, jnp.float32)
    run_sum = jnp.zeros((image_count, head_count, query_count), jnp.float32)
    run_acc = jnp.zeros((image_count, head_count, query_count, head_dim), jnp.float32)
    piece_rows = key_piece.shape[1]
    values_part = key_piece[..., features:].reshape(image_count, piece_rows, head_count, head_dim)
    scores = key_scores(key_piece)
    new_max = jnp.maximum(run_max, jnp.max(scores, -1))
    weights_exp = jnp.exp(scores - new_max[..., None])
    factor = jnp.exp(run_max - new_max)
    run_sum = run_sum * factor + jnp.sum(weights_exp, -1)
    run_acc = run_acc * factor[..., None] + jnp.einsum(
        "bhqk,bkhc->bhqc", weights_exp, values_part.astype(jnp.float32), precision=highest
    )
    run_max, run_sum, run_acc = (new_max, run_sum, run_acc)
    log_total = run_max + jnp.log(run_sum)
    attended = (run_acc / run_sum[..., None]).transpose(0, 2, 1, 3) + query_flat.astype(jnp.float32)
    attended_low = attended.reshape(image_count, row_count, col_count, features).astype(
        jnp.bfloat16
    )
    branch = (
        jnp.einsum("bxyd,de->bxye", attended_low, full_proj, preferred_element_type=jnp.float32)
        + shift_rows[5]
    )
    middle = inputs_f + branch
    normed_two, norm_two_pullback = jax.vjp(layer_norm, middle, gain_rows[1], shift_rows[1])
    normed_two_low = normed_two.astype(jnp.bfloat16)
    hidden = jnp.einsum(
        "bxyd,df->bxyf", normed_two_low, full_up, preferred_element_type=jnp.float32
    ) + shift_rows[6:-1].reshape(-1)
    activated, gelu_pullback = jax.vjp(gelu_tanh, hidden)
    activated_low = activated.astype(jnp.bfloat16)
    output = (
        middle
        + jnp.einsum("bxyf,fd->bxyd", activated_low, full_down, preferred_element_type=jnp.float32)
        + shift_rows[-1]
    )
    output_low = output.astype(jnp.bfloat16)
    upstream = cotangent.astype(jnp.float32)
    grad_down = jnp.einsum(
        "bxyf,bxyd->fd", activated_low, cotangent, preferred_element_type=jnp.float32
    )
    grad_shift_down = jnp.sum(upstream, (0, 1, 2))
    grad_activated = jnp.einsum(
        "bxyd,fd->bxyf", cotangent, full_down, preferred_element_type=jnp.float32
    )
    (grad_hidden,) = gelu_pullback(grad_activated)
    grad_hidden_low = grad_hidden.astype(jnp.bfloat16)
    grad_up = jnp.einsum(
        "bxyd,bxyf->df", normed_two_low, grad_hidden_low, preferred_element_type=jnp.float32
    )
    grad_shift_up = jnp.sum(grad_hidden_low.astype(jnp.float32), (0, 1, 2))
    grad_normed_two = jnp.einsum(
        "bxyf,df->bxyd", grad_hidden_low, full_up, preferred_element_type=jnp.float32
    )
    grad_middle_norm, grad_gain_two, grad_shift_two = norm_two_pullback(grad_normed_two)
    grad_middle = upstream + grad_middle_norm
    grad_branch_low = grad_middle.astype(jnp.bfloat16)
    grad_proj = jnp.einsum(
        "bxyd,bxye->de", attended_low, grad_branch_low, preferred_element_type=jnp.float32
    )
    grad_shift_proj = jnp.sum(grad_branch_low.astype(jnp.float32), (0, 1, 2))
    grad_attended = jnp.einsum(
        "bxye,de->bxyd", grad_branch_low, full_proj, preferred_element_type=jnp.float32
    )
    grad_flat = grad_attended.astype(jnp.bfloat16).reshape(
        image_count, query_count, head_count, head_dim
    )
    grad_flat_f = grad_flat.astype(jnp.float32)
    key_value_all = lax.all_gather(key_value, "rows", axis=1, tiled=True)
    scores = key_scores(key_value_all)
    soft = jnp.exp(scores - log_total[..., None])
    keys_all = key_value_all[..., :features].reshape(image_count, key_total, head_count, head_dim)
    values_all = key_value_all[..., features:].reshape(image_count, key_total, head_count, head_dim)
    grad_soft = jnp.einsum(
        "bqhc,bkhc->bhqk", grad_flat, values_all, preferred_element_type=jnp.float32
    )
    row_dot = jnp.sum(soft * grad_soft, -1, keepdims=True)
    grad_scores = (soft * (grad_soft - row_dot)).astype(jnp.bfloat16)
    grad_queries = (
        scale_factor
        * jnp.einsum("bhqk,bkhc->bqhc", grad_scores, keys_all, preferred_element_type=jnp.float32)
        + grad_flat_f
    )
    grad_scores_f = grad_scores.astype(jnp.float32).reshape(
        image_count, head_count, row_count, col_count, key_rows_all, key_cols
    )
    grad_query_rel, grad_rel_h, grad_rel_w = rel_pullback(
        (jnp.sum(grad_scores_f, -1), jnp.sum(grad_scores_f, -2))
    )
    grad_queries = (
        grad_queries.reshape(image_count, row_count, col_count, head_count, head_dim)
        + grad_query_rel
    )
    key_span = key_local * lax.axis_size("rows")
    part_scores = lax.slice_in_dim(grad_scores, 0, key_span, axis=3)
    part_soft = lax.slice_in_dim(soft, 0, key_span, axis=3)
    grad_keys_part = scale_factor * jnp.einsum(
        "bhqk,bqhc->kbhc", part_scores, query_flat, preferred_element_type=jnp.float32
    )
    grad_values_part = jnp.einsum("bhqk,bqhc->kbhc", part_soft, grad_flat_f, precision=highest)
    key_grads = (
        lax.psum_scatter(
            jnp.concatenate(
                [
                    grad_keys_part.reshape(key_span, image_count, features),
                    grad_values_part.reshape(key_span, image_count, features),
                ],
                -1,
            ).astype(jnp.bfloat16),
            "rows",
            scatter_dimension=0,
            tiled=True,
        )
        .astype(jnp.float32)
        .transpose(1, 0, 2)
    )
    grad_keys = key_grads[..., :features].reshape(
        image_count, row_count // 2, key_cols, head_count, head_dim
    )
    grad_values = key_grads[..., features:].reshape(
        image_count, row_count // 2, key_cols, head_count, head_dim
    )
    grad_extended, grad_kernels, grad_pool_gain, grad_pool_shift = pool_pullback(
        (grad_queries, grad_keys, grad_values)
    )
    rims = jnp.concatenate([grad_extended[:, :, :1], grad_extended[:, :, -1:]], 2)
    rims_all = padded(rims.astype(jnp.bfloat16), (("rows", 2),), 1).astype(rims.dtype)
    grad_mixed = grad_extended[:, :, 1:-1]
    grad_mixed = grad_mixed.at[:, :, 0].add(rims_all[:, :, 0]).at[:, :, -1].add(rims_all[:, :, 3])
    grad_mixed_low = grad_mixed.astype(jnp.bfloat16)
    grad_qkv = jnp.einsum(
        "bxyd,mbxye->dme", normed_low, grad_mixed_low, preferred_element_type=jnp.float32
    ).reshape(features, 3 * features)
    grad_shift_qkv = jnp.sum(grad_mixed_low.astype(jnp.float32), (1, 2, 3))
    grad_normed_one = jnp.einsum(
        "mbxye,dme->bxyd", grad_mixed_low, qkv_split, preferred_element_type=jnp.float32
    )
    grad_inputs_norm, grad_gain_one, grad_shift_one = norm_one_pullback(grad_normed_one)
    grad_images = grad_middle + grad_inputs_norm
    grad_gains = jnp.stack([grad_gain_one, grad_gain_two])
    grad_shifts = jnp.concatenate(
        [
            grad_shift_one[None],
            grad_shift_two[None],
            grad_shift_qkv,
            grad_shift_proj[None],
            grad_shift_up.reshape(-1, features),
            grad_shift_down[None],
        ],
        0,
    )
    small_summed = lax.psum(
        (
            grad_gains,
            grad_shifts,
            grad_kernels,
            grad_pool_gain,
            grad_pool_shift,
            grad_rel_h,
            grad_rel_w,
        ),
        ("batch", "rows"),
    )
    matrix_grads = (grad_qkv, grad_proj, grad_up, grad_down)
    summed_rows = (
        lax.psum(matrix_grads[0].astype(jnp.bfloat16), "rows").astype(jnp.float32),
        lax.psum(matrix_grads[1].astype(jnp.bfloat16), "rows").astype(jnp.float32),
        lax.psum(matrix_grads[2].astype(jnp.bfloat16), "rows").astype(jnp.float32),
        lax.psum(matrix_grads[3].astype(jnp.bfloat16), "rows").astype(jnp.float32),
    )
    owned = (
        lax.psum_scatter(
            summed_rows[0].astype(jnp.bfloat16), "batch", scatter_dimension=0, tiled=True
        ).astype(jnp.float32),
        lax.psum_scatter(
            summed_rows[1].astype(jnp.bfloat16), "batch", scatter_dimension=0, tiled=True
        ).astype(jnp.float32),
        lax.psum_scatter(
            summed_rows[2].astype(jnp.bfloat16), "batch", scatter_dimension=0, tiled=True
        ).astype(jnp.float32),
        lax.psum_scatter(
            summed_rows[3].astype(jnp.bfloat16), "batch", scatter_dimension=0, tiled=True
        ).astype(jnp.float32),
    )
    return (
        output_low,
        grad_images,
        owned[0],
        owned[1],
        owned[2],
        owned[3],
        small_summed[0],
        small_summed[1],
        small_summed[2],
        small_summed[3],
        small_summed[4],
        small_summed[5],
        small_summed[6],
    )


LANES = 128
NT = (((1,), (1,)), ((), ()))
TN = (((0,), (0,)), ((), ()))
NN = (((1,), (0,)), ((), ()))
f32 = jnp.float32
bf16 = jnp.bfloat16


def dot(a, b, dims=NN):
    return lax.dot_general(a, b, dims, preferred_element_type=f32)


def lane_ids(shape):
    return lax.broadcasted_iota(jnp.int32, shape, len(shape) - 1)


def head_mask(rows):
    return (lane_ids((rows, LANES)) < HEAD_DIM).astype(f32)


def head_piece(values, start):
    base = start // LANES * LANES
    move = start - base
    if move == 0:
        piece = values[:, base : base + LANES]
    else:
        piece = pltpu.roll(values[:, base : base + 2 * LANES], 2 * LANES - move, 1)[:, :LANES]
    return piece * head_mask(values.shape[0])


def norm_parts(values, count):
    centre = jnp.sum(values, -1, keepdims=True) * (1.0 / count)
    centred = values - centre
    spread = jnp.sum(centred * centred, -1, keepdims=True) * (1.0 / count)
    scale = lax.rsqrt(spread + norm_eps)
    return centred * scale, scale


def head_norm_parts(values, mask):
    centre = jnp.sum(values, -1, keepdims=True) * (1.0 / HEAD_DIM)
    centred = (values - centre) * mask
    spread = jnp.sum(centred * centred, -1, keepdims=True) * (1.0 / HEAD_DIM)
    scale = lax.rsqrt(spread + norm_eps)
    return centred * scale, scale


def norm_back(grad, unit, scale, count):
    first = jnp.sum(grad, -1, keepdims=True) * (1.0 / count)
    second = jnp.sum(grad * unit, -1, keepdims=True) * (1.0 / count)
    return scale * (grad - first - unit * second)


def fold_rows(values):
    rows, lanes = values.shape
    return jnp.sum(values.reshape(rows // 8, 8, lanes), 0)


def fold_block(values):
    rows = values.shape[0]
    tail = values[:, LANES : LANES + 64].astype(f32)
    tail = jnp.concatenate([tail, jnp.zeros_like(tail)], 1)
    side = tail[: rows // 2] + pltpu.roll(tail[rows // 2 :], 64, 1)
    return jnp.concatenate([values[:, :LANES].astype(bf16), side.astype(bf16)], 0)


def unfold_block(folded):
    rows = folded.shape[0] * 2 // 3
    side = folded[rows:].astype(f32)
    tail = jnp.concatenate([side, pltpu.roll(side, 64, 1)], 0).astype(folded.dtype)
    return jnp.concatenate([folded[:rows], tail[:, :64]], 1)


def turned(shift):
    return lax.rem(lax.axis_index("rows") + shift, 4)


def copy_all(pairs, sems):
    copies = []
    for near, far in pairs:
        copies.append(pltpu.make_async_copy(near, far, sems.at[len(copies)]))
        copies[-1].start()
    return copies


def wait_all(copies):
    for copy in copies:
        copy.wait()


def pack_kernel(qkv_ref, proj_ref, up_ref, down_ref, packed_ref, qkv_in, proj_in, up_in, down_in, sems):
    wait_all(
        copy_all(
            [(qkv_ref, qkv_in), (proj_ref, proj_in), (up_ref, up_in), (down_ref, down_in)], sems
        )
    )
    share = qkv_in.shape[0]
    packed_ref[...] = jnp.concatenate(
        [qkv_in[...].astype(f32), proj_in[...].astype(f32), up_in[...].astype(f32)]
        + [
            down_in[...].astype(f32)[share * i : share * (i + 1)]
            for i in range(down_in.shape[0] // share)
        ],
        1,
    ).astype(bf16)


def fold_images_kernel(img_ref, out_ref, img_in, sems):
    loads = copy_all([(img_ref.at[k], img_in.at[k]) for k in range(4)], sems)
    for block in range(4):
        loads[block].wait()
        out_ref[block] = fold_block(img_in[block])


def fold_kernel(cot_ref, cot_0, cot_1, cot_2, cot_3, cot_in, cot_scr, in_sems, sems):
    loads = copy_all([(cot_ref.at[turned(k)], cot_in.at[k]) for k in range(4)], in_sems)
    copies = []
    for shift, far in enumerate((cot_0, cot_1, cot_2, cot_3)):
        loads[shift].wait()
        cot_scr[shift] = fold_block(cot_in[shift])
        copies.append(pltpu.make_async_copy(cot_scr.at[shift], far, sems.at[shift]))
        copies[-1].start()
    wait_all(copies)


def flipped(flip):
    place = lax.axis_index("batch")
    owner = place
    for bit in (1, 2, 4):
        if flip & bit:
            owner = owner + bit - 2 * bit * lax.rem(place // bit, 2)
    return owner


def gather_rows(own_ref, other_ref, first, last, full_scr):
    share = own_ref.shape[1]
    for flip in range(8):
        source = other_ref if flip & 1 else own_ref
        rows = pl.ds(pl.multiple_of(flipped(flip) * share, 8), share)
        full_scr[rows, :] = source[flip // 2, :, first:last].astype(f32)


def load_taps(kernel_ref, kernel_scr):
    kernel_scr[...] = jnp.zeros_like(kernel_scr)
    for tap in range(9):
        kernel_scr[tap, 0:3, 0:HEAD_DIM] = kernel_ref[tap].astype(f32)


def load_gains(gain_ref, shift_ref, gain_scr):
    gain_scr[...] = jnp.zeros_like(gain_scr)
    gain_scr[0:3, 0:HEAD_DIM] = gain_ref[...].astype(f32)
    gain_scr[3:5, 0:HEAD_DIM] = shift_ref[...].astype(f32)


def clear_rim(padded_scr):
    rows, cols, lanes = padded_scr.shape[-3:]
    for place in range(padded_scr.shape[0] if len(padded_scr.shape) == 4 else 1):
        cells = padded_scr.at[place] if len(padded_scr.shape) == 4 else padded_scr
        cells[0:1] = jnp.zeros((1, cols, lanes), f32)
        cells[rows - 1 : rows] = jnp.zeros((1, cols, lanes), f32)
        cells[:, 0:8, :] = jnp.zeros((rows, 8, lanes), f32)
        cells[:, cols - 8 : cols, :] = jnp.zeros((rows, 8, lanes), f32)


CHUNK_ROWS = 16
MIX_ROWS = 32
ATTEND_ROWS = 32
BACK_ROWS = 32
WEIGH_TILE = 1024
IMAGE_TILE = 1024
LOG2_E = 1.4426950408889634


def stride_windows(padded, place, side, key_rows, key_cols):
    columns = pl.ds(7 + side, key_cols, stride=2)
    even = padded[place, pl.ds(0, key_rows + 1, stride=2), columns, :]
    odd = padded[place, pl.ds(1, key_rows, stride=2), columns, :]
    return even[:key_rows], odd, even[1:]


def attend_kernel(
    stage, weight_scr, bias_ref, rows_ref, kern_scr, gain_scr, table_ref,
    img_ref, padded, qraw_out, kvraw_out, soft_out, att_out, key_out, val_out,
    query_scr, keyaug_scr,
):
    cols = padded.shape[2] - 16
    rows = padded.shape[1] - 2
    tile = CHUNK_ROWS * cols
    chunks = rows // CHUNK_ROWS
    key_cols = cols // 2
    key_rows = rows // 2
    key_total = key_rows * key_cols
    features = img_ref.shape[1]
    clear_rim(padded)
    gain_one = rows_ref[16:17, 0:features]
    shift_one = rows_ref[0:1, 0:features]
    table = table_ref[...]

    mix_tile = MIX_ROWS * cols

    img_ref[...] = jnp.concatenate(
        [unfold_block(stage[place]) for place in range(4)], 0
    )

    def mix(step, carry):
        span = pl.ds(pl.multiple_of(step * mix_tile, mix_tile), mix_tile)
        unit, _ = norm_parts(img_ref[span, :].astype(f32), features)
        normed = (unit * gain_one + shift_one).astype(bf16)
        mixed = dot(normed, weight_scr[...]) + bias_ref[0:1, :]
        for place in range(3 * HEADS):
            low = mixed[:, place * LANES : (place + 1) * LANES].astype(bf16)
            padded[place, pl.ds(1 + step * MIX_ROWS, MIX_ROWS), 8 : 8 + cols, :] = low.astype(
                f32
            ).reshape(MIX_ROWS, cols, LANES)
        return carry

    lax.fori_loop(0, rows // MIX_ROWS, mix, 0, unroll=True)

    tile_mask = head_mask(tile)

    def pool_queries(step, carry):
        span = pl.ds(pl.multiple_of(step * tile, tile), tile)
        for head in range(HEADS):
            total = jnp.zeros((CHUNK_ROWS, cols, LANES), f32)
            for side in range(3):
                window = padded[
                    head, pl.ds(step * CHUNK_ROWS, CHUNK_ROWS + 2), 7 + side : 7 + side + cols, :
                ]
                for up in range(3):
                    total = total + window[up : up + CHUNK_ROWS] * kern_scr[3 * up + side, 0:1, :]
            raw = total.reshape(tile, LANES)
            qraw_out[head, span, :] = raw
            unit, _ = head_norm_parts(raw, tile_mask)
            query_scr[head, span, :] = (unit * gain_scr[0:1, :] + gain_scr[3:4, :]).astype(bf16)
        return carry

    lax.fori_loop(0, chunks, pool_queries, 0, unroll=True)

    for place in range(2 * HEADS):
        member = 1 + place // HEADS
        total = jnp.zeros((key_rows, key_cols, LANES), f32)
        for side in range(3):
            for up, window in enumerate(stride_windows(padded, HEADS + place, side, key_rows, key_cols)):
                total = total + window * kern_scr[3 * up + side, member : member + 1, :]
        kvraw_out[place] = total.reshape(key_total, LANES)

    key_mask = head_mask(key_total)
    key_place = lax.broadcasted_iota(jnp.int32, (key_total, LANES), 0)
    lanes = lane_ids((key_total, LANES))
    from_row = 30 - 2 * (key_place // key_cols)
    from_col = 96 + 2 * (key_place % key_cols)
    hot = (
        (lanes == from_row)
        | (lanes == from_row + 64)
        | (lanes == from_col)
        | (lanes == from_col - 64)
    ).astype(bf16)
    for head in range(HEADS):
        unit, _ = head_norm_parts(kvraw_out[head], key_mask)
        low = (unit * gain_scr[1:2, :]).astype(bf16)
        key_out[head] = low
        keyaug_scr[head, :, 0:LANES] = low
        keyaug_scr[head, :, LANES : 2 * LANES] = hot
        unit, _ = head_norm_parts(kvraw_out[HEADS + head], key_mask)
        val_out[head] = (unit * gain_scr[2:3, :] + gain_scr[4:5, :]).astype(bf16)

    scale_factor = HEAD_DIM ** (-0.5)
    row_lanes = lane_ids((cols, LANES))
    part_tile = ATTEND_ROWS * cols
    part_lanes = lane_ids((part_tile, LANES))

    def attend(step, carry):
        span = pl.ds(pl.multiple_of(step * part_tile, part_tile), part_tile)
        for head in range(HEADS):
            query = query_scr[head, span, :]
            looked = dot(query, table, NT) * (1.0 / scale_factor)
            pieces = []
            for row in range(ATTEND_ROWS):
                part = looked[row * cols : (row + 1) * cols, :]
                place = step * ATTEND_ROWS + row
                by_row = pltpu.roll(part, LANES - place, 1)
                by_col = pltpu.roll(part, 0, 1, stride=1, stride_axis=0)
                pieces.append(jnp.where(row_lanes < 64, by_row, by_col))
            terms = jnp.concatenate(pieces, 0)
            high = terms.astype(bf16).astype(f32)
            rest = pltpu.roll(terms - high, 64, 1)
            both = jnp.where((part_lanes < 32) | (part_lanes >= 96), high, rest).astype(bf16)
            scores = dot(jnp.concatenate([query, both], 1), keyaug_scr[head], NT)
            top = jnp.max(scores, -1, keepdims=True)
            powers = jnp.exp2((scores - top) * (scale_factor * LOG2_E))
            soft = (powers * (1.0 / jnp.sum(powers, -1, keepdims=True))).astype(bf16)
            soft_out[head, span, :] = soft
            att = dot(soft, val_out[head]) + query.astype(f32)
            att_out[span, head * LANES : (head + 1) * LANES] = att.astype(bf16)
        return carry

    lax.fori_loop(0, rows // ATTEND_ROWS, attend, 0, unroll=True)


def stack_blocks(values, block_scr):
    owners = block_scr.shape[0]
    share = values.shape[0] // owners
    for block in range(values.shape[1] // LANES):
        for owner in range(owners):
            block_scr[owner, share * block : share * (block + 1), :] = values[
                share * owner : share * (owner + 1), block * LANES : (block + 1) * LANES
            ]


def split_owners(block_scr, mine_ref, theirs_ref, order):
    count = block_scr.shape[1]
    for place, flip in enumerate(order):
        span = pl.ds(place * count, count)
        mine_ref[span, :] = block_scr[flipped(flip)].astype(bf16)
        theirs_ref[span, :] = block_scr[flipped(flip + 1)].astype(bf16)


def weights_kernel(
    owners, own_ref, other_ref, gains_far, shifts_far, kern_far, pgain_far, pshift_far, relh_far, relw_far,
    wide_ref, proj_ref, up_ref, down_ref, bias_ref, rows_ref, columns_ref, taps_ref, pool_ref, ahead_ref, behind_ref,
    full_scr, down_scr, gains_in, shifts_in, kern_in, pgain_in, pshift_in, relh_in, relw_in, table_scr, sems,
):
    loads = copy_all(
        [
            (gains_far, gains_in), (shifts_far, shifts_in), (kern_far, kern_in), (pgain_far, pgain_in),
            (pshift_far, pshift_in), (relh_far, relh_in), (relw_far, relw_in),
        ],
        sems,
    )
    gather_rows(own_ref, other_ref, 0, own_ref.shape[2], full_scr)
    for place in range(3 * HEADS):
        wide_ref[:, place * LANES : (place + 1) * LANES] = head_piece(
            full_scr[:, 0 : 5 * LANES], place * HEAD_DIM
        ).astype(bf16)
    features, hidden_count = up_ref.shape
    proj = pltpu.roll(full_scr[:, 4 * LANES : 6 * LANES], 192, 1)[:, 0:features]
    gap = jnp.zeros((LANES - HEAD_DIM, features), f32)
    proj_ref[...] = jnp.concatenate(
        [proj[0:HEAD_DIM, :], gap, proj[HEAD_DIM : 2 * HEAD_DIM, :], gap], 0
    ).astype(bf16)
    up_ref[...] = full_scr[:, 4 * features : 4 * features + hidden_count].astype(bf16)
    columns = full_scr[:, 4 * features + hidden_count :]
    share = features // owners
    pieces = hidden_count // features
    for piece in range(pieces):
        start = piece * features
        base = start // LANES * LANES
        window = columns[:, base : base + 2 * LANES]
        if start != base:
            window = pltpu.roll(window, 2 * LANES - (start - base), 1)
        for owner in range(owners):
            place = owner * share * pieces + piece * share
            down_scr[place : place + share, :] = window[
                owner * share : (owner + 1) * share, 0:features
            ]
    down_ref[...] = down_scr[...].astype(bf16)
    wait_all(loads)
    rows_ref[...] = jnp.zeros_like(rows_ref)
    rows_ref[0 : shifts_in.shape[0], 0:features] = shifts_in[...].astype(f32)
    rows_ref[16:18, 0:features] = gains_in[...].astype(f32)
    columns_ref[...] = jnp.concatenate(
        [rows_ref[...], jnp.zeros((LANES - rows_ref.shape[0], 2 * LANES), f32)], 0
    ).T
    bias_ref[...] = jnp.zeros_like(bias_ref)
    for section in range(3):
        for head in range(HEADS):
            place = (section * HEADS + head) * LANES
            bias_ref[0:1, place : place + LANES] = head_piece(
                rows_ref[2 + section : 3 + section, :], head * HEAD_DIM
            )
    for piece in range(pieces):
        bias_ref[1:2, piece * features : (piece + 1) * features] = rows_ref[
            6 + piece : 7 + piece, 0:features
        ]
    load_taps(kern_in, taps_ref)
    load_gains(pgain_in, pshift_in, pool_ref)
    count = relw_in.shape[0]
    table_scr[...] = jnp.zeros_like(table_scr)
    table_scr[0:count, 0:HEAD_DIM] = relh_in[...].astype(f32)
    table_scr[64 : 64 + count, 0:HEAD_DIM] = relw_in[...].astype(f32)
    behind_ref[...] = table_scr[...].astype(bf16)
    flip = (
        lax.broadcasted_iota(jnp.int32, (64, count), 0) + lax.broadcasted_iota(jnp.int32, (64, count), 1)
        == count - 1
    ).astype(bf16)
    table_scr[64:128, 0:HEAD_DIM] = dot(flip, relw_in[...])
    ahead_ref[...] = table_scr[...].astype(bf16)


def send_turned(near, fars, sems):
    sends = []
    for shift, far in enumerate(fars):
        sends.append(pltpu.make_async_copy(near.at[turned(shift)], far, sems.at[shift]))
        sends[-1].start()
    return sends


GELU_A = 0.7978845608028654
GELU_B = 0.044715


def feed_ahead_kernel(
    img_ref, att_ref, proj_ref, up_ref, down_ref, bias_ref, rows_ref,
    out_0, out_1, out_2, out_3, normed_ref, unit_ref, scale_ref, active_ref, slope_ref,
    out_stage, turn_sems,
):
    tokens, features = img_ref.shape
    pieces = up_ref.shape[1] // features
    block = tokens // 4
    middle = img_ref[...].astype(f32) + (dot(att_ref[...], proj_ref[...]) + rows_ref[5:6, 0:features])
    unit, scale = norm_parts(middle, features)
    normed = (unit * rows_ref[17:18, 0:features] + rows_ref[1:2, 0:features]).astype(bf16)
    unit_ref[...] = unit
    scale_ref[...] = jnp.broadcast_to(scale, scale_ref.shape)
    normed_ref[...] = normed
    hidden = dot(normed, up_ref[...]) + bias_ref[1:2, :]
    square = hidden * hidden
    wave = jnp.tanh(hidden * (GELU_A + (GELU_A * GELU_B) * square))
    half = 0.5 + 0.5 * wave
    active = (hidden * half).astype(bf16)
    active_ref[...] = active
    slope_ref[...] = half * (
        1.0 + (1.0 - half) * (hidden * (2.0 * GELU_A + (6.0 * GELU_A * GELU_B) * square))
    )
    out = middle + dot(active, down_ref[...]) + rows_ref[6 + pieces : 7 + pieces, 0:features]
    for place in range(4):
        out_stage[place] = fold_block(out[place * block : (place + 1) * block, :])
    wait_all(send_turned(out_stage, (out_0, out_1, out_2, out_3), turn_sems))


def feed_back_kernel(
    owners,
    att_ref, cot_0, cot_1, cot_2, cot_3, normed_ref, unit_ref, scale_ref, active_ref, slope_ref,
    proj_ref, up_ref, down_ref, rows_ref,
    mid_ref, gatt_ref, mine_ref, theirs_ref,
    gdown, gup, gproj, gbias, gsmall, block_scr, cot_stage, cot_sems,
):
    cot_loads = copy_all(
        [(piece, cot_stage.at[turned(4 - k)]) for k, piece in enumerate((cot_0, cot_1, cot_2, cot_3))],
        cot_sems,
    )
    tokens, features = unit_ref.shape
    hidden_count = up_ref.shape[1]
    pieces = hidden_count // features
    unit = unit_ref[...]
    att = att_ref[...]
    wait_all(cot_loads)
    cot_low = jnp.concatenate([unfold_block(cot_stage[place]) for place in range(4)], 0)
    cot = cot_low.astype(f32)
    gdown[...] = dot(cot_low, active_ref[...], TN)
    gact = dot(cot_low, down_ref[...], NT)
    ghid = (gact * slope_ref[...]).astype(bf16)
    gup[...] = dot(normed_ref[...], ghid, TN)
    gbias[...] = fold_rows(ghid.astype(f32))
    gnorm = dot(ghid, up_ref[...], NT)
    gsmall[0:8, :] = fold_rows(gnorm * unit)
    gsmall[8:16, :] = fold_rows(gnorm)
    gmid = cot + norm_back(gnorm * rows_ref[17:18, 0:features], unit, scale_ref[:, 0:1], features)
    gbranch = gmid.astype(bf16)
    mid_ref[...] = gbranch
    gsmall[16:24, :] = fold_rows(gbranch.astype(f32))
    gsmall[24:32, :] = fold_rows(cot)
    gproj[...] = dot(att, gbranch, TN)
    gatt_ref[...] = dot(gbranch, proj_ref[...], NT).astype(bf16)

    share = features // owners
    proj = jnp.concatenate(
        [gproj[head * LANES : head * LANES + HEAD_DIM, :] for head in range(HEADS)], 0
    )
    down = gdown[...].T
    down_pieces = []
    for piece in range(pieces):
        down_pieces.append(
            jnp.concatenate(
                [
                    down[
                        owner * share * pieces + piece * share : owner * share * pieces
                        + (piece + 1) * share,
                        :,
                    ]
                    for owner in range(owners)
                ],
                0,
            )
        )
    sums = [jnp.sum(gsmall[8 * i : 8 * i + 8, :], 0, keepdims=True) for i in range(4)]
    bias_row = jnp.sum(gbias[...], 0, keepdims=True)
    block = jnp.concatenate(
        sums + [bias_row[:, i * features : (i + 1) * features] for i in range(pieces)], 0
    )
    block = jnp.concatenate([block, jnp.zeros((share - 8, features), f32)], 0)
    small = jnp.concatenate([block] * owners, 0)
    block_scr[...] = jnp.zeros_like(block_scr)
    stack_blocks(jnp.concatenate([proj, gup[...]] + down_pieces + [small], 1), block_scr)
    split_owners(block_scr, mine_ref, theirs_ref, (0, 4, 2, 6))


SMALL_ROWS = 168
DENSE_ROWS = 128
LATE_ROWS = 128


def back_attend_kernel(
    head, qraw_ref, kvraw_ref, soft_ref, gatt_ref, key_ref, val_ref,
    gain_scr, table_ref,
    gpadded, gkeypad, sums_ref,
    keyaug_scr, gtable, gkey, gval, gsums,
):
    cols = gpadded.shape[1] - 16
    rows = gpadded.shape[0] - 2
    tile = BACK_ROWS * cols
    chunks = rows // BACK_ROWS
    key_cols = cols // 2
    key_rows = rows // 2
    key_total = kvraw_ref.shape[1]
    clear_rim(gpadded)
    gkeypad[...] = jnp.zeros_like(gkeypad)
    table = table_ref[...]
    gsums[...] = jnp.zeros_like(gsums)

    key_place = lax.broadcasted_iota(jnp.int32, (key_total, LANES), 0)
    lanes = lane_ids((key_total, LANES))
    hot = (
        (lanes == 30 - 2 * (key_place // key_cols)) | (lanes == 94 - 2 * (key_place % key_cols))
    ).astype(bf16)
    keyaug_scr[:, 0:LANES] = key_ref[head]
    keyaug_scr[:, LANES : 2 * LANES] = hot

    scale_factor = HEAD_DIM ** (-0.5)
    tile_mask = head_mask(tile)
    row_lanes = lane_ids((cols, LANES))

    def attend(step, carry):
        span = pl.ds(pl.multiple_of(step * tile, tile), tile)
        unit, scale = head_norm_parts(qraw_ref[head, span, :], tile_mask)
        query = (unit * gain_scr[0:1, :] + gain_scr[3:4, :]).astype(bf16)
        gatt = gatt_ref[span, head * LANES : (head + 1) * LANES]
        soft_low = soft_ref[head, span, :]
        soft = soft_low.astype(f32)
        gsoft = dot(gatt, val_ref[head], NT)
        inner = jnp.sum(soft * gsoft, -1, keepdims=True)
        gscore = (soft * (gsoft - inner)).astype(bf16)
        gkey[...] = dot(query, gscore, TN)
        gval[...] = dot(gatt, soft_low, TN)
        wide = dot(gscore, keyaug_scr[...])
        gterm = wide[:, LANES : 2 * LANES]
        pieces = []
        for row in range(BACK_ROWS):
            part = gterm[row * cols : (row + 1) * cols, :]
            place = step * BACK_ROWS + row
            by_row = pltpu.roll(part, place, 1)
            by_col = pltpu.roll(part, 0, 1, stride=1, stride_axis=0)
            pieces.append(jnp.where(row_lanes < 64, by_row, by_col))
        glook = jnp.concatenate(pieces, 0).astype(bf16)
        gtable[...] = dot(glook, query, TN)
        gquery = scale_factor * wide[:, 0:LANES] + gatt.astype(f32) + dot(glook, table)
        gsums[0:8, :] = fold_rows(gquery * unit)
        gsums[8:16, :] = fold_rows(gquery)
        graw = norm_back(gquery * gain_scr[0:1, :], unit, scale, HEAD_DIM) * tile_mask
        gpadded[pl.ds(1 + step * BACK_ROWS, BACK_ROWS), 8 : 8 + cols, :] = graw.reshape(
            BACK_ROWS, cols, LANES
        )
        return carry

    lax.fori_loop(0, chunks, attend, 0, unroll=True)

    key_mask = head_mask(key_total)
    for member, grad in ((1, gkey[...].T * scale_factor), (2, gval[...].T)):
        unit, scale = head_norm_parts(kvraw_ref[(member - 1) * HEADS + head], key_mask)
        base = 16 if member == 1 else 24
        gsums[base : base + 8, :] += fold_rows(grad * unit)
        if member == 2:
            gsums[32:40, :] += fold_rows(grad)
        graw = norm_back(grad * gain_scr[member : member + 1, :], unit, scale, HEAD_DIM) * key_mask
        gkeypad[member - 1, 0:key_rows, 0:key_cols, :] = graw.reshape(key_rows, key_cols, LANES)

    sums_ref[...] = jnp.zeros_like(sums_ref)
    sums_ref[0:63, :] = gtable[0:63, :]
    sums_ref[63:126, :] = gtable[64:127, :]
    for place, base in enumerate((0, 16, 24, 8, 32)):
        sums_ref[126 + place : 127 + place, :] = jnp.sum(gsums[base : base + 8, :], 0, keepdims=True)


def back_weights_kernel(
    img_ref, padded, gpadded_0, gpadded_1, gkeypad_0, gkeypad_1, sums_0, sums_1, weight_ref, columns_ref, kern_scr,
    gmix_scr, mine_ref, theirs_ref,
    gmixrow, gkern, gweight, gbias, small_scr, dense_scr, block_scr,
):
    tokens, features = img_ref.shape
    cols = padded.shape[2] - 16
    rows = padded.shape[1] - 2
    tile = CHUNK_ROWS * cols
    chunks = rows // CHUNK_ROWS
    key_cols = cols // 2
    key_rows = rows // 2
    gkern[...] = jnp.zeros_like(gkern)

    def spread_queries(step, carry):
        span = pl.ds(pl.multiple_of(step * tile, tile), tile)
        around = pl.ds(step * CHUNK_ROWS, CHUNK_ROWS + 2)
        for head, gpadded in enumerate((gpadded_0, gpadded_1)):
            total = jnp.zeros((CHUNK_ROWS, cols, LANES), f32)
            own = gpadded[pl.ds(1 + step * CHUNK_ROWS, CHUNK_ROWS), 8 : 8 + cols, :]
            for side in range(3):
                window = gpadded[around, 9 - side : 9 - side + cols, :]
                cells = padded[head, around, 7 + side : 7 + side + cols, :]
                for up in range(3):
                    tap = 3 * up + side
                    total = total + window[2 - up : 2 - up + CHUNK_ROWS] * kern_scr[tap, 0:1, :]
                    gkern[tap] += fold_rows((own * cells[up : up + CHUNK_ROWS]).reshape(tile, LANES))
            flat = total.reshape(tile, LANES).astype(bf16)
            gmix_scr[span, head * LANES : (head + 1) * LANES] = flat
        return carry

    lax.fori_loop(0, chunks, spread_queries, 0, unroll=True)

    evens = pl.ds(0, key_cols, stride=2)
    odds = pl.ds(1, key_cols, stride=2)
    for place in range(2 * HEADS):
        member = 1 + place // HEADS
        taps = [kern_scr[tap, member : member + 1, :] for tap in range(9)]
        gkeypad = (gkeypad_0, gkeypad_1)[place % HEADS].at[place // HEADS]
        left = gkeypad[0 : key_rows + 1, 0:key_cols, :]
        right = gkeypad[0 : key_rows + 1, 1 : 1 + key_cols, :]
        here, below, beside, cross = left[:key_rows], left[1:], right[:key_rows], right[1:]
        gmixrow[:, 0, evens, :] = here * taps[4]
        gmixrow[:, 0, odds, :] = beside * taps[3] + here * taps[5]
        gmixrow[:, 1, evens, :] = below * taps[1] + here * taps[7]
        gmixrow[:, 1, odds, :] = (
            cross * taps[0] + below * taps[2] + beside * taps[6] + here * taps[8]
        )
        lane = (HEADS + place) * LANES
        gmix_scr[:, lane : lane + LANES] = gmixrow[...].reshape(rows * cols, LANES).astype(bf16)
        for side in range(3):
            for up, cells in enumerate(stride_windows(padded, HEADS + place, side, key_rows, key_cols)):
                gkern[9 * member + 3 * up + side] += fold_rows(
                    (here * cells).reshape(key_rows * key_cols, LANES)
                )

    def weigh(step, carry):
        span = pl.ds(pl.multiple_of(step * WEIGH_TILE, WEIGH_TILE), WEIGH_TILE)
        unit, _ = norm_parts(img_ref[span, :].astype(f32), features)
        gmix = gmix_scr[span, :]
        gweight[...] = dot(unit.astype(bf16), gmix, TN)
        gbias[...] = fold_rows(gmix.astype(f32))
        return carry

    lax.fori_loop(0, tokens // WEIGH_TILE, weigh, 0, unroll=True)

    bias_row = jnp.sum(gbias[...], 0, keepdims=True)
    weight = weight_ref[...].astype(f32)
    raw = gweight[...]
    lanes = lane_ids((features, LANES))
    norm_sums = jnp.where(
        lanes == 0,
        jnp.sum(weight * raw, 1, keepdims=True),
        jnp.where(lanes == 1, jnp.sum(weight * bias_row, 1, keepdims=True), 0.0),
    )
    norm_rows = jnp.concatenate([norm_sums, jnp.zeros((2 * LANES - features, LANES), f32)], 0).T
    gweight[...] = raw * columns_ref[0:features, 16:17] + columns_ref[0:features, 0:1] * bias_row

    for tap in range(27):
        row = 3 * (tap % 9) + tap // 9
        small_scr[row : row + 1, :] = jnp.sum(gkern[tap], 0, keepdims=True)
    small_scr[27:158, :] = sums_0[0:131, :] + sums_1[0:131, :]
    for place in range(3 * HEADS):
        small_scr[158 + place : 159 + place, :] = bias_row[:, place * LANES : (place + 1) * LANES]
    for place in range(2):
        for head in range(HEADS):
            at = 164 + HEADS * place + head
            small_scr[at : at + 1, :] = head_piece(norm_rows[place : place + 1, :], head * HEAD_DIM)
    weights = jnp.concatenate(
        [gweight[:, place * LANES : place * LANES + HEAD_DIM] for place in range(3 * HEADS)]
        + [jnp.zeros((features, 64), f32)],
        1,
    )
    block_scr[...] = jnp.zeros_like(block_scr)
    stack_blocks(weights, block_scr)
    split_owners(block_scr, mine_ref, theirs_ref, (0, 2, 4, 6))
    count = block_scr.shape[1]
    dense_scr[...] = jnp.zeros_like(dense_scr)
    dense_scr[0:126, :] = small_scr[0:126, :] * head_mask(126)
    beside = lane_ids((42, LANES)) >= HEAD_DIM
    for piece in range(3):
        moved = small_scr[126:168, :]
        moved = pltpu.roll(moved, HEAD_DIM - 32 * piece, 1)
        dense_scr[42 * piece : 42 * (piece + 1), :] += jnp.where(beside, moved, 0.0)
    small = dense_scr[...].astype(bf16)
    mine_ref[4 * count :, :] = small
    theirs_ref[4 * count :, :] = small


def back_images_kernel(img_ref, gmix_ref, gmid_ref, weight_ref, rows_ref, gimg_ref):
    tokens, features = img_ref.shape
    tile = IMAGE_TILE
    block = tokens // 4
    gain_one = rows_ref[16:17, 0:features]

    def finish(step, carry):
        span = pl.ds(pl.multiple_of(step * tile, tile), tile)
        unit, scale = norm_parts(img_ref[span, :].astype(f32), features)
        gnorm = dot(gmix_ref[span, :], weight_ref[...], NT)
        gimg = gmid_ref[span, :].astype(f32) + norm_back(gnorm * gain_one, unit, scale, features)
        for place in range(tile // block):
            gimg_ref[step * (tile // block) + place] = fold_block(
                gimg[place * block : (place + 1) * block, :]
            )
        return carry

    lax.fori_loop(0, tokens // tile, finish, 0, unroll=True)


def halve_kernel(mine_ref, got_ref, keep_ref, send_ref):
    half = keep_ref.shape[0]
    total = (mine_ref[...].astype(f32) + got_ref[...].astype(f32)).astype(bf16)
    keep_ref[...] = total[:half]
    send_ref[...] = total[half:]


def pair_kernel(shared, mine_ref, got_ref, own_ref, msg_1, msg_2, msg_3):
    total = (mine_ref[...].astype(f32) + got_ref[...].astype(f32)).astype(bf16)
    count = (total.shape[0] - shared) // 4
    for place, out in enumerate((own_ref, msg_1, msg_2, msg_3)):
        out[0:count, :] = total[place * count : (place + 1) * count]
        if shared:
            out[count:, :] = total[4 * count :]


def chips_sum(own_ref, got_1, got_2, got_3):
    return (own_ref[...].astype(f32) + got_1[...].astype(f32)) + (
        got_2[...].astype(f32) + got_3[...].astype(f32)
    )


def two_kernel(own_ref, got_ref, out_ref):
    out_ref[...] = (own_ref[...].astype(f32) + got_ref[...].astype(f32)).astype(bf16)


def four_kernel(own_ref, got_1, got_2, got_3, out_ref):
    out_ref[...] = chips_sum(own_ref, got_1, got_2, got_3).astype(bf16)


def pictures_kernel(out_0, out_1, out_2, out_3, gimg_low, out_ref, gimg_ref):
    for shift in range(4):
        gimg_ref[shift] = unfold_block(gimg_low[shift]).astype(f32)
        block = (out_0, out_1, out_2, out_3)[shift][...]
        out_ref[turned(4 - shift)] = unfold_block(block)


def finish_kernel(
    early_0, early_1, late_0, late_1,
    gqkv_ref, gproj_ref, gup_ref, gdown_ref, ggain_ref, gshift_ref, gkern_ref,
    gpgain_ref, gpshift_ref, grelh_ref, grelw_ref,
    small_scr, dense_scr,
):
    share, features = gproj_ref.shape
    hidden = gup_ref.shape[1]
    pieces = hidden // features
    early = early_0[...].astype(f32) + early_1[...].astype(f32)
    early = jnp.concatenate(
        [early[share * i : share * (i + 1), :] for i in range((2 * features + 2 * hidden) // LANES)], 1
    )
    gproj_ref[...] = early[:, 0:features]
    gup_ref[...] = early[:, features : features + hidden]
    for piece in range(pieces):
        start = features + hidden + piece * features
        gdown_ref[piece * share : (piece + 1) * share, :] = early[:, start : start + features]
    start = features + 2 * hidden
    block = early[0:8, start : start + features]
    late = late_0[...].astype(f32) + late_1[...].astype(f32)
    gqkv_ref[...] = jnp.concatenate([late[share * i : share * (i + 1), :] for i in range(5)], 1)[
        :, 0 : 3 * features
    ]
    dense = late[LATE_ROWS : LATE_ROWS + DENSE_ROWS, :]
    small_scr[0:126, :] = dense[0:126, :]
    dense_scr[...] = dense
    lanes = lane_ids((42, LANES))
    rest = jnp.zeros((42, LANES), f32)
    for piece in range(3):
        moved = pltpu.roll(dense_scr[42 * piece : 42 * (piece + 1), :], 32 + 32 * piece, 1)
        rest = jnp.where((lanes >= 32 * piece) & (lanes < 32 * piece + 32), moved, rest)
    small_scr[126:168, :] = rest
    for tap in range(9):
        gkern_ref[tap] = small_scr[3 * tap : 3 * tap + 3, 0:HEAD_DIM]
    gpgain_ref[...] = small_scr[153:156, 0:HEAD_DIM]
    gpshift_ref[...] = small_scr[156:158, 0:HEAD_DIM]
    grelh_ref[...] = small_scr[27:90, 0:HEAD_DIM]
    grelw_ref[...] = small_scr[90:153, 0:HEAD_DIM]
    ggain_ref[1:2, :] = block[0:1, :]
    gshift_ref[1:2, :] = block[1:2, :]
    for head in range(HEADS):
        lanes = slice(head * HEAD_DIM, (head + 1) * HEAD_DIM)
        ggain_ref[0:1, lanes] = small_scr[164 + head : 165 + head, 0:HEAD_DIM]
        gshift_ref[0:1, lanes] = small_scr[166 + head : 167 + head, 0:HEAD_DIM]
        for section in range(3):
            row = 158 + section * HEADS + head
            gshift_ref[2 + section : 3 + section, lanes] = small_scr[row : row + 1, 0:HEAD_DIM]
    gshift_ref[5:6, :] = block[2:3, :]
    gshift_ref[6 : 6 + pieces, :] = block[4 : 4 + pieces, :]
    gshift_ref[6 + pieces : 7 + pieces, :] = block[3:4, :]


LONG = {"back_attend_1": 2 * 10**10}


def call(kernel, name, outs, scratch, flops, limit, spaces, out_spaces, *args):
    place = {"v": pltpu.VMEM, "p": pltpu.VMEM, "h": pltpu.HBM, "a": pl.ANY}
    keep = {"p": pltpu.VMEM, "h": pltpu.HBM}
    args = [
        pltpu.with_memory_space_constraint(a, keep[c]) if c in keep else a for c, a in zip(spaces, args)
    ]
    outs = [keep[c](o.shape, o.dtype) if c in keep else o for c, o in zip(out_spaces, outs)]
    return pl.pallas_call(
        kernel,
        name=name,
        out_shape=outs,
        in_specs=[pl.BlockSpec(memory_space=place[c]) for c in spaces],
        out_specs=[pl.BlockSpec(memory_space=place[c]) for c in out_spaces],
        scratch_shapes=scratch,
        cost_estimate=pl.CostEstimate(flops=LONG.get(name, 1), bytes_accessed=LONG.get(name, 1) // 500, transcendentals=0),
        compiler_params=pltpu.CompilerParams(vmem_limit_bytes=limit * 2**20),
    )(*args)


KA_LIMIT = 36


def whole_image(
    images,
    w_qkv,
    w_proj,
    w_up,
    w_down,
    gains_main,
    shifts_main,
    pool_kernels,
    pool_gains,
    pool_shifts,
    rel_height,
    rel_width,
    cotangent,
):
    owners = lax.axis_size("batch")
    cycle = lax.axis_size("rows")
    image_count, row_count, cols, features = images.shape
    rows = row_count * cycle
    tokens = rows * cols
    hidden = w_up.shape[1]
    share = w_proj.shape[0]
    pieces = hidden // features
    key_total = tokens // 4
    early_used = (2 * features + 2 * hidden) // LANES * share
    early_rows = -(-early_used // 16) * 16
    def shaped(shape, dtype):
        return jax.ShapeDtypeStruct(shape, dtype)

    block = tokens // cycle
    folded = (block * features // LANES, LANES)
    width = 4 * features + 2 * hidden

    def send_on(pieces):
        return list(pieces[:1]) + [
            lax.ppermute(pieces[k], "rows", [(i, (i + k) % cycle) for i in range(cycle)])
            for k in range(1, cycle)
        ]

    def trade(cells, flip):
        return lax.ppermute(cells, "batch", [(i, i ^ flip) for i in range(owners)])

    img = call(
        fold_images_kernel,
        "fold_images",
        [shaped((cycle,) + folded, bf16)],
        [pltpu.VMEM((cycle, block, features), bf16), pltpu.SemaphoreType.DMA((4,))],
        1,
        4,
        "h",
        "v",
        images.reshape(cycle, block, features),
    )[0]
    img, w_qkv = lax.optimization_barrier((img, w_qkv))
    img = lax.all_to_all(img, "rows", 0, 0, tiled=True)
    packed = call(
        pack_kernel,
        "pack",
        [shaped((share, width), bf16)],
        [pltpu.VMEM(w.shape, bf16) for w in (w_qkv, w_proj, w_up, w_down)]
        + [pltpu.SemaphoreType.DMA((4,))],
        10**6,
        4,
        "hhhh",
        "v",
        w_qkv, w_proj, w_up, w_down,
    )[0]
    packed, cotangent = lax.optimization_barrier((packed, cotangent))
    cot_pieces = call(
        fold_kernel,
        "fold",
        [shaped(folded, bf16)] * cycle,
        [
            pltpu.VMEM((cycle, block, features), bf16),
            pltpu.VMEM((cycle,) + folded, bf16),
            pltpu.SemaphoreType.DMA((4,)),
            pltpu.SemaphoreType.DMA((4,)),
        ],
        10**6,
        8,
        "h",
        "a" * 4,
        cotangent.reshape(cycle, block, features),
    )
    img, cot_pieces, *shards = lax.optimization_barrier(
        (img, cot_pieces, *[trade(packed, flip) for flip in (2, 4, 6)])
    )
    own = jnp.stack([packed, *shards])
    other = trade(own, 1)
    taps = pool_kernels.transpose(1, 0, 2)
    small = (gains_main, shifts_main, taps, pool_gains, pool_shifts, rel_height, rel_width)
    wide, full_proj, full_up, full_down, biases, lines, columns, taps_wide, pool_lines, ahead, behind = call(
        functools.partial(weights_kernel, owners),
        "weights",
        [
            shaped((features, 3 * HEADS * LANES), bf16),
            shaped((HEADS * LANES, features), bf16),
            shaped((features, hidden), bf16),
            shaped((hidden, features), bf16),
            shaped((8, hidden), f32),
            shaped((24, 2 * LANES), f32),
            shaped((2 * LANES, LANES), f32),
            shaped((9, 8, LANES), f32),
            shaped((8, LANES), f32),
            shaped((LANES, LANES), bf16),
            shaped((LANES, LANES), bf16),
        ],
        [pltpu.VMEM((features, width), f32), pltpu.VMEM((hidden, features), f32)]
        + [pltpu.VMEM(a.shape, bf16) for a in small]
        + [pltpu.VMEM((LANES, LANES), f32), pltpu.SemaphoreType.DMA((7,))],
        10**6,
        12,
        "vv" + "h" * 7,
        "v" * 11,
        own, other, *small,
    )
    cot_pieces = send_on(cot_pieces)
    whole = [
        shaped((3 * HEADS, rows + 2, cols + 16, LANES), f32),
        shaped((HEADS, tokens, LANES), f32),
        shaped((2 * HEADS, key_total, LANES), f32),
        shaped((HEADS, tokens, key_total), bf16),
        shaped((tokens, HEADS * LANES), bf16),
    ]
    img, padded, qraw, kvraw, soft, att, keys, values = call(
        attend_kernel,
        "attend",
        [shaped((tokens, features), bf16)] + whole + [shaped((HEADS, key_total, LANES), bf16)] * 2,
        [
            pltpu.VMEM((HEADS, tokens, LANES), bf16),
            pltpu.VMEM((HEADS, key_total, 2 * LANES), bf16),
        ],
        10**10,
        KA_LIMIT,
        "v" * 7,
        "p" * 8,
        img, wide, biases, lines, taps_wide, pool_lines, ahead,
    )
    *out_pieces, normed, unit, scale, active, slope = call(
        feed_ahead_kernel,
        "feed_ahead",
        [shaped(folded, bf16)] * cycle
        + [
            shaped((tokens, features), bf16),
            shaped((tokens, features), f32),
            shaped((tokens, LANES), f32),
            shaped((tokens, hidden), bf16),
            shaped((tokens, hidden), f32),
        ],
        [pltpu.VMEM((cycle,) + folded, bf16), pltpu.SemaphoreType.DMA((4,))],
        1,
        36,
        "pp" + "v" * 5,
        "a" * cycle + "p" * 5,
        img, att, full_proj, full_up, full_down, biases, lines,
    )
    gmid, gatt, mine, theirs = call(
        functools.partial(feed_back_kernel, owners),
        "feed_back",
        [shaped((tokens, features), bf16), shaped((tokens, HEADS * LANES), bf16)]
        + [shaped((4 * early_rows, LANES), bf16)] * 2,
        [
            pltpu.VMEM((features, hidden), f32),
            pltpu.VMEM((features, hidden), f32),
            pltpu.VMEM((HEADS * LANES, features), f32),
            pltpu.VMEM((8, hidden), f32),
            pltpu.VMEM((32, features), f32),
            pltpu.VMEM((owners, early_rows, LANES), f32),
            pltpu.VMEM((cycle,) + folded, bf16),
            pltpu.SemaphoreType.DMA((4,)),
        ],
        1,
        36,
        "p" + "a" * 4 + "p" * 5 + "v" * 4,
        "pp" + "vv",
        att, *cot_pieces, normed, unit, scale, active, slope, full_proj, full_up, full_down, lines,
    )

    def halved(mine, got):
        return call(
            halve_kernel,
            "halve",
            [shaped((mine.shape[0] // 2, LANES), bf16)] * 2,
            [],
            10**6,
            4,
            "vv",
            "vv",
            mine, got,
        )

    got = trade(theirs, 1)

    def back_attend(head, behind):
        return call(
            functools.partial(back_attend_kernel, head),
            f"back_attend_{head}",
            [
                shaped((rows + 2, cols + 16, LANES), f32),
                shaped((2, rows // 2 + 1, cols // 2 + 8, LANES), f32),
                shaped((136, LANES), f32),
            ],
            [
                pltpu.VMEM((key_total, 2 * LANES), bf16),
                pltpu.VMEM((LANES, LANES), f32),
                pltpu.VMEM((LANES, key_total), f32),
                pltpu.VMEM((LANES, key_total), f32),
                pltpu.VMEM((40, LANES), f32),
            ],
            10**10,
            30,
            "p" * 6 + "vv",
            "ppp",
            qraw, kvraw, soft, gatt, keys, values, pool_lines, behind,
        )

    gpadded_0, gkeypad_0, sums_0 = back_attend(0, behind)
    got, gkeypad_0, behind = lax.optimization_barrier((got, gkeypad_0, behind))
    early, away = halved(mine, got)
    away = trade(away, 2)
    out_pieces = send_on(out_pieces)
    gpadded_1, gkeypad_1, sums_1 = back_attend(1, behind)
    gmix, mine, theirs = call(
        back_weights_kernel,
        "back_weights",
        [shaped((tokens, 3 * HEADS * LANES), bf16)]
        + [shaped((4 * LATE_ROWS + DENSE_ROWS, LANES), bf16)] * 2,
        [
            pltpu.VMEM((rows // 2, 2, cols, LANES), f32),
            pltpu.VMEM((27, 8, LANES), f32),
            pltpu.VMEM((features, 3 * HEADS * LANES), f32),
            pltpu.VMEM((8, 3 * HEADS * LANES), f32),
            pltpu.VMEM((SMALL_ROWS, LANES), f32),
            pltpu.VMEM((DENSE_ROWS, LANES), f32),
            pltpu.VMEM((owners, LATE_ROWS, LANES), f32),
        ],
        10**10,
        30,
        "p" + "p" * 7 + "v" * 3,
        "pvv",
        img, padded, gpadded_0, gpadded_1, gkeypad_0, gkeypad_1, sums_0, sums_1, wide, columns, taps_wide,
    )

    def summed(kernel, *pieces):
        return call(
            kernel,
            "sum_four" if len(pieces) == 4 else "sum_two",
            [shaped(pieces[0].shape, bf16)],
            [],
            1,
            4,
            "v" * len(pieces),
            "v",
            *pieces,
        )[0]

    def ring_trade(cells, flip):
        return lax.ppermute(cells, "rows", [(i, i ^ flip) for i in range(cycle)])

    away, out_pieces, gmix, mine, theirs = lax.optimization_barrier(
        (away, out_pieces, gmix, mine, theirs)
    )
    early, away = halved(early, away)
    away = trade(away, 4)
    got = trade(theirs, 1)
    gimg = call(
        back_images_kernel,
        "back_images",
        [shaped((cycle,) + folded, bf16)],
        [],
        10**10,
        24,
        "pppvv",
        "v",
        img, gmix, gmid, wide, lines,
    )[0]
    got, gimg = lax.optimization_barrier((got, gimg))
    gimg = lax.all_to_all(gimg, "rows", 0, 0, tiled=True)
    early = summed(two_kernel, early, away)
    early = summed(two_kernel, early, ring_trade(early, 1))
    away = ring_trade(early, 2)
    own, *apart = call(
        functools.partial(pair_kernel, DENSE_ROWS),
        "pair",
        [shaped((LATE_ROWS + DENSE_ROWS, LANES), bf16)] * 4,
        [],
        10**6,
        4,
        "vv",
        "vvvv",
        mine, got,
    )
    late = summed(four_kernel, own, *[trade(apart[k], 2 * k + 2) for k in (2, 1, 0)])
    late = summed(two_kernel, late, ring_trade(late, 1))
    late_away = ring_trade(late, 2)
    output, grad_images = call(
        pictures_kernel,
        "pictures",
        [shaped((cycle, block, features), bf16), shaped((cycle, block, features), f32)],
        [],
        1,
        16,
        "v" * 5,
        "v" * 2,
        *out_pieces, gimg,
    )
    late, output, grad_images = lax.optimization_barrier((late, output, grad_images))
    grads = call(
        finish_kernel,
        "finish",
        [
            shaped((share, 3 * features), f32),
            shaped((share, features), f32),
            shaped((share, hidden), f32),
            shaped((share * pieces, features), f32),
            shaped(gains_main.shape, f32),
            shaped(shifts_main.shape, f32),
            shaped(taps.shape, f32),
            shaped(pool_gains.shape, f32),
            shaped(pool_shifts.shape, f32),
            shaped(rel_height.shape, f32),
            shaped(rel_width.shape, f32),
        ],
        [pltpu.VMEM((SMALL_ROWS, LANES), f32), pltpu.VMEM((DENSE_ROWS, LANES), f32)],
        10**8,
        16,
        "v" * 4,
        "v" * 11,
        early, away, late, late_away,
    )
    grads = list(grads)
    grads[6] = grads[6].transpose(1, 0, 2)
    return (output.reshape(images.shape), grad_images.reshape(images.shape), *grads)

def per_device(images, *rest):
    cycle = lax.axis_size("rows")
    image_count, row_count, cols, _ = images.shape
    fits = image_count == cycle and row_count * cycle == 32 and cols == 32
    return whole_image(images, *rest) if fits else row_sharded(images, *rest)


def solution(mesh):
    return jax.shard_map(
        per_device,
        mesh=mesh,
        in_specs=(
            P("batch", "rows", None, None),
            P("batch", None),
            P("batch", None),
            P("batch", None),
            P("batch", None),
            P(),
            P(),
            P(),
            P(),
            P(),
            P(),
            P(),
            P("batch", "rows", None, None),
        ),
        out_specs=(
            P("batch", "rows", None, None),
            P("batch", "rows", None, None),
            P("batch", None),
            P("batch", None),
            P("batch", None),
            P("batch", None),
            P(),
            P(),
            P(),
            P(),
            P(),
            P(),
            P(),
        ),
        check_vma=False,
    )
```

```python
import functools

import jax
import jax.numpy as jnp
from jax import lax
from jax.experimental import pallas as pl
from jax.experimental.pallas import tpu as pltpu
from jax.sharding import PartitionSpec as P

HEADS = 2
HEAD_DIM = 96


norm_eps = 1e-06
highest = lax.Precision.HIGHEST


def padded(cells, sides, width):
    for axis, dim in sides:
        count = lax.axis_size(axis)
        ends = count - 1
        head = lax.slice_in_dim(cells, 0, width, axis=dim)
        tail = lax.slice_in_dim(cells, cells.shape[dim] - width, cells.shape[dim], axis=dim)
        cells = jnp.concatenate(
            [
                lax.ppermute(tail, axis, [(i, (i + 1) % count) for i in range(ends)]),
                cells,
                lax.ppermute(head, axis, [((i + 1) % count, i) for i in range(ends)]),
            ],
            axis=dim,
        )
    return cells


def layer_norm(values, gains, shifts):
    centre = jnp.mean(values, -1, keepdims=True)
    centred = values - centre
    spread = jnp.mean(centred * centred, -1, keepdims=True)
    return centred * lax.rsqrt(spread + norm_eps) * gains + shifts


def gelu_tanh(values):
    return jax.nn.gelu(values, approximate=True)


def pool_section(section, kernel, stride):
    image_count, ext_rows, col_count, features = section.shape
    out_rows = (ext_rows - 2) // stride
    out_cols = col_count // stride
    col_out = jnp.arange(out_cols)[:, None] * stride
    col_in = jnp.arange(col_count)[None, :]
    shifted = []
    for offset_col in range(3):
        picker = (col_out + offset_col - 1 == col_in).astype(jnp.float32)
        shifted.append(jnp.einsum("jy,bxyc->bxjc", picker, section, precision=highest))
    summed = jnp.zeros((image_count, out_rows, out_cols, features), jnp.float32)
    for offset_row in range(3):
        for offset_col in range(3):
            window = shifted[offset_col][:, offset_row : offset_row + ext_rows - 2]
            if stride == 2:
                window = window.reshape(image_count, out_rows, 2, out_cols, features)[:, :, 0]
            summed = summed + window * kernel[3 * offset_row + offset_col]
    return summed


def pooled_local(extended_f, kernels, gains, shifts):
    features = extended_f.shape[-1]
    head_dim = kernels.shape[-1]
    head_count = features // head_dim
    results = []
    for member, stride in ((0, 1), (1, 2), (2, 2)):
        pooled = pool_section(
            extended_f[member], jnp.tile(kernels[member], (1, head_count)), stride
        )
        pooled = pooled.reshape(pooled.shape[:-1] + (head_count, head_dim))
        offset = (
            shifts[0] if member == 0 else shifts[1] if member == 2 else jnp.zeros_like(shifts[0])
        )
        results.append(layer_norm(pooled, gains[member], offset))
    return tuple(results)


def row_sharded(
    images,
    w_qkv,
    w_proj,
    w_up,
    w_down,
    gains_main,
    shifts_main,
    pool_kernels,
    pool_gains,
    pool_shifts,
    rel_height,
    rel_width,
    cotangent,
):
    image_count, row_count, col_count, features = images.shape
    head_dim = HEAD_DIM
    head_count = HEADS
    scale_factor = head_dim ** (-0.5)
    cycle_size = lax.axis_size("rows")
    key_rows_all = row_count * cycle_size // 2
    key_cols = col_count // 2
    key_total = key_rows_all * key_cols
    query_count = row_count * col_count
    key_local = row_count // 2 * key_cols
    gain_rows = gains_main.astype(jnp.float32)
    shift_rows = shifts_main.astype(jnp.float32)
    full_qkv, full_proj, full_up, full_down = (
        lax.all_gather(w_qkv, "batch", axis=0, tiled=True),
        lax.all_gather(w_proj, "batch", axis=0, tiled=True),
        lax.all_gather(w_up, "batch", axis=0, tiled=True),
        lax.all_gather(w_down, "batch", axis=0, tiled=True),
    )
    qkv_split = full_qkv.reshape(features, 3, features)
    inputs_f = images.astype(jnp.float32)
    normed_one, norm_one_pullback = jax.vjp(layer_norm, inputs_f, gain_rows[0], shift_rows[0])
    normed_low = normed_one.astype(jnp.bfloat16)
    mixed = (
        jnp.einsum("bxyd,dme->mbxye", normed_low, qkv_split, preferred_element_type=jnp.float32)
        + shift_rows[2:5][:, None, None, None, :]
    )
    mixed_low = mixed.astype(jnp.bfloat16)
    extended = padded(mixed_low, (("rows", 2),), 1)
    (queries, keys_pooled, values_pooled), pool_pullback = jax.vjp(
        pooled_local,
        extended.astype(jnp.float32),
        pool_kernels.astype(jnp.float32),
        pool_gains.astype(jnp.float32),
        pool_shifts.astype(jnp.float32),
    )
    queries_low = queries.astype(jnp.bfloat16)
    query_flat = queries_low.reshape(image_count, query_count, head_count, head_dim)
    keys_low = keys_pooled.astype(jnp.bfloat16).reshape(image_count, key_local, features)
    values_low = values_pooled.astype(jnp.bfloat16).reshape(image_count, key_local, features)
    key_value = jnp.concatenate([keys_low, values_low], -1)
    first_row = lax.axis_index("rows") * row_count

    def rel_terms(query_vals, table_height, table_width):
        row_place = first_row + jnp.arange(row_count)
        dist_height = (
            row_place[:, None] - 2 * jnp.arange(key_rows_all)[None, :] + 2 * (key_rows_all - 1)
        )
        pick_height = (
            dist_height[:, :, None] == jnp.arange(table_height.shape[0])[None, None, :]
        ).astype(jnp.float32)
        lookup_height = jnp.einsum("xjt,tc->xjc", pick_height, table_height, precision=highest)
        dist_width = (
            jnp.arange(col_count)[:, None] - 2 * jnp.arange(key_cols)[None, :] + 2 * (key_cols - 1)
        )
        pick_width = (
            dist_width[:, :, None] == jnp.arange(table_width.shape[0])[None, None, :]
        ).astype(jnp.float32)
        lookup_width = jnp.einsum("yjt,tc->yjc", pick_width, table_width, precision=highest)
        term_height = jnp.einsum("bxyhc,xjc->bhxyj", query_vals, lookup_height, precision=highest)
        term_width = jnp.einsum("bxyhc,yjc->bhxyj", query_vals, lookup_width, precision=highest)
        return (term_height, term_width)

    (term_height, term_width), rel_pullback = jax.vjp(
        rel_terms,
        queries_low.astype(jnp.float32),
        rel_height.astype(jnp.float32),
        rel_width.astype(jnp.float32),
    )
    rel_full = (term_height[..., :, None] + term_width[..., None, :]).reshape(
        image_count, head_count, query_count, key_total
    )

    def key_scores(key_piece):
        piece_rows = key_piece.shape[1]
        keys_part = key_piece[..., :features].reshape(image_count, piece_rows, head_count, head_dim)
        products = jnp.einsum(
            "bqhc,bkhc->bhqk", query_flat, keys_part, preferred_element_type=jnp.float32
        )
        return products * scale_factor + lax.slice_in_dim(rel_full, 0, piece_rows, axis=3)

    key_piece = lax.all_gather(key_value, "rows", axis=1, tiled=True)
    run_max = jnp.full((image_count, head_count, query_count), -1e30, jnp.float32)
    run_sum = jnp.zeros((image_count, head_count, query_count), jnp.float32)
    run_acc = jnp.zeros((image_count, head_count, query_count, head_dim), jnp.float32)
    piece_rows = key_piece.shape[1]
    values_part = key_piece[..., features:].reshape(image_count, piece_rows, head_count, head_dim)
    scores = key_scores(key_piece)
    new_max = jnp.maximum(run_max, jnp.max(scores, -1))
    weights_exp = jnp.exp(scores - new_max[..., None])
    factor = jnp.exp(run_max - new_max)
    run_sum = run_sum * factor + jnp.sum(weights_exp, -1)
    run_acc = run_acc * factor[..., None] + jnp.einsum(
        "bhqk,bkhc->bhqc", weights_exp, values_part.astype(jnp.float32), precision=highest
    )
    run_max, run_sum, run_acc = (new_max, run_sum, run_acc)
    log_total = run_max + jnp.log(run_sum)
    attended = (run_acc / run_sum[..., None]).transpose(0, 2, 1, 3) + query_flat.astype(jnp.float32)
    attended_low = attended.reshape(image_count, row_count, col_count, features).astype(
        jnp.bfloat16
    )
    branch = (
        jnp.einsum("bxyd,de->bxye", attended_low, full_proj, preferred_element_type=jnp.float32)
        + shift_rows[5]
    )
    middle = inputs_f + branch
    normed_two, norm_two_pullback = jax.vjp(layer_norm, middle, gain_rows[1], shift_rows[1])
    normed_two_low = normed_two.astype(jnp.bfloat16)
    hidden = jnp.einsum(
        "bxyd,df->bxyf", normed_two_low, full_up, preferred_element_type=jnp.float32
    ) + shift_rows[6:-1].reshape(-1)
    activated, gelu_pullback = jax.vjp(gelu_tanh, hidden)
    activated_low = activated.astype(jnp.bfloat16)
    output = (
        middle
        + jnp.einsum("bxyf,fd->bxyd", activated_low, full_down, preferred_element_type=jnp.float32)
        + shift_rows[-1]
    )
    output_low = output.astype(jnp.bfloat16)
    upstream = cotangent.astype(jnp.float32)
    grad_down = jnp.einsum(
        "bxyf,bxyd->fd", activated_low, cotangent, preferred_element_type=jnp.float32
    )
    grad_shift_down = jnp.sum(upstream, (0, 1, 2))
    grad_activated = jnp.einsum(
        "bxyd,fd->bxyf", cotangent, full_down, preferred_element_type=jnp.float32
    )
    (grad_hidden,) = gelu_pullback(grad_activated)
    grad_hidden_low = grad_hidden.astype(jnp.bfloat16)
    grad_up = jnp.einsum(
        "bxyd,bxyf->df", normed_two_low, grad_hidden_low, preferred_element_type=jnp.float32
    )
    grad_shift_up = jnp.sum(grad_hidden_low.astype(jnp.float32), (0, 1, 2))
    grad_normed_two = jnp.einsum(
        "bxyf,df->bxyd", grad_hidden_low, full_up, preferred_element_type=jnp.float32
    )
    grad_middle_norm, grad_gain_two, grad_shift_two = norm_two_pullback(grad_normed_two)
    grad_middle = upstream + grad_middle_norm
    grad_branch_low = grad_middle.astype(jnp.bfloat16)
    grad_proj = jnp.einsum(
        "bxyd,bxye->de", attended_low, grad_branch_low, preferred_element_type=jnp.float32
    )
    grad_shift_proj = jnp.sum(grad_branch_low.astype(jnp.float32), (0, 1, 2))
    grad_attended = jnp.einsum(
        "bxye,de->bxyd", grad_branch_low, full_proj, preferred_element_type=jnp.float32
    )
    grad_flat = grad_attended.astype(jnp.bfloat16).reshape(
        image_count, query_count, head_count, head_dim
    )
    grad_flat_f = grad_flat.astype(jnp.float32)
    key_value_all = lax.all_gather(key_value, "rows", axis=1, tiled=True)
    scores = key_scores(key_value_all)
    soft = jnp.exp(scores - log_total[..., None])
    keys_all = key_value_all[..., :features].reshape(image_count, key_total, head_count, head_dim)
    values_all = key_value_all[..., features:].reshape(image_count, key_total, head_count, head_dim)
    grad_soft = jnp.einsum(
        "bqhc,bkhc->bhqk", grad_flat, values_all, preferred_element_type=jnp.float32
    )
    row_dot = jnp.sum(soft * grad_soft, -1, keepdims=True)
    grad_scores = (soft * (grad_soft - row_dot)).astype(jnp.bfloat16)
    grad_queries = (
        scale_factor
        * jnp.einsum("bhqk,bkhc->bqhc", grad_scores, keys_all, preferred_element_type=jnp.float32)
        + grad_flat_f
    )
    grad_scores_f = grad_scores.astype(jnp.float32).reshape(
        image_count, head_count, row_count, col_count, key_rows_all, key_cols
    )
    grad_query_rel, grad_rel_h, grad_rel_w = rel_pullback(
        (jnp.sum(grad_scores_f, -1), jnp.sum(grad_scores_f, -2))
    )
    grad_queries = (
        grad_queries.reshape(image_count, row_count, col_count, head_count, head_dim)
        + grad_query_rel
    )
    key_span = key_local * lax.axis_size("rows")
    part_scores = lax.slice_in_dim(grad_scores, 0, key_span, axis=3)
    part_soft = lax.slice_in_dim(soft, 0, key_span, axis=3)
    grad_keys_part = scale_factor * jnp.einsum(
        "bhqk,bqhc->kbhc", part_scores, query_flat, preferred_element_type=jnp.float32
    )
    grad_values_part = jnp.einsum("bhqk,bqhc->kbhc", part_soft, grad_flat_f, precision=highest)
    key_grads = (
        lax.psum_scatter(
            jnp.concatenate(
                [
                    grad_keys_part.reshape(key_span, image_count, features),
                    grad_values_part.reshape(key_span, image_count, features),
                ],
                -1,
            ).astype(jnp.bfloat16),
            "rows",
            scatter_dimension=0,
            tiled=True,
        )
        .astype(jnp.float32)
        .transpose(1, 0, 2)
    )
    grad_keys = key_grads[..., :features].reshape(
        image_count, row_count // 2, key_cols, head_count, head_dim
    )
    grad_values = key_grads[..., features:].reshape(
        image_count, row_count // 2, key_cols, head_count, head_dim
    )
    grad_extended, grad_kernels, grad_pool_gain, grad_pool_shift = pool_pullback(
        (grad_queries, grad_keys, grad_values)
    )
    rims = jnp.concatenate([grad_extended[:, :, :1], grad_extended[:, :, -1:]], 2)
    rims_all = padded(rims.astype(jnp.bfloat16), (("rows", 2),), 1).astype(rims.dtype)
    grad_mixed = grad_extended[:, :, 1:-1]
    grad_mixed = grad_mixed.at[:, :, 0].add(rims_all[:, :, 0]).at[:, :, -1].add(rims_all[:, :, 3])
    grad_mixed_low = grad_mixed.astype(jnp.bfloat16)
    grad_qkv = jnp.einsum(
        "bxyd,mbxye->dme", normed_low, grad_mixed_low, preferred_element_type=jnp.float32
    ).reshape(features, 3 * features)
    grad_shift_qkv = jnp.sum(grad_mixed_low.astype(jnp.float32), (1, 2, 3))
    grad_normed_one = jnp.einsum(
        "mbxye,dme->bxyd", grad_mixed_low, qkv_split, preferred_element_type=jnp.float32
    )
    grad_inputs_norm, grad_gain_one, grad_shift_one = norm_one_pullback(grad_normed_one)
    grad_images = grad_middle + grad_inputs_norm
    grad_gains = jnp.stack([grad_gain_one, grad_gain_two])
    grad_shifts = jnp.concatenate(
        [
            grad_shift_one[None],
            grad_shift_two[None],
            grad_shift_qkv,
            grad_shift_proj[None],
            grad_shift_up.reshape(-1, features),
            grad_shift_down[None],
        ],
        0,
    )
    small_summed = lax.psum(
        (
            grad_gains,
            grad_shifts,
            grad_kernels,
            grad_pool_gain,
            grad_pool_shift,
            grad_rel_h,
            grad_rel_w,
        ),
        ("batch", "rows"),
    )
    matrix_grads = (grad_qkv, grad_proj, grad_up, grad_down)
    summed_rows = (
        lax.psum(matrix_grads[0].astype(jnp.bfloat16), "rows").astype(jnp.float32),
        lax.psum(matrix_grads[1].astype(jnp.bfloat16), "rows").astype(jnp.float32),
        lax.psum(matrix_grads[2].astype(jnp.bfloat16), "rows").astype(jnp.float32),
        lax.psum(matrix_grads[3].astype(jnp.bfloat16), "rows").astype(jnp.float32),
    )
    owned = (
        lax.psum_scatter(
            summed_rows[0].astype(jnp.bfloat16), "batch", scatter_dimension=0, tiled=True
        ).astype(jnp.float32),
        lax.psum_scatter(
            summed_rows[1].astype(jnp.bfloat16), "batch", scatter_dimension=0, tiled=True
        ).astype(jnp.float32),
        lax.psum_scatter(
            summed_rows[2].astype(jnp.bfloat16), "batch", scatter_dimension=0, tiled=True
        ).astype(jnp.float32),
        lax.psum_scatter(
            summed_rows[3].astype(jnp.bfloat16), "batch", scatter_dimension=0, tiled=True
        ).astype(jnp.float32),
    )
    return (
        output_low,
        grad_images,
        owned[0],
        owned[1],
        owned[2],
        owned[3],
        small_summed[0],
        small_summed[1],
        small_summed[2],
        small_summed[3],
        small_summed[4],
        small_summed[5],
        small_summed[6],
    )


LANES = 128
NT = (((1,), (1,)), ((), ()))
TN = (((0,), (0,)), ((), ()))
NN = (((1,), (0,)), ((), ()))
f32 = jnp.float32
bf16 = jnp.bfloat16


def dot(a, b, dims=NN):
    return lax.dot_general(a, b, dims, preferred_element_type=f32)


def lane_ids(shape):
    return lax.broadcasted_iota(jnp.int32, shape, len(shape) - 1)


def head_mask(rows):
    return (lane_ids((rows, LANES)) < HEAD_DIM).astype(f32)


def head_piece(values, start):
    base = start // LANES * LANES
    move = start - base
    if move == 0:
        piece = values[:, base : base + LANES]
    else:
        piece = pltpu.roll(values[:, base : base + 2 * LANES], 2 * LANES - move, 1)[:, :LANES]
    return piece * head_mask(values.shape[0])


def norm_parts(values, count):
    centre = jnp.sum(values, -1, keepdims=True) * (1.0 / count)
    centred = values - centre
    spread = jnp.sum(centred * centred, -1, keepdims=True) * (1.0 / count)
    scale = lax.rsqrt(spread + norm_eps)
    return centred * scale, scale


def head_norm_parts(values, mask):
    centre = jnp.sum(values, -1, keepdims=True) * (1.0 / HEAD_DIM)
    centred = (values - centre) * mask
    spread = jnp.sum(centred * centred, -1, keepdims=True) * (1.0 / HEAD_DIM)
    scale = lax.rsqrt(spread + norm_eps)
    return centred * scale, scale


def norm_back(grad, unit, scale, count):
    first = jnp.sum(grad, -1, keepdims=True) * (1.0 / count)
    second = jnp.sum(grad * unit, -1, keepdims=True) * (1.0 / count)
    return scale * (grad - first - unit * second)


def fold_rows(values):
    rows, lanes = values.shape
    return jnp.sum(values.reshape(rows // 8, 8, lanes), 0)


def fold_block(values):
    rows = values.shape[0]
    tail = values[:, LANES : LANES + 64].astype(f32)
    tail = jnp.concatenate([tail, jnp.zeros_like(tail)], 1)
    side = tail[: rows // 2] + pltpu.roll(tail[rows // 2 :], 64, 1)
    return jnp.concatenate([values[:, :LANES].astype(bf16), side.astype(bf16)], 0)


def unfold_block(folded):
    rows = folded.shape[0] * 2 // 3
    side = folded[rows:].astype(f32)
    tail = jnp.concatenate([side, pltpu.roll(side, 64, 1)], 0).astype(folded.dtype)
    return jnp.concatenate([folded[:rows], tail[:, :64]], 1)


def turned(shift):
    return lax.rem(lax.axis_index("rows") + shift, 4)


def copy_all(pairs, sems):
    copies = []
    for near, far in pairs:
        copies.append(pltpu.make_async_copy(near, far, sems.at[len(copies)]))
        copies[-1].start()
    return copies


def wait_all(copies):
    for copy in copies:
        copy.wait()


def pack_kernel(qkv_ref, proj_ref, up_ref, down_ref, packed_ref, qkv_in, proj_in, up_in, down_in, sems):
    wait_all(
        copy_all(
            [(qkv_ref, qkv_in), (proj_ref, proj_in), (up_ref, up_in), (down_ref, down_in)], sems
        )
    )
    share = qkv_in.shape[0]
    packed_ref[...] = jnp.concatenate(
        [qkv_in[...].astype(f32), proj_in[...].astype(f32), up_in[...].astype(f32)]
        + [
            down_in[...].astype(f32)[share * i : share * (i + 1)]
            for i in range(down_in.shape[0] // share)
        ],
        1,
    ).astype(bf16)


def fold_images_kernel(img_ref, out_ref, img_in, sems):
    loads = copy_all([(img_ref.at[k], img_in.at[k]) for k in range(4)], sems)
    for block in range(4):
        loads[block].wait()
        out_ref[block] = fold_block(img_in[block])


def fold_kernel(cot_ref, cot_0, cot_1, cot_2, cot_3, cot_in, cot_scr, in_sems, sems):
    loads = copy_all([(cot_ref.at[turned(k)], cot_in.at[k]) for k in range(4)], in_sems)
    copies = []
    for shift, far in enumerate((cot_0, cot_1, cot_2, cot_3)):
        loads[shift].wait()
        cot_scr[shift] = fold_block(cot_in[shift])
        copies.append(pltpu.make_async_copy(cot_scr.at[shift], far, sems.at[shift]))
        copies[-1].start()
    wait_all(copies)


def flipped(flip):
    place = lax.axis_index("batch")
    owner = place
    for bit in (1, 2, 4):
        if flip & bit:
            owner = owner + bit - 2 * bit * lax.rem(place // bit, 2)
    return owner


def gather_rows(own_ref, other_ref, first, last, full_scr):
    share = own_ref.shape[1]
    for flip in range(8):
        source = other_ref if flip & 1 else own_ref
        rows = pl.ds(pl.multiple_of(flipped(flip) * share, 8), share)
        full_scr[rows, :] = source[flip // 2, :, first:last].astype(f32)


def load_taps(kernel_ref, kernel_scr):
    kernel_scr[...] = jnp.zeros_like(kernel_scr)
    for tap in range(9):
        kernel_scr[tap, 0:3, 0:HEAD_DIM] = kernel_ref[tap].astype(f32)


def load_gains(gain_ref, shift_ref, gain_scr):
    gain_scr[...] = jnp.zeros_like(gain_scr)
    gain_scr[0:3, 0:HEAD_DIM] = gain_ref[...].astype(f32)
    gain_scr[3:5, 0:HEAD_DIM] = shift_ref[...].astype(f32)


def clear_rim(padded_scr):
    rows, cols, lanes = padded_scr.shape[-3:]
    for place in range(padded_scr.shape[0] if len(padded_scr.shape) == 4 else 1):
        cells = padded_scr.at[place] if len(padded_scr.shape) == 4 else padded_scr
        cells[0:1] = jnp.zeros((1, cols, lanes), f32)
        cells[rows - 1 : rows] = jnp.zeros((1, cols, lanes), f32)
        cells[:, 0:8, :] = jnp.zeros((rows, 8, lanes), f32)
        cells[:, cols - 8 : cols, :] = jnp.zeros((rows, 8, lanes), f32)


CHUNK_ROWS = 4
MIX_ROWS = 32
ATTEND_ROWS = 32
BACK_ROWS = 32
WEIGH_TILE = 1024
IMAGE_TILE = 1024
LOG2_E = 1.4426950408889634


def stride_windows(padded, place, side, key_rows, key_cols):
    columns = pl.ds(7 + side, key_cols, stride=2)
    even = padded[place, pl.ds(0, key_rows + 1, stride=2), columns, :]
    odd = padded[place, pl.ds(1, key_rows, stride=2), columns, :]
    return even[:key_rows], odd, even[1:]


def attend_kernel(
    stage, weight_scr, bias_ref, rows_ref, kern_scr, gain_scr, table_ref,
    img_ref, norm_out, scale_out, padded, qunit_out, qscale_out, kvraw_out, soft_out, att_out, key_out, val_out,
    query_scr, keyaug_scr,
):
    cols = padded.shape[2] - 16
    rows = padded.shape[1] - 2
    tile = CHUNK_ROWS * cols
    chunks = rows // CHUNK_ROWS
    key_cols = cols // 2
    key_rows = rows // 2
    key_total = key_rows * key_cols
    features = img_ref.shape[1]
    clear_rim(padded)
    gain_one = rows_ref[16:17, 0:features]
    shift_one = rows_ref[0:1, 0:features]
    table = table_ref[...]

    mix_tile = MIX_ROWS * cols

    img_ref[...] = jnp.concatenate(
        [unfold_block(stage[place]) for place in range(4)], 0
    )

    def mix(step, carry):
        span = pl.ds(pl.multiple_of(step * mix_tile, mix_tile), mix_tile)
        unit, scale = norm_parts(img_ref[span, :].astype(f32), features)
        norm_out[span, :] = unit
        scale_out[span, :] = jnp.broadcast_to(scale, (mix_tile, features))
        normed = (unit * gain_one + shift_one).astype(bf16)
        mixed = dot(normed, weight_scr[...]) + bias_ref[0:1, :]
        for place in range(3 * HEADS):
            low = mixed[:, place * LANES : (place + 1) * LANES].astype(bf16)
            padded[place, pl.ds(1 + step * MIX_ROWS, MIX_ROWS), 8 : 8 + cols, :] = low.astype(
                f32
            ).reshape(MIX_ROWS, cols, LANES)
        return carry

    lax.fori_loop(0, rows // MIX_ROWS, mix, 0, unroll=True)

    tile_mask = head_mask(tile)

    def pool_queries(step, carry):
        span = pl.ds(pl.multiple_of(step * tile, tile), tile)
        for head in range(HEADS):
            total = jnp.zeros((CHUNK_ROWS, cols, LANES), f32)
            for side in range(3):
                window = padded[
                    head, pl.ds(step * CHUNK_ROWS, CHUNK_ROWS + 2), 7 + side : 7 + side + cols, :
                ]
                for up in range(3):
                    total = total + window[up : up + CHUNK_ROWS] * kern_scr[3 * up + side, 0:1, :]
            unit, scale = head_norm_parts(total.reshape(tile, LANES), tile_mask)
            qunit_out[head, span, :] = unit
            qscale_out[head, span, :] = jnp.broadcast_to(scale, (tile, LANES))
            query_scr[head, span, :] = (unit * gain_scr[0:1, :] + gain_scr[3:4, :]).astype(bf16)
        return carry

    lax.fori_loop(0, chunks, pool_queries, 0, unroll=True)

    for place in range(2 * HEADS):
        member = 1 + place // HEADS
        total = jnp.zeros((key_rows, key_cols, LANES), f32)
        for side in range(3):
            for up, window in enumerate(stride_windows(padded, HEADS + place, side, key_rows, key_cols)):
                total = total + window * kern_scr[3 * up + side, member : member + 1, :]
        kvraw_out[place] = total.reshape(key_total, LANES)

    key_mask = head_mask(key_total)
    key_place = lax.broadcasted_iota(jnp.int32, (key_total, LANES), 0)
    lanes = lane_ids((key_total, LANES))
    from_row = 30 - 2 * (key_place // key_cols)
    from_col = 96 + 2 * (key_place % key_cols)
    hot = (
        (lanes == from_row)
        | (lanes == from_row + 64)
        | (lanes == from_col)
        | (lanes == from_col - 64)
    ).astype(bf16)
    for head in range(HEADS):
        unit, _ = head_norm_parts(kvraw_out[head], key_mask)
        low = (unit * gain_scr[1:2, :]).astype(bf16)
        key_out[head] = low
        keyaug_scr[head, :, 0:LANES] = low
        keyaug_scr[head, :, LANES : 2 * LANES] = hot
        unit, _ = head_norm_parts(kvraw_out[HEADS + head], key_mask)
        val_out[head] = (unit * gain_scr[2:3, :] + gain_scr[4:5, :]).astype(bf16)

    scale_factor = HEAD_DIM ** (-0.5)
    row_lanes = lane_ids((cols, LANES))
    part_tile = ATTEND_ROWS * cols
    part_lanes = lane_ids((part_tile, LANES))

    def attend(step, carry):
        span = pl.ds(pl.multiple_of(step * part_tile, part_tile), part_tile)
        for head in range(HEADS):
            query = query_scr[head, span, :]
            looked = dot(query, table, NT) * (1.0 / scale_factor)
            pieces = []
            for row in range(ATTEND_ROWS):
                part = looked[row * cols : (row + 1) * cols, :]
                place = step * ATTEND_ROWS + row
                by_row = pltpu.roll(part, LANES - place, 1)
                by_col = pltpu.roll(part, 0, 1, stride=1, stride_axis=0)
                pieces.append(jnp.where(row_lanes < 64, by_row, by_col))
            terms = jnp.concatenate(pieces, 0)
            high = terms.astype(bf16).astype(f32)
            rest = pltpu.roll(terms - high, 64, 1)
            both = jnp.where((part_lanes < 32) | (part_lanes >= 96), high, rest).astype(bf16)
            scores = dot(jnp.concatenate([query, both], 1), keyaug_scr[head], NT)
            top = jnp.max(scores, -1, keepdims=True)
            powers = jnp.exp2((scores - top) * (scale_factor * LOG2_E))
            soft = (powers * (1.0 / jnp.sum(powers, -1, keepdims=True))).astype(bf16)
            soft_out[head, span, :] = soft
            att = dot(soft, val_out[head]) + query.astype(f32)
            att_out[span, head * LANES : (head + 1) * LANES] = att.astype(bf16)
        return carry

    lax.fori_loop(0, rows // ATTEND_ROWS, attend, 0, unroll=True)


def stack_blocks(values, block_scr):
    owners = block_scr.shape[0]
    share = values.shape[0] // owners
    for block in range(values.shape[1] // LANES):
        for owner in range(owners):
            block_scr[owner, share * block : share * (block + 1), :] = values[
                share * owner : share * (owner + 1), block * LANES : (block + 1) * LANES
            ]


def split_owners(block_scr, mine_ref, theirs_ref, order):
    count = block_scr.shape[1]
    for place, flip in enumerate(order):
        span = pl.ds(place * count, count)
        mine_ref[span, :] = block_scr[flipped(flip)].astype(bf16)
        theirs_ref[span, :] = block_scr[flipped(flip + 1)].astype(bf16)


def weights_kernel(
    owners, own_ref, other_ref, gains_far, shifts_far, kern_far, pgain_far, pshift_far, relh_far, relw_far,
    wide_ref, proj_ref, up_ref, down_ref, bias_ref, rows_ref, columns_ref, taps_ref, pool_ref, ahead_ref, behind_ref,
    full_scr, down_scr, gains_in, shifts_in, kern_in, pgain_in, pshift_in, relh_in, relw_in, table_scr, sems,
):
    loads = copy_all(
        [
            (gains_far, gains_in), (shifts_far, shifts_in), (kern_far, kern_in), (pgain_far, pgain_in),
            (pshift_far, pshift_in), (relh_far, relh_in), (relw_far, relw_in),
        ],
        sems,
    )
    gather_rows(own_ref, other_ref, 0, own_ref.shape[2], full_scr)
    for place in range(3 * HEADS):
        wide_ref[:, place * LANES : (place + 1) * LANES] = head_piece(
            full_scr[:, 0 : 5 * LANES], place * HEAD_DIM
        ).astype(bf16)
    features, hidden_count = up_ref.shape
    proj = pltpu.roll(full_scr[:, 4 * LANES : 6 * LANES], 192, 1)[:, 0:features]
    gap = jnp.zeros((LANES - HEAD_DIM, features), f32)
    proj_ref[...] = jnp.concatenate(
        [proj[0:HEAD_DIM, :], gap, proj[HEAD_DIM : 2 * HEAD_DIM, :], gap], 0
    ).astype(bf16)
    up_ref[...] = full_scr[:, 4 * features : 4 * features + hidden_count].astype(bf16)
    columns = full_scr[:, 4 * features + hidden_count :]
    share = features // owners
    pieces = hidden_count // features
    for piece in range(pieces):
        start = piece * features
        base = start // LANES * LANES
        window = columns[:, base : base + 2 * LANES]
        if start != base:
            window = pltpu.roll(window, 2 * LANES - (start - base), 1)
        for owner in range(owners):
            place = owner * share * pieces + piece * share
            down_scr[place : place + share, :] = window[
                owner * share : (owner + 1) * share, 0:features
            ]
    down_ref[...] = down_scr[...].astype(bf16)
    wait_all(loads)
    rows_ref[...] = jnp.zeros_like(rows_ref)
    rows_ref[0 : shifts_in.shape[0], 0:features] = shifts_in[...].astype(f32)
    rows_ref[16:18, 0:features] = gains_in[...].astype(f32)
    columns_ref[...] = jnp.concatenate(
        [rows_ref[...], jnp.zeros((LANES - rows_ref.shape[0], 2 * LANES), f32)], 0
    ).T
    bias_ref[...] = jnp.zeros_like(bias_ref)
    for section in range(3):
        for head in range(HEADS):
            place = (section * HEADS + head) * LANES
            bias_ref[0:1, place : place + LANES] = head_piece(
                rows_ref[2 + section : 3 + section, :], head * HEAD_DIM
            )
    for piece in range(pieces):
        bias_ref[1:2, piece * features : (piece + 1) * features] = rows_ref[
            6 + piece : 7 + piece, 0:features
        ]
    load_taps(kern_in, taps_ref)
    load_gains(pgain_in, pshift_in, pool_ref)
    count = relw_in.shape[0]
    table_scr[...] = jnp.zeros_like(table_scr)
    table_scr[0:count, 0:HEAD_DIM] = relh_in[...].astype(f32)
    table_scr[64 : 64 + count, 0:HEAD_DIM] = relw_in[...].astype(f32)
    behind_ref[...] = table_scr[...].astype(bf16)
    flip = (
        lax.broadcasted_iota(jnp.int32, (64, count), 0) + lax.broadcasted_iota(jnp.int32, (64, count), 1)
        == count - 1
    ).astype(bf16)
    table_scr[64:128, 0:HEAD_DIM] = dot(flip, relw_in[...])
    ahead_ref[...] = table_scr[...].astype(bf16)


def send_turned(near, fars, sems):
    sends = []
    for shift, far in enumerate(fars):
        sends.append(pltpu.make_async_copy(near.at[turned(shift)], far, sems.at[shift]))
        sends[-1].start()
    return sends


GELU_A = 0.7978845608028654
GELU_B = 0.044715


def feed_ahead_kernel(
    img_ref, att_ref, proj_ref, up_ref, down_ref, bias_ref, rows_ref,
    out_0, out_1, out_2, out_3, normed_ref, unit_ref, scale_ref, active_ref, slope_ref,
    out_stage, turn_sems,
):
    tokens, features = img_ref.shape
    pieces = up_ref.shape[1] // features
    block = tokens // 4
    middle = img_ref[...].astype(f32) + (dot(att_ref[...], proj_ref[...]) + rows_ref[5:6, 0:features])
    unit, scale = norm_parts(middle, features)
    normed = (unit * rows_ref[17:18, 0:features] + rows_ref[1:2, 0:features]).astype(bf16)
    unit_ref[...] = unit
    scale_ref[...] = jnp.broadcast_to(scale, scale_ref.shape)
    normed_ref[...] = normed
    hidden = dot(normed, up_ref[...]) + bias_ref[1:2, :]
    square = hidden * hidden
    wave = jnp.tanh(hidden * (GELU_A + (GELU_A * GELU_B) * square))
    half = 0.5 + 0.5 * wave
    active = (hidden * half).astype(bf16)
    active_ref[...] = active
    slope_ref[...] = half * (
        1.0 + (1.0 - half) * (hidden * (2.0 * GELU_A + (6.0 * GELU_A * GELU_B) * square))
    )
    out = middle + dot(active, down_ref[...]) + rows_ref[6 + pieces : 7 + pieces, 0:features]
    for place in range(4):
        out_stage[place] = fold_block(out[place * block : (place + 1) * block, :])
    wait_all(send_turned(out_stage, (out_0, out_1, out_2, out_3), turn_sems))


def feed_back_kernel(
    owners,
    att_ref, cot_0, cot_1, cot_2, cot_3, normed_ref, unit_ref, scale_ref, active_ref, slope_ref,
    proj_ref, up_ref, down_ref, rows_ref,
    mid_ref, gatt_ref, mine_ref, theirs_ref,
    gdown, gup, gproj, gbias, gsmall, block_scr, cot_stage, cot_sems,
):
    cot_loads = copy_all(
        [(piece, cot_stage.at[turned(4 - k)]) for k, piece in enumerate((cot_0, cot_1, cot_2, cot_3))],
        cot_sems,
    )
    tokens, features = unit_ref.shape
    hidden_count = up_ref.shape[1]
    pieces = hidden_count // features
    unit = unit_ref[...]
    att = att_ref[...]
    wait_all(cot_loads)
    cot_low = jnp.concatenate([unfold_block(cot_stage[place]) for place in range(4)], 0)
    cot = cot_low.astype(f32)
    gdown[...] = dot(cot_low, active_ref[...], TN)
    gact = dot(cot_low, down_ref[...], NT)
    ghid = (gact * slope_ref[...]).astype(bf16)
    gup[...] = dot(normed_ref[...], ghid, TN)
    gbias[...] = fold_rows(ghid.astype(f32))
    gnorm = dot(ghid, up_ref[...], NT)
    gsmall[0:8, :] = fold_rows(gnorm * unit)
    gsmall[8:16, :] = fold_rows(gnorm)
    gmid = cot + norm_back(gnorm * rows_ref[17:18, 0:features], unit, scale_ref[...], features)
    gbranch = gmid.astype(bf16)
    mid_ref[...] = gbranch
    gsmall[16:24, :] = fold_rows(gbranch.astype(f32))
    gsmall[24:32, :] = fold_rows(cot)
    gproj[...] = dot(att, gbranch, TN)
    gatt_ref[...] = dot(gbranch, proj_ref[...], NT).astype(bf16)

    share = features // owners
    proj = jnp.concatenate(
        [gproj[head * LANES : head * LANES + HEAD_DIM, :] for head in range(HEADS)], 0
    )
    down = gdown[...].T
    down_pieces = []
    for piece in range(pieces):
        down_pieces.append(
            jnp.concatenate(
                [
                    down[
                        owner * share * pieces + piece * share : owner * share * pieces
                        + (piece + 1) * share,
                        :,
                    ]
                    for owner in range(owners)
                ],
                0,
            )
        )
    sums = [jnp.sum(gsmall[8 * i : 8 * i + 8, :], 0, keepdims=True) for i in range(4)]
    bias_row = jnp.sum(gbias[...], 0, keepdims=True)
    block = jnp.concatenate(
        sums + [bias_row[:, i * features : (i + 1) * features] for i in range(pieces)], 0
    )
    block = jnp.concatenate([block, jnp.zeros((share - 8, features), f32)], 0)
    small = jnp.concatenate([block] * owners, 0)
    block_scr[...] = jnp.zeros_like(block_scr)
    stack_blocks(jnp.concatenate([proj, gup[...]] + down_pieces + [small], 1), block_scr)
    split_owners(block_scr, mine_ref, theirs_ref, (0, 4, 2, 6))


SMALL_ROWS = 168
DENSE_ROWS = 128
LATE_ROWS = 128


def back_attend_kernel(
    head, qunit_ref, qscale_ref, kvraw_ref, soft_ref, gatt_ref, key_ref, val_ref,
    gain_scr, table_ref,
    gpadded, gkeypad, sums_ref,
    keyaug_scr, gtable, gkey, gval, gsums,
):
    cols = gpadded.shape[1] - 16
    rows = gpadded.shape[0] - 2
    tile = BACK_ROWS * cols
    chunks = rows // BACK_ROWS
    key_cols = cols // 2
    key_rows = rows // 2
    key_total = kvraw_ref.shape[1]
    clear_rim(gpadded)
    gkeypad[...] = jnp.zeros_like(gkeypad)
    table = table_ref[...]
    gsums[...] = jnp.zeros_like(gsums)

    key_place = lax.broadcasted_iota(jnp.int32, (key_total, LANES), 0)
    lanes = lane_ids((key_total, LANES))
    hot = (
        (lanes == 30 - 2 * (key_place // key_cols)) | (lanes == 94 - 2 * (key_place % key_cols))
    ).astype(bf16)
    keyaug_scr[:, 0:LANES] = key_ref[head]
    keyaug_scr[:, LANES : 2 * LANES] = hot

    scale_factor = HEAD_DIM ** (-0.5)
    tile_mask = head_mask(tile)
    row_lanes = lane_ids((cols, LANES))

    def attend(step, carry):
        span = pl.ds(pl.multiple_of(step * tile, tile), tile)
        unit, scale = qunit_ref[head, span, :], qscale_ref[head, span, :]
        query = (unit * gain_scr[0:1, :] + gain_scr[3:4, :]).astype(bf16)
        gatt = gatt_ref[span, head * LANES : (head + 1) * LANES]
        soft_low = soft_ref[head, span, :]
        soft = soft_low.astype(f32)
        gsoft = dot(gatt, val_ref[head], NT)
        inner = jnp.sum(soft * gsoft, -1, keepdims=True)
        gscore = (soft * (gsoft - inner)).astype(bf16)
        gkey[...] = dot(query, gscore, TN)
        gval[...] = dot(gatt, soft_low, TN)
        wide = dot(gscore, keyaug_scr[...])
        gterm = wide[:, LANES : 2 * LANES]
        pieces = []
        for row in range(BACK_ROWS):
            part = gterm[row * cols : (row + 1) * cols, :]
            place = step * BACK_ROWS + row
            by_row = pltpu.roll(part, place, 1)
            by_col = pltpu.roll(part, 0, 1, stride=1, stride_axis=0)
            pieces.append(jnp.where(row_lanes < 64, by_row, by_col))
        glook = jnp.concatenate(pieces, 0).astype(bf16)
        gtable[...] = dot(glook, query, TN)
        gquery = scale_factor * wide[:, 0:LANES] + gatt.astype(f32) + dot(glook, table)
        gsums[0:8, :] = fold_rows(gquery * unit)
        gsums[8:16, :] = fold_rows(gquery)
        graw = norm_back(gquery * gain_scr[0:1, :], unit, scale, HEAD_DIM) * tile_mask
        gpadded[pl.ds(1 + step * BACK_ROWS, BACK_ROWS), 8 : 8 + cols, :] = graw.reshape(
            BACK_ROWS, cols, LANES
        )
        return carry

    lax.fori_loop(0, chunks, attend, 0, unroll=True)

    key_mask = head_mask(key_total)
    for member, grad in ((1, gkey[...].T * scale_factor), (2, gval[...].T)):
        unit, scale = head_norm_parts(kvraw_ref[(member - 1) * HEADS + head], key_mask)
        base = 16 if member == 1 else 24
        gsums[base : base + 8, :] += fold_rows(grad * unit)
        if member == 2:
            gsums[32:40, :] += fold_rows(grad)
        graw = norm_back(grad * gain_scr[member : member + 1, :], unit, scale, HEAD_DIM) * key_mask
        gkeypad[member - 1, 0:key_rows, 0:key_cols, :] = graw.reshape(key_rows, key_cols, LANES)

    sums_ref[...] = jnp.zeros_like(sums_ref)
    sums_ref[0:63, :] = gtable[0:63, :]
    sums_ref[63:126, :] = gtable[64:127, :]
    for place, base in enumerate((0, 16, 24, 8, 32)):
        sums_ref[126 + place : 127 + place, :] = jnp.sum(gsums[base : base + 8, :], 0, keepdims=True)


def back_weights_kernel(
    norm_ref, padded, gpadded_0, gpadded_1, gkeypad_0, gkeypad_1, sums_0, sums_1, weight_ref, columns_ref, kern_scr,
    gmix_scr, mine_ref, theirs_ref,
    gmixrow, gkern, gweight, gbias, small_scr, dense_scr, block_scr,
):
    tokens, features = norm_ref.shape
    cols = padded.shape[2] - 16
    rows = padded.shape[1] - 2
    tile = CHUNK_ROWS * cols
    chunks = rows // CHUNK_ROWS
    key_cols = cols // 2
    key_rows = rows // 2
    gkern[...] = jnp.zeros_like(gkern)

    def spread_queries(step, carry):
        span = pl.ds(pl.multiple_of(step * tile, tile), tile)
        around = pl.ds(step * CHUNK_ROWS, CHUNK_ROWS + 2)
        for head, gpadded in enumerate((gpadded_0, gpadded_1)):
            total = jnp.zeros((CHUNK_ROWS, cols, LANES), f32)
            own = gpadded[pl.ds(1 + step * CHUNK_ROWS, CHUNK_ROWS), 8 : 8 + cols, :]
            for side in range(3):
                window = gpadded[around, 9 - side : 9 - side + cols, :]
                cells = padded[head, around, 7 + side : 7 + side + cols, :]
                for up in range(3):
                    tap = 3 * up + side
                    total = total + window[2 - up : 2 - up + CHUNK_ROWS] * kern_scr[tap, 0:1, :]
                    gkern[tap] += fold_rows((own * cells[up : up + CHUNK_ROWS]).reshape(tile, LANES))
            flat = total.reshape(tile, LANES).astype(bf16)
            gmix_scr[span, head * LANES : (head + 1) * LANES] = flat
        return carry

    lax.fori_loop(0, chunks, spread_queries, 0, unroll=True)

    evens = pl.ds(0, key_cols, stride=2)
    odds = pl.ds(1, key_cols, stride=2)
    for place in range(2 * HEADS):
        member = 1 + place // HEADS
        taps = [kern_scr[tap, member : member + 1, :] for tap in range(9)]
        gkeypad = (gkeypad_0, gkeypad_1)[place % HEADS].at[place // HEADS]
        left = gkeypad[0 : key_rows + 1, 0:key_cols, :]
        right = gkeypad[0 : key_rows + 1, 1 : 1 + key_cols, :]
        here, below, beside, cross = left[:key_rows], left[1:], right[:key_rows], right[1:]
        gmixrow[:, 0, evens, :] = here * taps[4]
        gmixrow[:, 0, odds, :] = beside * taps[3] + here * taps[5]
        gmixrow[:, 1, evens, :] = below * taps[1] + here * taps[7]
        gmixrow[:, 1, odds, :] = (
            cross * taps[0] + below * taps[2] + beside * taps[6] + here * taps[8]
        )
        lane = (HEADS + place) * LANES
        gmix_scr[:, lane : lane + LANES] = gmixrow[...].reshape(rows * cols, LANES).astype(bf16)
        for side in range(3):
            for up, cells in enumerate(stride_windows(padded, HEADS + place, side, key_rows, key_cols)):
                gkern[9 * member + 3 * up + side] += fold_rows(
                    (here * cells).reshape(key_rows * key_cols, LANES)
                )

    def weigh(step, carry):
        span = pl.ds(pl.multiple_of(step * WEIGH_TILE, WEIGH_TILE), WEIGH_TILE)
        gmix = gmix_scr[span, :]
        gweight[...] = dot(norm_ref[span, :].astype(bf16), gmix, TN)
        gbias[...] = fold_rows(gmix.astype(f32))
        return carry

    lax.fori_loop(0, tokens // WEIGH_TILE, weigh, 0, unroll=True)

    bias_row = jnp.sum(gbias[...], 0, keepdims=True)
    weight = weight_ref[...].astype(f32)
    raw = gweight[...]
    lanes = lane_ids((features, LANES))
    norm_sums = jnp.where(
        lanes == 0,
        jnp.sum(weight * raw, 1, keepdims=True),
        jnp.where(lanes == 1, jnp.sum(weight * bias_row, 1, keepdims=True), 0.0),
    )
    norm_rows = jnp.concatenate([norm_sums, jnp.zeros((2 * LANES - features, LANES), f32)], 0).T
    gweight[...] = raw * columns_ref[0:features, 16:17] + columns_ref[0:features, 0:1] * bias_row

    for tap in range(27):
        row = 3 * (tap % 9) + tap // 9
        small_scr[row : row + 1, :] = jnp.sum(gkern[tap], 0, keepdims=True)
    small_scr[27:158, :] = sums_0[0:131, :] + sums_1[0:131, :]
    for place in range(3 * HEADS):
        small_scr[158 + place : 159 + place, :] = bias_row[:, place * LANES : (place + 1) * LANES]
    for place in range(2):
        for head in range(HEADS):
            at = 164 + HEADS * place + head
            small_scr[at : at + 1, :] = head_piece(norm_rows[place : place + 1, :], head * HEAD_DIM)
    weights = jnp.concatenate(
        [gweight[:, place * LANES : place * LANES + HEAD_DIM] for place in range(3 * HEADS)]
        + [jnp.zeros((features, 64), f32)],
        1,
    )
    block_scr[...] = jnp.zeros_like(block_scr)
    stack_blocks(weights, block_scr)
    split_owners(block_scr, mine_ref, theirs_ref, (0, 2, 4, 6))
    count = block_scr.shape[1]
    dense_scr[...] = jnp.zeros_like(dense_scr)
    dense_scr[0:126, :] = small_scr[0:126, :] * head_mask(126)
    beside = lane_ids((42, LANES)) >= HEAD_DIM
    for piece in range(3):
        moved = small_scr[126:168, :]
        moved = pltpu.roll(moved, HEAD_DIM - 32 * piece, 1)
        dense_scr[42 * piece : 42 * (piece + 1), :] += jnp.where(beside, moved, 0.0)
    small = dense_scr[...].astype(bf16)
    mine_ref[4 * count :, :] = small
    theirs_ref[4 * count :, :] = small


def back_images_kernel(norm_ref, scale_ref, gmix_ref, gmid_ref, weight_ref, rows_ref, gimg_ref):
    tokens, features = norm_ref.shape
    tile = IMAGE_TILE
    block = tokens // 4
    gain_one = rows_ref[16:17, 0:features]

    def finish(step, carry):
        span = pl.ds(pl.multiple_of(step * tile, tile), tile)
        unit, scale = norm_ref[span, :], scale_ref[span, :]
        gnorm = dot(gmix_ref[span, :], weight_ref[...], NT)
        gimg = gmid_ref[span, :].astype(f32) + norm_back(gnorm * gain_one, unit, scale, features)
        for place in range(tile // block):
            gimg_ref[step * (tile // block) + place] = fold_block(
                gimg[place * block : (place + 1) * block, :]
            )
        return carry

    lax.fori_loop(0, tokens // tile, finish, 0, unroll=True)


def halve_kernel(mine_ref, got_ref, keep_ref, send_ref):
    half = keep_ref.shape[0]
    total = (mine_ref[...].astype(f32) + got_ref[...].astype(f32)).astype(bf16)
    keep_ref[...] = total[:half]
    send_ref[...] = total[half:]


def pair_kernel(shared, mine_ref, got_ref, own_ref, msg_1, msg_2, msg_3):
    total = (mine_ref[...].astype(f32) + got_ref[...].astype(f32)).astype(bf16)
    count = (total.shape[0] - shared) // 4
    for place, out in enumerate((own_ref, msg_1, msg_2, msg_3)):
        out[0:count, :] = total[place * count : (place + 1) * count]
        if shared:
            out[count:, :] = total[4 * count :]


def chips_sum(own_ref, got_1, got_2, got_3):
    return (own_ref[...].astype(f32) + got_1[...].astype(f32)) + (
        got_2[...].astype(f32) + got_3[...].astype(f32)
    )


def two_kernel(own_ref, got_ref, out_ref):
    out_ref[...] = (own_ref[...].astype(f32) + got_ref[...].astype(f32)).astype(bf16)


def four_kernel(own_ref, got_1, got_2, got_3, out_ref):
    out_ref[...] = chips_sum(own_ref, got_1, got_2, got_3).astype(bf16)


def pictures_kernel(out_0, out_1, out_2, out_3, gimg_low, out_ref, gimg_ref):
    for shift in range(4):
        gimg_ref[shift] = unfold_block(gimg_low[shift]).astype(f32)
        block = (out_0, out_1, out_2, out_3)[shift][...]
        out_ref[turned(4 - shift)] = unfold_block(block)


def finish_kernel(
    early_0, early_1, late_0, late_1,
    gqkv_ref, gproj_ref, gup_ref, gdown_ref, ggain_ref, gshift_ref, gkern_ref,
    gpgain_ref, gpshift_ref, grelh_ref, grelw_ref,
    small_scr, dense_scr,
):
    share, features = gproj_ref.shape
    hidden = gup_ref.shape[1]
    pieces = hidden // features
    early = early_0[...].astype(f32) + early_1[...].astype(f32)
    early = jnp.concatenate(
        [early[share * i : share * (i + 1), :] for i in range((2 * features + 2 * hidden) // LANES)], 1
    )
    gproj_ref[...] = early[:, 0:features]
    gup_ref[...] = early[:, features : features + hidden]
    for piece in range(pieces):
        start = features + hidden + piece * features
        gdown_ref[piece * share : (piece + 1) * share, :] = early[:, start : start + features]
    start = features + 2 * hidden
    block = early[0:8, start : start + features]
    late = late_0[...].astype(f32) + late_1[...].astype(f32)
    gqkv_ref[...] = jnp.concatenate([late[share * i : share * (i + 1), :] for i in range(5)], 1)[
        :, 0 : 3 * features
    ]
    dense = late[LATE_ROWS : LATE_ROWS + DENSE_ROWS, :]
    small_scr[0:126, :] = dense[0:126, :]
    dense_scr[...] = dense
    lanes = lane_ids((42, LANES))
    rest = jnp.zeros((42, LANES), f32)
    for piece in range(3):
        moved = pltpu.roll(dense_scr[42 * piece : 42 * (piece + 1), :], 32 + 32 * piece, 1)
        rest = jnp.where((lanes >= 32 * piece) & (lanes < 32 * piece + 32), moved, rest)
    small_scr[126:168, :] = rest
    for tap in range(9):
        gkern_ref[tap] = small_scr[3 * tap : 3 * tap + 3, 0:HEAD_DIM]
    gpgain_ref[...] = small_scr[153:156, 0:HEAD_DIM]
    gpshift_ref[...] = small_scr[156:158, 0:HEAD_DIM]
    grelh_ref[...] = small_scr[27:90, 0:HEAD_DIM]
    grelw_ref[...] = small_scr[90:153, 0:HEAD_DIM]
    ggain_ref[1:2, :] = block[0:1, :]
    gshift_ref[1:2, :] = block[1:2, :]
    for head in range(HEADS):
        lanes = slice(head * HEAD_DIM, (head + 1) * HEAD_DIM)
        ggain_ref[0:1, lanes] = small_scr[164 + head : 165 + head, 0:HEAD_DIM]
        gshift_ref[0:1, lanes] = small_scr[166 + head : 167 + head, 0:HEAD_DIM]
        for section in range(3):
            row = 158 + section * HEADS + head
            gshift_ref[2 + section : 3 + section, lanes] = small_scr[row : row + 1, 0:HEAD_DIM]
    gshift_ref[5:6, :] = block[2:3, :]
    gshift_ref[6 : 6 + pieces, :] = block[4 : 4 + pieces, :]
    gshift_ref[6 + pieces : 7 + pieces, :] = block[3:4, :]


LONG = {"back_attend_1": 2 * 10**10}


def call(kernel, name, outs, scratch, flops, limit, spaces, out_spaces, *args):
    place = {"v": pltpu.VMEM, "p": pltpu.VMEM, "h": pltpu.HBM, "a": pl.ANY}
    keep = {"p": pltpu.VMEM, "h": pltpu.HBM}
    args = [
        pltpu.with_memory_space_constraint(a, keep[c]) if c in keep else a for c, a in zip(spaces, args)
    ]
    outs = [keep[c](o.shape, o.dtype) if c in keep else o for c, o in zip(out_spaces, outs)]
    return pl.pallas_call(
        kernel,
        name=name,
        out_shape=outs,
        in_specs=[pl.BlockSpec(memory_space=place[c]) for c in spaces],
        out_specs=[pl.BlockSpec(memory_space=place[c]) for c in out_spaces],
        scratch_shapes=scratch,
        cost_estimate=pl.CostEstimate(flops=LONG.get(name, 1), bytes_accessed=LONG.get(name, 1) // 500, transcendentals=0),
        compiler_params=pltpu.CompilerParams(vmem_limit_bytes=limit * 2**20),
    )(*args)


KA_LIMIT = 36


def whole_image(
    images,
    w_qkv,
    w_proj,
    w_up,
    w_down,
    gains_main,
    shifts_main,
    pool_kernels,
    pool_gains,
    pool_shifts,
    rel_height,
    rel_width,
    cotangent,
):
    owners = lax.axis_size("batch")
    cycle = lax.axis_size("rows")
    image_count, row_count, cols, features = images.shape
    rows = row_count * cycle
    tokens = rows * cols
    hidden = w_up.shape[1]
    share = w_proj.shape[0]
    pieces = hidden // features
    key_total = tokens // 4
    early_used = (2 * features + 2 * hidden) // LANES * share
    early_rows = -(-early_used // 16) * 16
    def shaped(shape, dtype):
        return jax.ShapeDtypeStruct(shape, dtype)

    block = tokens // cycle
    folded = (block * features // LANES, LANES)
    width = 4 * features + 2 * hidden

    def send_on(pieces):
        return list(pieces[:1]) + [
            lax.ppermute(pieces[k], "rows", [(i, (i + k) % cycle) for i in range(cycle)])
            for k in range(1, cycle)
        ]

    def trade(cells, flip):
        return lax.ppermute(cells, "batch", [(i, i ^ flip) for i in range(owners)])

    img = call(
        fold_images_kernel,
        "fold_images",
        [shaped((cycle,) + folded, bf16)],
        [pltpu.VMEM((cycle, block, features), bf16), pltpu.SemaphoreType.DMA((4,))],
        1,
        4,
        "h",
        "v",
        images.reshape(cycle, block, features),
    )[0]
    img, w_qkv = lax.optimization_barrier((img, w_qkv))
    img = lax.all_to_all(img, "rows", 0, 0, tiled=True)
    packed = call(
        pack_kernel,
        "pack",
        [shaped((share, width), bf16)],
        [pltpu.VMEM(w.shape, bf16) for w in (w_qkv, w_proj, w_up, w_down)]
        + [pltpu.SemaphoreType.DMA((4,))],
        10**6,
        4,
        "hhhh",
        "v",
        w_qkv, w_proj, w_up, w_down,
    )[0]
    packed, cotangent = lax.optimization_barrier((packed, cotangent))
    cot_pieces = call(
        fold_kernel,
        "fold",
        [shaped(folded, bf16)] * cycle,
        [
            pltpu.VMEM((cycle, block, features), bf16),
            pltpu.VMEM((cycle,) + folded, bf16),
            pltpu.SemaphoreType.DMA((4,)),
            pltpu.SemaphoreType.DMA((4,)),
        ],
        10**6,
        8,
        "h",
        "a" * 4,
        cotangent.reshape(cycle, block, features),
    )
    img, cot_pieces, *shards = lax.optimization_barrier(
        (img, cot_pieces, *[trade(packed, flip) for flip in (2, 4, 6)])
    )
    own = jnp.stack([packed, *shards])
    other = trade(own, 1)
    taps = pool_kernels.transpose(1, 0, 2)
    small = (gains_main, shifts_main, taps, pool_gains, pool_shifts, rel_height, rel_width)
    wide, full_proj, full_up, full_down, biases, lines, columns, taps_wide, pool_lines, ahead, behind = call(
        functools.partial(weights_kernel, owners),
        "weights",
        [
            shaped((features, 3 * HEADS * LANES), bf16),
            shaped((HEADS * LANES, features), bf16),
            shaped((features, hidden), bf16),
            shaped((hidden, features), bf16),
            shaped((8, hidden), f32),
            shaped((24, 2 * LANES), f32),
            shaped((2 * LANES, LANES), f32),
            shaped((9, 8, LANES), f32),
            shaped((8, LANES), f32),
            shaped((LANES, LANES), bf16),
            shaped((LANES, LANES), bf16),
        ],
        [pltpu.VMEM((features, width), f32), pltpu.VMEM((hidden, features), f32)]
        + [pltpu.VMEM(a.shape, bf16) for a in small]
        + [pltpu.VMEM((LANES, LANES), f32), pltpu.SemaphoreType.DMA((7,))],
        10**6,
        12,
        "vv" + "h" * 7,
        "v" * 11,
        own, other, *small,
    )
    cot_pieces = send_on(cot_pieces)
    whole = [
        shaped((3 * HEADS, rows + 2, cols + 16, LANES), f32),
        shaped((HEADS, tokens, LANES), f32),
        shaped((HEADS, tokens, LANES), f32),
        shaped((2 * HEADS, key_total, LANES), f32),
        shaped((HEADS, tokens, key_total), bf16),
        shaped((tokens, HEADS * LANES), bf16),
    ]
    img, norm_one, scale_one, padded, qunit, qscale, kvraw, soft, att, keys, values = call(
        attend_kernel,
        "attend",
        [
            shaped((tokens, features), bf16),
            shaped((tokens, features), f32),
            shaped((tokens, features), f32),
        ]
        + whole + [shaped((HEADS, key_total, LANES), bf16)] * 2,
        [
            pltpu.VMEM((HEADS, tokens, LANES), bf16),
            pltpu.VMEM((HEADS, key_total, 2 * LANES), bf16),
        ],
        10**10,
        KA_LIMIT,
        "v" * 7,
        "p" * 11,
        img, wide, biases, lines, taps_wide, pool_lines, ahead,
    )
    *out_pieces, normed, unit, scale, active, slope = call(
        feed_ahead_kernel,
        "feed_ahead",
        [shaped(folded, bf16)] * cycle
        + [
            shaped((tokens, features), bf16),
            shaped((tokens, features), f32),
            shaped((tokens, features), f32),
            shaped((tokens, hidden), bf16),
            shaped((tokens, hidden), f32),
        ],
        [pltpu.VMEM((cycle,) + folded, bf16), pltpu.SemaphoreType.DMA((4,))],
        1,
        36,
        "pp" + "v" * 5,
        "a" * cycle + "p" * 5,
        img, att, full_proj, full_up, full_down, biases, lines,
    )
    gmid, gatt, mine, theirs = call(
        functools.partial(feed_back_kernel, owners),
        "feed_back",
        [shaped((tokens, features), bf16), shaped((tokens, HEADS * LANES), bf16)]
        + [shaped((4 * early_rows, LANES), bf16)] * 2,
        [
            pltpu.VMEM((features, hidden), f32),
            pltpu.VMEM((features, hidden), f32),
            pltpu.VMEM((HEADS * LANES, features), f32),
            pltpu.VMEM((8, hidden), f32),
            pltpu.VMEM((32, features), f32),
            pltpu.VMEM((owners, early_rows, LANES), f32),
            pltpu.VMEM((cycle,) + folded, bf16),
            pltpu.SemaphoreType.DMA((4,)),
        ],
        1,
        36,
        "p" + "a" * 4 + "p" * 5 + "v" * 4,
        "pp" + "vv",
        att, *cot_pieces, normed, unit, scale, active, slope, full_proj, full_up, full_down, lines,
    )

    def halved(mine, got):
        return call(
            halve_kernel,
            "halve",
            [shaped((mine.shape[0] // 2, LANES), bf16)] * 2,
            [],
            10**6,
            4,
            "vv",
            "vv",
            mine, got,
        )

    got = trade(theirs, 1)

    def back_attend(head, behind):
        return call(
            functools.partial(back_attend_kernel, head),
            f"back_attend_{head}",
            [
                shaped((rows + 2, cols + 16, LANES), f32),
                shaped((2, rows // 2 + 1, cols // 2 + 8, LANES), f32),
                shaped((136, LANES), f32),
            ],
            [
                pltpu.VMEM((key_total, 2 * LANES), bf16),
                pltpu.VMEM((LANES, LANES), f32),
                pltpu.VMEM((LANES, key_total), f32),
                pltpu.VMEM((LANES, key_total), f32),
                pltpu.VMEM((40, LANES), f32),
            ],
            10**10,
            30,
            "p" * 7 + "vv",
            "ppp",
            qunit, qscale, kvraw, soft, gatt, keys, values, pool_lines, behind,
        )

    gpadded_0, gkeypad_0, sums_0 = back_attend(0, behind)
    got, gkeypad_0, behind = lax.optimization_barrier((got, gkeypad_0, behind))
    early, away = halved(mine, got)
    away = trade(away, 2)
    out_pieces = send_on(out_pieces)
    gpadded_1, gkeypad_1, sums_1 = back_attend(1, behind)
    gmix, mine, theirs = call(
        back_weights_kernel,
        "back_weights",
        [shaped((tokens, 3 * HEADS * LANES), bf16)]
        + [shaped((4 * LATE_ROWS + DENSE_ROWS, LANES), bf16)] * 2,
        [
            pltpu.VMEM((rows // 2, 2, cols, LANES), f32),
            pltpu.VMEM((27, 8, LANES), f32),
            pltpu.VMEM((features, 3 * HEADS * LANES), f32),
            pltpu.VMEM((8, 3 * HEADS * LANES), f32),
            pltpu.VMEM((SMALL_ROWS, LANES), f32),
            pltpu.VMEM((DENSE_ROWS, LANES), f32),
            pltpu.VMEM((owners, LATE_ROWS, LANES), f32),
        ],
        10**10,
        30,
        "p" + "p" * 7 + "v" * 3,
        "pvv",
        norm_one, padded, gpadded_0, gpadded_1, gkeypad_0, gkeypad_1, sums_0, sums_1, wide, columns, taps_wide,
    )

    def summed(kernel, *pieces):
        return call(
            kernel,
            "sum_four" if len(pieces) == 4 else "sum_two",
            [shaped(pieces[0].shape, bf16)],
            [],
            1,
            4,
            "v" * len(pieces),
            "v",
            *pieces,
        )[0]

    def ring_trade(cells, flip):
        return lax.ppermute(cells, "rows", [(i, i ^ flip) for i in range(cycle)])

    away, out_pieces, gmix, mine, theirs = lax.optimization_barrier(
        (away, out_pieces, gmix, mine, theirs)
    )
    early, away = halved(early, away)
    away = trade(away, 4)
    got = trade(theirs, 1)
    gimg = call(
        back_images_kernel,
        "back_images",
        [shaped((cycle,) + folded, bf16)],
        [],
        10**10,
        24,
        "ppppvv",
        "v",
        norm_one, scale_one, gmix, gmid, wide, lines,
    )[0]
    got, gimg = lax.optimization_barrier((got, gimg))
    gimg = lax.all_to_all(gimg, "rows", 0, 0, tiled=True)
    early = summed(two_kernel, early, away)
    early = summed(two_kernel, early, ring_trade(early, 1))
    away = ring_trade(early, 2)
    own, *apart = call(
        functools.partial(pair_kernel, DENSE_ROWS),
        "pair",
        [shaped((LATE_ROWS + DENSE_ROWS, LANES), bf16)] * 4,
        [],
        10**6,
        4,
        "vv",
        "vvvv",
        mine, got,
    )
    late = summed(four_kernel, own, *[trade(apart[k], 2 * k + 2) for k in range(3)])
    late = summed(two_kernel, late, ring_trade(late, 1))
    late_away = ring_trade(late, 2)
    output, grad_images = call(
        pictures_kernel,
        "pictures",
        [shaped((cycle, block, features), bf16), shaped((cycle, block, features), f32)],
        [],
        1,
        16,
        "v" * 5,
        "v" * 2,
        *out_pieces, gimg,
    )
    late, output, grad_images = lax.optimization_barrier((late, output, grad_images))
    grads = call(
        finish_kernel,
        "finish",
        [
            shaped((share, 3 * features), f32),
            shaped((share, features), f32),
            shaped((share, hidden), f32),
            shaped((share * pieces, features), f32),
            shaped(gains_main.shape, f32),
            shaped(shifts_main.shape, f32),
            shaped(taps.shape, f32),
            shaped(pool_gains.shape, f32),
            shaped(pool_shifts.shape, f32),
            shaped(rel_height.shape, f32),
            shaped(rel_width.shape, f32),
        ],
        [pltpu.VMEM((SMALL_ROWS, LANES), f32), pltpu.VMEM((DENSE_ROWS, LANES), f32)],
        10**8,
        16,
        "v" * 4,
        "v" * 11,
        early, away, late, late_away,
    )
    grads = list(grads)
    grads[6] = grads[6].transpose(1, 0, 2)
    return (output.reshape(images.shape), grad_images.reshape(images.shape), *grads)

def per_device(images, *rest):
    cycle = lax.axis_size("rows")
    image_count, row_count, cols, _ = images.shape
    fits = image_count == cycle and row_count * cycle == 32 and cols == 32
    return whole_image(images, *rest) if fits else row_sharded(images, *rest)


def solution(mesh):
    return jax.shard_map(
        per_device,
        mesh=mesh,
        in_specs=(
            P("batch", "rows", None, None),
            P("batch", None),
            P("batch", None),
            P("batch", None),
            P("batch", None),
            P(),
            P(),
            P(),
            P(),
            P(),
            P(),
            P(),
            P("batch", "rows", None, None),
        ),
        out_specs=(
            P("batch", "rows", None, None),
            P("batch", "rows", None, None),
            P("batch", None),
            P("batch", None),
            P("batch", None),
            P("batch", None),
            P(),
            P(),
            P(),
            P(),
            P(),
            P(),
            P(),
        ),
        check_vma=False,
    )
```

```python
import functools

import jax
import jax.numpy as jnp
from jax import lax
from jax.experimental import pallas as pl
from jax.experimental.pallas import tpu as pltpu
from jax.sharding import PartitionSpec as P

HEADS = 2
HEAD_DIM = 96


norm_eps = 1e-06
highest = lax.Precision.HIGHEST


def padded(cells, sides, width):
    for axis, dim in sides:
        count = lax.axis_size(axis)
        ends = count - 1
        head = lax.slice_in_dim(cells, 0, width, axis=dim)
        tail = lax.slice_in_dim(cells, cells.shape[dim] - width, cells.shape[dim], axis=dim)
        cells = jnp.concatenate(
            [
                lax.ppermute(tail, axis, [(i, (i + 1) % count) for i in range(ends)]),
                cells,
                lax.ppermute(head, axis, [((i + 1) % count, i) for i in range(ends)]),
            ],
            axis=dim,
        )
    return cells


def layer_norm(values, gains, shifts):
    centre = jnp.mean(values, -1, keepdims=True)
    centred = values - centre
    spread = jnp.mean(centred * centred, -1, keepdims=True)
    return centred * lax.rsqrt(spread + norm_eps) * gains + shifts


def gelu_tanh(values):
    return jax.nn.gelu(values, approximate=True)


def pool_section(section, kernel, stride):
    image_count, ext_rows, col_count, features = section.shape
    out_rows = (ext_rows - 2) // stride
    out_cols = col_count // stride
    col_out = jnp.arange(out_cols)[:, None] * stride
    col_in = jnp.arange(col_count)[None, :]
    shifted = []
    for offset_col in range(3):
        picker = (col_out + offset_col - 1 == col_in).astype(jnp.float32)
        shifted.append(jnp.einsum("jy,bxyc->bxjc", picker, section, precision=highest))
    summed = jnp.zeros((image_count, out_rows, out_cols, features), jnp.float32)
    for offset_row in range(3):
        for offset_col in range(3):
            window = shifted[offset_col][:, offset_row : offset_row + ext_rows - 2]
            if stride == 2:
                window = window.reshape(image_count, out_rows, 2, out_cols, features)[:, :, 0]
            summed = summed + window * kernel[3 * offset_row + offset_col]
    return summed


def pooled_local(extended_f, kernels, gains, shifts):
    features = extended_f.shape[-1]
    head_dim = kernels.shape[-1]
    head_count = features // head_dim
    results = []
    for member, stride in ((0, 1), (1, 2), (2, 2)):
        pooled = pool_section(
            extended_f[member], jnp.tile(kernels[member], (1, head_count)), stride
        )
        pooled = pooled.reshape(pooled.shape[:-1] + (head_count, head_dim))
        offset = (
            shifts[0] if member == 0 else shifts[1] if member == 2 else jnp.zeros_like(shifts[0])
        )
        results.append(layer_norm(pooled, gains[member], offset))
    return tuple(results)


def row_sharded(
    images,
    w_qkv,
    w_proj,
    w_up,
    w_down,
    gains_main,
    shifts_main,
    pool_kernels,
    pool_gains,
    pool_shifts,
    rel_height,
    rel_width,
    cotangent,
):
    image_count, row_count, col_count, features = images.shape
    head_dim = HEAD_DIM
    head_count = HEADS
    scale_factor = head_dim ** (-0.5)
    cycle_size = lax.axis_size("rows")
    key_rows_all = row_count * cycle_size // 2
    key_cols = col_count // 2
    key_total = key_rows_all * key_cols
    query_count = row_count * col_count
    key_local = row_count // 2 * key_cols
    gain_rows = gains_main.astype(jnp.float32)
    shift_rows = shifts_main.astype(jnp.float32)
    full_qkv, full_proj, full_up, full_down = (
        lax.all_gather(w_qkv, "batch", axis=0, tiled=True),
        lax.all_gather(w_proj, "batch", axis=0, tiled=True),
        lax.all_gather(w_up, "batch", axis=0, tiled=True),
        lax.all_gather(w_down, "batch", axis=0, tiled=True),
    )
    qkv_split = full_qkv.reshape(features, 3, features)
    inputs_f = images.astype(jnp.float32)
    normed_one, norm_one_pullback = jax.vjp(layer_norm, inputs_f, gain_rows[0], shift_rows[0])
    normed_low = normed_one.astype(jnp.bfloat16)
    mixed = (
        jnp.einsum("bxyd,dme->mbxye", normed_low, qkv_split, preferred_element_type=jnp.float32)
        + shift_rows[2:5][:, None, None, None, :]
    )
    mixed_low = mixed.astype(jnp.bfloat16)
    extended = padded(mixed_low, (("rows", 2),), 1)
    (queries, keys_pooled, values_pooled), pool_pullback = jax.vjp(
        pooled_local,
        extended.astype(jnp.float32),
        pool_kernels.astype(jnp.float32),
        pool_gains.astype(jnp.float32),
        pool_shifts.astype(jnp.float32),
    )
    queries_low = queries.astype(jnp.bfloat16)
    query_flat = queries_low.reshape(image_count, query_count, head_count, head_dim)
    keys_low = keys_pooled.astype(jnp.bfloat16).reshape(image_count, key_local, features)
    values_low = values_pooled.astype(jnp.bfloat16).reshape(image_count, key_local, features)
    key_value = jnp.concatenate([keys_low, values_low], -1)
    first_row = lax.axis_index("rows") * row_count

    def rel_terms(query_vals, table_height, table_width):
        row_place = first_row + jnp.arange(row_count)
        dist_height = (
            row_place[:, None] - 2 * jnp.arange(key_rows_all)[None, :] + 2 * (key_rows_all - 1)
        )
        pick_height = (
            dist_height[:, :, None] == jnp.arange(table_height.shape[0])[None, None, :]
        ).astype(jnp.float32)
        lookup_height = jnp.einsum("xjt,tc->xjc", pick_height, table_height, precision=highest)
        dist_width = (
            jnp.arange(col_count)[:, None] - 2 * jnp.arange(key_cols)[None, :] + 2 * (key_cols - 1)
        )
        pick_width = (
            dist_width[:, :, None] == jnp.arange(table_width.shape[0])[None, None, :]
        ).astype(jnp.float32)
        lookup_width = jnp.einsum("yjt,tc->yjc", pick_width, table_width, precision=highest)
        term_height = jnp.einsum("bxyhc,xjc->bhxyj", query_vals, lookup_height, precision=highest)
        term_width = jnp.einsum("bxyhc,yjc->bhxyj", query_vals, lookup_width, precision=highest)
        return (term_height, term_width)

    (term_height, term_width), rel_pullback = jax.vjp(
        rel_terms,
        queries_low.astype(jnp.float32),
        rel_height.astype(jnp.float32),
        rel_width.astype(jnp.float32),
    )
    rel_full = (term_height[..., :, None] + term_width[..., None, :]).reshape(
        image_count, head_count, query_count, key_total
    )

    def key_scores(key_piece):
        piece_rows = key_piece.shape[1]
        keys_part = key_piece[..., :features].reshape(image_count, piece_rows, head_count, head_dim)
        products = jnp.einsum(
            "bqhc,bkhc->bhqk", query_flat, keys_part, preferred_element_type=jnp.float32
        )
        return products * scale_factor + lax.slice_in_dim(rel_full, 0, piece_rows, axis=3)

    key_piece = lax.all_gather(key_value, "rows", axis=1, tiled=True)
    run_max = jnp.full((image_count, head_count, query_count), -1e30, jnp.float32)
    run_sum = jnp.zeros((image_count, head_count, query_count), jnp.float32)
    run_acc = jnp.zeros((image_count, head_count, query_count, head_dim), jnp.float32)
    piece_rows = key_piece.shape[1]
    values_part = key_piece[..., features:].reshape(image_count, piece_rows, head_count, head_dim)
    scores = key_scores(key_piece)
    new_max = jnp.maximum(run_max, jnp.max(scores, -1))
    weights_exp = jnp.exp(scores - new_max[..., None])
    factor = jnp.exp(run_max - new_max)
    run_sum = run_sum * factor + jnp.sum(weights_exp, -1)
    run_acc = run_acc * factor[..., None] + jnp.einsum(
        "bhqk,bkhc->bhqc", weights_exp, values_part.astype(jnp.float32), precision=highest
    )
    run_max, run_sum, run_acc = (new_max, run_sum, run_acc)
    log_total = run_max + jnp.log(run_sum)
    attended = (run_acc / run_sum[..., None]).transpose(0, 2, 1, 3) + query_flat.astype(jnp.float32)
    attended_low = attended.reshape(image_count, row_count, col_count, features).astype(
        jnp.bfloat16
    )
    branch = (
        jnp.einsum("bxyd,de->bxye", attended_low, full_proj, preferred_element_type=jnp.float32)
        + shift_rows[5]
    )
    middle = inputs_f + branch
    normed_two, norm_two_pullback = jax.vjp(layer_norm, middle, gain_rows[1], shift_rows[1])
    normed_two_low = normed_two.astype(jnp.bfloat16)
    hidden = jnp.einsum(
        "bxyd,df->bxyf", normed_two_low, full_up, preferred_element_type=jnp.float32
    ) + shift_rows[6:-1].reshape(-1)
    activated, gelu_pullback = jax.vjp(gelu_tanh, hidden)
    activated_low = activated.astype(jnp.bfloat16)
    output = (
        middle
        + jnp.einsum("bxyf,fd->bxyd", activated_low, full_down, preferred_element_type=jnp.float32)
        + shift_rows[-1]
    )
    output_low = output.astype(jnp.bfloat16)
    upstream = cotangent.astype(jnp.float32)
    grad_down = jnp.einsum(
        "bxyf,bxyd->fd", activated_low, cotangent, preferred_element_type=jnp.float32
    )
    grad_shift_down = jnp.sum(upstream, (0, 1, 2))
    grad_activated = jnp.einsum(
        "bxyd,fd->bxyf", cotangent, full_down, preferred_element_type=jnp.float32
    )
    (grad_hidden,) = gelu_pullback(grad_activated)
    grad_hidden_low = grad_hidden.astype(jnp.bfloat16)
    grad_up = jnp.einsum(
        "bxyd,bxyf->df", normed_two_low, grad_hidden_low, preferred_element_type=jnp.float32
    )
    grad_shift_up = jnp.sum(grad_hidden_low.astype(jnp.float32), (0, 1, 2))
    grad_normed_two = jnp.einsum(
        "bxyf,df->bxyd", grad_hidden_low, full_up, preferred_element_type=jnp.float32
    )
    grad_middle_norm, grad_gain_two, grad_shift_two = norm_two_pullback(grad_normed_two)
    grad_middle = upstream + grad_middle_norm
    grad_branch_low = grad_middle.astype(jnp.bfloat16)
    grad_proj = jnp.einsum(
        "bxyd,bxye->de", attended_low, grad_branch_low, preferred_element_type=jnp.float32
    )
    grad_shift_proj = jnp.sum(grad_branch_low.astype(jnp.float32), (0, 1, 2))
    grad_attended = jnp.einsum(
        "bxye,de->bxyd", grad_branch_low, full_proj, preferred_element_type=jnp.float32
    )
    grad_flat = grad_attended.astype(jnp.bfloat16).reshape(
        image_count, query_count, head_count, head_dim
    )
    grad_flat_f = grad_flat.astype(jnp.float32)
    key_value_all = lax.all_gather(key_value, "rows", axis=1, tiled=True)
    scores = key_scores(key_value_all)
    soft = jnp.exp(scores - log_total[..., None])
    keys_all = key_value_all[..., :features].reshape(image_count, key_total, head_count, head_dim)
    values_all = key_value_all[..., features:].reshape(image_count, key_total, head_count, head_dim)
    grad_soft = jnp.einsum(
        "bqhc,bkhc->bhqk", grad_flat, values_all, preferred_element_type=jnp.float32
    )
    row_dot = jnp.sum(soft * grad_soft, -1, keepdims=True)
    grad_scores = (soft * (grad_soft - row_dot)).astype(jnp.bfloat16)
    grad_queries = (
        scale_factor
        * jnp.einsum("bhqk,bkhc->bqhc", grad_scores, keys_all, preferred_element_type=jnp.float32)
        + grad_flat_f
    )
    grad_scores_f = grad_scores.astype(jnp.float32).reshape(
        image_count, head_count, row_count, col_count, key_rows_all, key_cols
    )
    grad_query_rel, grad_rel_h, grad_rel_w = rel_pullback(
        (jnp.sum(grad_scores_f, -1), jnp.sum(grad_scores_f, -2))
    )
    grad_queries = (
        grad_queries.reshape(image_count, row_count, col_count, head_count, head_dim)
        + grad_query_rel
    )
    key_span = key_local * lax.axis_size("rows")
    part_scores = lax.slice_in_dim(grad_scores, 0, key_span, axis=3)
    part_soft = lax.slice_in_dim(soft, 0, key_span, axis=3)
    grad_keys_part = scale_factor * jnp.einsum(
        "bhqk,bqhc->kbhc", part_scores, query_flat, preferred_element_type=jnp.float32
    )
    grad_values_part = jnp.einsum("bhqk,bqhc->kbhc", part_soft, grad_flat_f, precision=highest)
    key_grads = (
        lax.psum_scatter(
            jnp.concatenate(
                [
                    grad_keys_part.reshape(key_span, image_count, features),
                    grad_values_part.reshape(key_span, image_count, features),
                ],
                -1,
            ).astype(jnp.bfloat16),
            "rows",
            scatter_dimension=0,
            tiled=True,
        )
        .astype(jnp.float32)
        .transpose(1, 0, 2)
    )
    grad_keys = key_grads[..., :features].reshape(
        image_count, row_count // 2, key_cols, head_count, head_dim
    )
    grad_values = key_grads[..., features:].reshape(
        image_count, row_count // 2, key_cols, head_count, head_dim
    )
    grad_extended, grad_kernels, grad_pool_gain, grad_pool_shift = pool_pullback(
        (grad_queries, grad_keys, grad_values)
    )
    rims = jnp.concatenate([grad_extended[:, :, :1], grad_extended[:, :, -1:]], 2)
    rims_all = padded(rims.astype(jnp.bfloat16), (("rows", 2),), 1).astype(rims.dtype)
    grad_mixed = grad_extended[:, :, 1:-1]
    grad_mixed = grad_mixed.at[:, :, 0].add(rims_all[:, :, 0]).at[:, :, -1].add(rims_all[:, :, 3])
    grad_mixed_low = grad_mixed.astype(jnp.bfloat16)
    grad_qkv = jnp.einsum(
        "bxyd,mbxye->dme", normed_low, grad_mixed_low, preferred_element_type=jnp.float32
    ).reshape(features, 3 * features)
    grad_shift_qkv = jnp.sum(grad_mixed_low.astype(jnp.float32), (1, 2, 3))
    grad_normed_one = jnp.einsum(
        "mbxye,dme->bxyd", grad_mixed_low, qkv_split, preferred_element_type=jnp.float32
    )
    grad_inputs_norm, grad_gain_one, grad_shift_one = norm_one_pullback(grad_normed_one)
    grad_images = grad_middle + grad_inputs_norm
    grad_gains = jnp.stack([grad_gain_one, grad_gain_two])
    grad_shifts = jnp.concatenate(
        [
            grad_shift_one[None],
            grad_shift_two[None],
            grad_shift_qkv,
            grad_shift_proj[None],
            grad_shift_up.reshape(-1, features),
            grad_shift_down[None],
        ],
        0,
    )
    small_summed = lax.psum(
        (
            grad_gains,
            grad_shifts,
            grad_kernels,
            grad_pool_gain,
            grad_pool_shift,
            grad_rel_h,
            grad_rel_w,
        ),
        ("batch", "rows"),
    )
    matrix_grads = (grad_qkv, grad_proj, grad_up, grad_down)
    summed_rows = (
        lax.psum(matrix_grads[0].astype(jnp.bfloat16), "rows").astype(jnp.float32),
        lax.psum(matrix_grads[1].astype(jnp.bfloat16), "rows").astype(jnp.float32),
        lax.psum(matrix_grads[2].astype(jnp.bfloat16), "rows").astype(jnp.float32),
        lax.psum(matrix_grads[3].astype(jnp.bfloat16), "rows").astype(jnp.float32),
    )
    owned = (
        lax.psum_scatter(
            summed_rows[0].astype(jnp.bfloat16), "batch", scatter_dimension=0, tiled=True
        ).astype(jnp.float32),
        lax.psum_scatter(
            summed_rows[1].astype(jnp.bfloat16), "batch", scatter_dimension=0, tiled=True
        ).astype(jnp.float32),
        lax.psum_scatter(
            summed_rows[2].astype(jnp.bfloat16), "batch", scatter_dimension=0, tiled=True
        ).astype(jnp.float32),
        lax.psum_scatter(
            summed_rows[3].astype(jnp.bfloat16), "batch", scatter_dimension=0, tiled=True
        ).astype(jnp.float32),
    )
    return (
        output_low,
        grad_images,
        owned[0],
        owned[1],
        owned[2],
        owned[3],
        small_summed[0],
        small_summed[1],
        small_summed[2],
        small_summed[3],
        small_summed[4],
        small_summed[5],
        small_summed[6],
    )


LANES = 128
NT = (((1,), (1,)), ((), ()))
TN = (((0,), (0,)), ((), ()))
NN = (((1,), (0,)), ((), ()))
f32 = jnp.float32
bf16 = jnp.bfloat16


def dot(a, b, dims=NN):
    return lax.dot_general(a, b, dims, preferred_element_type=f32)


def lane_ids(shape):
    return lax.broadcasted_iota(jnp.int32, shape, len(shape) - 1)


def head_mask(rows):
    return (lane_ids((rows, LANES)) < HEAD_DIM).astype(f32)


def head_piece(values, start):
    base = start // LANES * LANES
    move = start - base
    if move == 0:
        piece = values[:, base : base + LANES]
    else:
        piece = pltpu.roll(values[:, base : base + 2 * LANES], 2 * LANES - move, 1)[:, :LANES]
    return piece * head_mask(values.shape[0])


def norm_parts(values, count):
    centre = jnp.sum(values, -1, keepdims=True) * (1.0 / count)
    centred = values - centre
    spread = jnp.sum(centred * centred, -1, keepdims=True) * (1.0 / count)
    scale = lax.rsqrt(spread + norm_eps)
    return centred * scale, scale


def head_norm_parts(values, mask):
    centre = jnp.sum(values, -1, keepdims=True) * (1.0 / HEAD_DIM)
    centred = (values - centre) * mask
    spread = jnp.sum(centred * centred, -1, keepdims=True) * (1.0 / HEAD_DIM)
    scale = lax.rsqrt(spread + norm_eps)
    return centred * scale, scale


def norm_back(grad, unit, scale, count):
    first = jnp.sum(grad, -1, keepdims=True) * (1.0 / count)
    second = jnp.sum(grad * unit, -1, keepdims=True) * (1.0 / count)
    return scale * (grad - first - unit * second)


def fold_rows(values):
    rows, lanes = values.shape
    return jnp.sum(values.reshape(rows // 8, 8, lanes), 0)


def fold_block(values):
    rows = values.shape[0]
    tail = values[:, LANES : LANES + 64].astype(f32)
    tail = jnp.concatenate([tail, jnp.zeros_like(tail)], 1)
    side = tail[: rows // 2] + pltpu.roll(tail[rows // 2 :], 64, 1)
    return jnp.concatenate([values[:, :LANES].astype(bf16), side.astype(bf16)], 0)


def unfold_block(folded):
    rows = folded.shape[0] * 2 // 3
    side = folded[rows:].astype(f32)
    tail = jnp.concatenate([side, pltpu.roll(side, 64, 1)], 0).astype(folded.dtype)
    return jnp.concatenate([folded[:rows], tail[:, :64]], 1)


def turned(shift):
    return lax.rem(lax.axis_index("rows") + shift, 4)


def copy_all(pairs, sems):
    copies = []
    for near, far in pairs:
        copies.append(pltpu.make_async_copy(near, far, sems.at[len(copies)]))
        copies[-1].start()
    return copies


def wait_all(copies):
    for copy in copies:
        copy.wait()


def pack_kernel(qkv_ref, proj_ref, up_ref, down_ref, packed_ref, qkv_in, proj_in, up_in, down_in, sems):
    wait_all(
        copy_all(
            [(qkv_ref, qkv_in), (proj_ref, proj_in), (up_ref, up_in), (down_ref, down_in)], sems
        )
    )
    share = qkv_in.shape[0]
    packed_ref[...] = jnp.concatenate(
        [qkv_in[...].astype(f32), proj_in[...].astype(f32), up_in[...].astype(f32)]
        + [
            down_in[...].astype(f32)[share * i : share * (i + 1)]
            for i in range(down_in.shape[0] // share)
        ],
        1,
    ).astype(bf16)


def fold_images_kernel(img_ref, out_ref, img_in, sems):
    loads = copy_all([(img_ref.at[k], img_in.at[k]) for k in range(4)], sems)
    for block in range(4):
        loads[block].wait()
        out_ref[block] = fold_block(img_in[block])


def fold_kernel(cot_ref, cot_0, cot_1, cot_2, cot_3, cot_in, cot_scr, in_sems, sems):
    loads = copy_all([(cot_ref.at[turned(k)], cot_in.at[k]) for k in range(4)], in_sems)
    copies = []
    for shift, far in enumerate((cot_0, cot_1, cot_2, cot_3)):
        loads[shift].wait()
        cot_scr[shift] = fold_block(cot_in[shift])
        copies.append(pltpu.make_async_copy(cot_scr.at[shift], far, sems.at[shift]))
        copies[-1].start()
    wait_all(copies)


def flipped(flip):
    place = lax.axis_index("batch")
    owner = place
    for bit in (1, 2, 4):
        if flip & bit:
            owner = owner + bit - 2 * bit * lax.rem(place // bit, 2)
    return owner


def gather_rows(own_ref, other_ref, first, last, full_scr):
    share = own_ref.shape[1]
    for flip in range(8):
        source = other_ref if flip & 1 else own_ref
        rows = pl.ds(pl.multiple_of(flipped(flip) * share, 8), share)
        full_scr[rows, :] = source[flip // 2, :, first:last].astype(f32)


def load_taps(kernel_ref, kernel_scr):
    kernel_scr[...] = jnp.zeros_like(kernel_scr)
    for tap in range(9):
        kernel_scr[tap, 0:3, 0:HEAD_DIM] = kernel_ref[tap].astype(f32)


def load_gains(gain_ref, shift_ref, gain_scr):
    gain_scr[...] = jnp.zeros_like(gain_scr)
    gain_scr[0:3, 0:HEAD_DIM] = gain_ref[...].astype(f32)
    gain_scr[3:5, 0:HEAD_DIM] = shift_ref[...].astype(f32)


def clear_rim(padded_scr):
    rows, cols, lanes = padded_scr.shape[-3:]
    for place in range(padded_scr.shape[0] if len(padded_scr.shape) == 4 else 1):
        cells = padded_scr.at[place] if len(padded_scr.shape) == 4 else padded_scr
        cells[0:1] = jnp.zeros((1, cols, lanes), f32)
        cells[rows - 1 : rows] = jnp.zeros((1, cols, lanes), f32)
        cells[:, 0:8, :] = jnp.zeros((rows, 8, lanes), f32)
        cells[:, cols - 8 : cols, :] = jnp.zeros((rows, 8, lanes), f32)


CHUNK_ROWS = 4
POOL_ROWS = 8
MIX_ROWS = 32
ATTEND_ROWS = 32
BACK_ROWS = 32
WEIGH_TILE = 1024
IMAGE_TILE = 1024
LOG2_E = 1.4426950408889634


def stride_windows(padded, place, side, key_rows, key_cols):
    columns = pl.ds(7 + side, key_cols, stride=2)
    even = padded[place, pl.ds(0, key_rows + 1, stride=2), columns, :]
    odd = padded[place, pl.ds(1, key_rows, stride=2), columns, :]
    return even[:key_rows], odd, even[1:]


def attend_kernel(
    stage, weight_scr, bias_ref, rows_ref, kern_scr, gain_scr, table_ref,
    img_ref, padded, qunit_out, qscale_out, kvraw_out, soft_out, att_out, key_out, val_out,
    query_scr, keyaug_scr,
):
    cols = padded.shape[2] - 16
    rows = padded.shape[1] - 2
    tile = POOL_ROWS * cols
    chunks = rows // POOL_ROWS
    key_cols = cols // 2
    key_rows = rows // 2
    key_total = key_rows * key_cols
    features = img_ref.shape[1]
    clear_rim(padded)
    gain_one = rows_ref[16:17, 0:features]
    shift_one = rows_ref[0:1, 0:features]
    table = table_ref[...]

    mix_tile = MIX_ROWS * cols

    img_ref[...] = jnp.concatenate(
        [unfold_block(stage[place]) for place in range(4)], 0
    )

    def mix(step, carry):
        span = pl.ds(pl.multiple_of(step * mix_tile, mix_tile), mix_tile)
        unit, _ = norm_parts(img_ref[span, :].astype(f32), features)
        normed = (unit * gain_one + shift_one).astype(bf16)
        mixed = dot(normed, weight_scr[...]) + bias_ref[0:1, :]
        for place in range(3 * HEADS):
            low = mixed[:, place * LANES : (place + 1) * LANES].astype(bf16)
            padded[place, pl.ds(1 + step * MIX_ROWS, MIX_ROWS), 8 : 8 + cols, :] = low.astype(
                f32
            ).reshape(MIX_ROWS, cols, LANES)
        return carry

    lax.fori_loop(0, rows // MIX_ROWS, mix, 0, unroll=True)

    tile_mask = head_mask(tile)

    def pool_queries(step, carry):
        span = pl.ds(pl.multiple_of(step * tile, tile), tile)
        for head in range(HEADS):
            total = jnp.zeros((POOL_ROWS, cols, LANES), f32)
            for side in range(3):
                window = padded[
                    head, pl.ds(step * POOL_ROWS, POOL_ROWS + 2), 7 + side : 7 + side + cols, :
                ]
                for up in range(3):
                    total = total + window[up : up + POOL_ROWS] * kern_scr[3 * up + side, 0:1, :]
            unit, scale = head_norm_parts(total.reshape(tile, LANES), tile_mask)
            qunit_out[head, span, :] = unit
            qscale_out[head, span, :] = jnp.broadcast_to(scale, (tile, LANES))
            query_scr[head, span, :] = (unit * gain_scr[0:1, :] + gain_scr[3:4, :]).astype(bf16)
        return carry

    lax.fori_loop(0, chunks, pool_queries, 0, unroll=True)

    for place in range(2 * HEADS):
        member = 1 + place // HEADS
        total = jnp.zeros((key_rows, key_cols, LANES), f32)
        for side in range(3):
            for up, window in enumerate(stride_windows(padded, HEADS + place, side, key_rows, key_cols)):
                total = total + window * kern_scr[3 * up + side, member : member + 1, :]
        kvraw_out[place] = total.reshape(key_total, LANES)

    key_mask = head_mask(key_total)
    key_place = lax.broadcasted_iota(jnp.int32, (key_total, LANES), 0)
    lanes = lane_ids((key_total, LANES))
    from_row = 30 - 2 * (key_place // key_cols)
    from_col = 96 + 2 * (key_place % key_cols)
    hot = (
        (lanes == from_row)
        | (lanes == from_row + 64)
        | (lanes == from_col)
        | (lanes == from_col - 64)
    ).astype(bf16)
    for head in range(HEADS):
        unit, _ = head_norm_parts(kvraw_out[head], key_mask)
        low = (unit * gain_scr[1:2, :]).astype(bf16)
        key_out[head] = low
        keyaug_scr[head, :, 0:LANES] = low
        keyaug_scr[head, :, LANES : 2 * LANES] = hot
        unit, _ = head_norm_parts(kvraw_out[HEADS + head], key_mask)
        val_out[head] = (unit * gain_scr[2:3, :] + gain_scr[4:5, :]).astype(bf16)

    scale_factor = HEAD_DIM ** (-0.5)
    row_lanes = lane_ids((cols, LANES))
    part_tile = ATTEND_ROWS * cols
    part_lanes = lane_ids((part_tile, LANES))

    def attend(step, carry):
        span = pl.ds(pl.multiple_of(step * part_tile, part_tile), part_tile)
        for head in range(HEADS):
            query = query_scr[head, span, :]
            looked = dot(query, table, NT) * (1.0 / scale_factor)
            pieces = []
            for row in range(ATTEND_ROWS):
                part = looked[row * cols : (row + 1) * cols, :]
                place = step * ATTEND_ROWS + row
                by_row = pltpu.roll(part, LANES - place, 1)
                by_col = pltpu.roll(part, 0, 1, stride=1, stride_axis=0)
                pieces.append(jnp.where(row_lanes < 64, by_row, by_col))
            terms = jnp.concatenate(pieces, 0)
            high = terms.astype(bf16).astype(f32)
            rest = pltpu.roll(terms - high, 64, 1)
            both = jnp.where((part_lanes < 32) | (part_lanes >= 96), high, rest).astype(bf16)
            scores = dot(jnp.concatenate([query, both], 1), keyaug_scr[head], NT)
            top = jnp.max(scores, -1, keepdims=True)
            powers = jnp.exp2((scores - top) * (scale_factor * LOG2_E))
            soft = (powers * (1.0 / jnp.sum(powers, -1, keepdims=True))).astype(bf16)
            soft_out[head, span, :] = soft
            att = dot(soft, val_out[head]) + query.astype(f32)
            att_out[span, head * LANES : (head + 1) * LANES] = att.astype(bf16)
        return carry

    lax.fori_loop(0, rows // ATTEND_ROWS, attend, 0, unroll=True)


def stack_blocks(values, block_scr):
    owners = block_scr.shape[0]
    share = values.shape[0] // owners
    for block in range(values.shape[1] // LANES):
        for owner in range(owners):
            block_scr[owner, share * block : share * (block + 1), :] = values[
                share * owner : share * (owner + 1), block * LANES : (block + 1) * LANES
            ]


def split_owners(block_scr, mine_ref, theirs_ref, order):
    count = block_scr.shape[1]
    for place, flip in enumerate(order):
        span = pl.ds(place * count, count)
        mine_ref[span, :] = block_scr[flipped(flip)].astype(bf16)
        theirs_ref[span, :] = block_scr[flipped(flip + 1)].astype(bf16)


def weights_kernel(
    owners, own_ref, other_ref, gains_far, shifts_far, kern_far, pgain_far, pshift_far, relh_far, relw_far,
    wide_ref, proj_ref, up_ref, down_ref, bias_ref, rows_ref, columns_ref, taps_ref, pool_ref, ahead_ref, behind_ref,
    full_scr, down_scr, gains_in, shifts_in, kern_in, pgain_in, pshift_in, relh_in, relw_in, table_scr, sems,
):
    loads = copy_all(
        [
            (gains_far, gains_in), (shifts_far, shifts_in), (kern_far, kern_in), (pgain_far, pgain_in),
            (pshift_far, pshift_in), (relh_far, relh_in), (relw_far, relw_in),
        ],
        sems,
    )
    gather_rows(own_ref, other_ref, 0, own_ref.shape[2], full_scr)
    for place in range(3 * HEADS):
        wide_ref[:, place * LANES : (place + 1) * LANES] = head_piece(
            full_scr[:, 0 : 5 * LANES], place * HEAD_DIM
        ).astype(bf16)
    features, hidden_count = up_ref.shape
    proj = pltpu.roll(full_scr[:, 4 * LANES : 6 * LANES], 192, 1)[:, 0:features]
    gap = jnp.zeros((LANES - HEAD_DIM, features), f32)
    proj_ref[...] = jnp.concatenate(
        [proj[0:HEAD_DIM, :], gap, proj[HEAD_DIM : 2 * HEAD_DIM, :], gap], 0
    ).astype(bf16)
    up_ref[...] = full_scr[:, 4 * features : 4 * features + hidden_count].astype(bf16)
    columns = full_scr[:, 4 * features + hidden_count :]
    share = features // owners
    pieces = hidden_count // features
    for piece in range(pieces):
        start = piece * features
        base = start // LANES * LANES
        window = columns[:, base : base + 2 * LANES]
        if start != base:
            window = pltpu.roll(window, 2 * LANES - (start - base), 1)
        for owner in range(owners):
            place = owner * share * pieces + piece * share
            down_scr[place : place + share, :] = window[
                owner * share : (owner + 1) * share, 0:features
            ]
    down_ref[...] = down_scr[...].astype(bf16)
    wait_all(loads)
    rows_ref[...] = jnp.zeros_like(rows_ref)
    rows_ref[0 : shifts_in.shape[0], 0:features] = shifts_in[...].astype(f32)
    rows_ref[16:18, 0:features] = gains_in[...].astype(f32)
    columns_ref[...] = jnp.concatenate(
        [rows_ref[...], jnp.zeros((LANES - rows_ref.shape[0], 2 * LANES), f32)], 0
    ).T
    bias_ref[...] = jnp.zeros_like(bias_ref)
    for section in range(3):
        for head in range(HEADS):
            place = (section * HEADS + head) * LANES
            bias_ref[0:1, place : place + LANES] = head_piece(
                rows_ref[2 + section : 3 + section, :], head * HEAD_DIM
            )
    for piece in range(pieces):
        bias_ref[1:2, piece * features : (piece + 1) * features] = rows_ref[
            6 + piece : 7 + piece, 0:features
        ]
    load_taps(kern_in, taps_ref)
    load_gains(pgain_in, pshift_in, pool_ref)
    count = relw_in.shape[0]
    table_scr[...] = jnp.zeros_like(table_scr)
    table_scr[0:count, 0:HEAD_DIM] = relh_in[...].astype(f32)
    table_scr[64 : 64 + count, 0:HEAD_DIM] = relw_in[...].astype(f32)
    behind_ref[...] = table_scr[...].astype(bf16)
    flip = (
        lax.broadcasted_iota(jnp.int32, (64, count), 0) + lax.broadcasted_iota(jnp.int32, (64, count), 1)
        == count - 1
    ).astype(bf16)
    table_scr[64:128, 0:HEAD_DIM] = dot(flip, relw_in[...])
    ahead_ref[...] = table_scr[...].astype(bf16)


def send_turned(near, fars, sems):
    sends = []
    for shift, far in enumerate(fars):
        sends.append(pltpu.make_async_copy(near.at[turned(shift)], far, sems.at[shift]))
        sends[-1].start()
    return sends


GELU_A = 0.7978845608028654
GELU_B = 0.044715


def feed_ahead_kernel(
    img_ref, att_ref, proj_ref, up_ref, down_ref, bias_ref, rows_ref,
    out_0, out_1, out_2, out_3, normed_ref, unit_ref, scale_ref, active_ref, slope_ref,
    out_stage, turn_sems,
):
    tokens, features = img_ref.shape
    pieces = up_ref.shape[1] // features
    block = tokens // 4
    middle = img_ref[...].astype(f32) + (dot(att_ref[...], proj_ref[...]) + rows_ref[5:6, 0:features])
    unit, scale = norm_parts(middle, features)
    normed = (unit * rows_ref[17:18, 0:features] + rows_ref[1:2, 0:features]).astype(bf16)
    unit_ref[...] = unit
    scale_ref[...] = jnp.broadcast_to(scale, scale_ref.shape)
    normed_ref[...] = normed
    hidden = dot(normed, up_ref[...]) + bias_ref[1:2, :]
    square = hidden * hidden
    wave = jnp.tanh(hidden * (GELU_A + (GELU_A * GELU_B) * square))
    half = 0.5 + 0.5 * wave
    active = (hidden * half).astype(bf16)
    active_ref[...] = active
    slope_ref[...] = half * (
        1.0 + (1.0 - half) * (hidden * (2.0 * GELU_A + (6.0 * GELU_A * GELU_B) * square))
    )
    out = middle + dot(active, down_ref[...]) + rows_ref[6 + pieces : 7 + pieces, 0:features]
    for place in range(4):
        out_stage[place] = fold_block(out[place * block : (place + 1) * block, :])
    wait_all(send_turned(out_stage, (out_0, out_1, out_2, out_3), turn_sems))


def feed_back_kernel(
    owners,
    att_ref, cot_0, cot_1, cot_2, cot_3, normed_ref, unit_ref, scale_ref, active_ref, slope_ref,
    proj_ref, up_ref, down_ref, rows_ref,
    mid_ref, gatt_ref, mine_ref, theirs_ref,
    gdown, gup, gproj, gbias, gsmall, block_scr, cot_stage, cot_sems,
):
    cot_loads = copy_all(
        [(piece, cot_stage.at[turned(4 - k)]) for k, piece in enumerate((cot_0, cot_1, cot_2, cot_3))],
        cot_sems,
    )
    tokens, features = unit_ref.shape
    hidden_count = up_ref.shape[1]
    pieces = hidden_count // features
    unit = unit_ref[...]
    att = att_ref[...]
    wait_all(cot_loads)
    cot_low = jnp.concatenate([unfold_block(cot_stage[place]) for place in range(4)], 0)
    cot = cot_low.astype(f32)
    gdown[...] = dot(cot_low, active_ref[...], TN)
    gact = dot(cot_low, down_ref[...], NT)
    ghid = (gact * slope_ref[...]).astype(bf16)
    gup[...] = dot(normed_ref[...], ghid, TN)
    gbias[...] = fold_rows(ghid.astype(f32))
    gnorm = dot(ghid, up_ref[...], NT)
    gsmall[0:8, :] = fold_rows(gnorm * unit)
    gsmall[8:16, :] = fold_rows(gnorm)
    gmid = cot + norm_back(gnorm * rows_ref[17:18, 0:features], unit, scale_ref[...], features)
    gbranch = gmid.astype(bf16)
    mid_ref[...] = gbranch
    gsmall[16:24, :] = fold_rows(gbranch.astype(f32))
    gsmall[24:32, :] = fold_rows(cot)
    gproj[...] = dot(att, gbranch, TN)
    gatt_ref[...] = dot(gbranch, proj_ref[...], NT).astype(bf16)

    share = features // owners
    proj = jnp.concatenate(
        [gproj[head * LANES : head * LANES + HEAD_DIM, :] for head in range(HEADS)], 0
    )
    down = gdown[...].T
    down_pieces = []
    for piece in range(pieces):
        down_pieces.append(
            jnp.concatenate(
                [
                    down[
                        owner * share * pieces + piece * share : owner * share * pieces
                        + (piece + 1) * share,
                        :,
                    ]
                    for owner in range(owners)
                ],
                0,
            )
        )
    sums = [jnp.sum(gsmall[8 * i : 8 * i + 8, :], 0, keepdims=True) for i in range(4)]
    bias_row = jnp.sum(gbias[...], 0, keepdims=True)
    block = jnp.concatenate(
        sums + [bias_row[:, i * features : (i + 1) * features] for i in range(pieces)], 0
    )
    block = jnp.concatenate([block, jnp.zeros((share - 8, features), f32)], 0)
    small = jnp.concatenate([block] * owners, 0)
    block_scr[...] = jnp.zeros_like(block_scr)
    stack_blocks(jnp.concatenate([proj, gup[...]] + down_pieces + [small], 1), block_scr)
    split_owners(block_scr, mine_ref, theirs_ref, (0, 4, 2, 6))


SMALL_ROWS = 168
DENSE_ROWS = 128
LATE_ROWS = 128


def back_attend_kernel(
    head, qunit_ref, qscale_ref, kvraw_ref, soft_ref, gatt_ref, key_ref, val_ref,
    gain_scr, table_ref,
    gpadded, gkeypad, sums_ref,
    keyaug_scr, gtable, gkey, gval, gsums,
):
    cols = gpadded.shape[1] - 16
    rows = gpadded.shape[0] - 2
    tile = BACK_ROWS * cols
    chunks = rows // BACK_ROWS
    key_cols = cols // 2
    key_rows = rows // 2
    key_total = kvraw_ref.shape[1]
    clear_rim(gpadded)
    gkeypad[...] = jnp.zeros_like(gkeypad)
    table = table_ref[...]
    gsums[...] = jnp.zeros_like(gsums)

    key_place = lax.broadcasted_iota(jnp.int32, (key_total, LANES), 0)
    lanes = lane_ids((key_total, LANES))
    hot = (
        (lanes == 30 - 2 * (key_place // key_cols)) | (lanes == 94 - 2 * (key_place % key_cols))
    ).astype(bf16)
    keyaug_scr[:, 0:LANES] = key_ref[head]
    keyaug_scr[:, LANES : 2 * LANES] = hot

    scale_factor = HEAD_DIM ** (-0.5)
    tile_mask = head_mask(tile)
    row_lanes = lane_ids((cols, LANES))

    def attend(step, carry):
        span = pl.ds(pl.multiple_of(step * tile, tile), tile)
        unit, scale = qunit_ref[head, span, :], qscale_ref[head, span, :]
        query = (unit * gain_scr[0:1, :] + gain_scr[3:4, :]).astype(bf16)
        gatt = gatt_ref[span, head * LANES : (head + 1) * LANES]
        soft_low = soft_ref[head, span, :]
        soft = soft_low.astype(f32)
        gsoft = dot(gatt, val_ref[head], NT)
        inner = jnp.sum(soft * gsoft, -1, keepdims=True)
        gscore = (soft * (gsoft - inner)).astype(bf16)
        gkey[...] = dot(query, gscore, TN)
        gval[...] = dot(gatt, soft_low, TN)
        wide = dot(gscore, keyaug_scr[...])
        gterm = wide[:, LANES : 2 * LANES]
        pieces = []
        for row in range(BACK_ROWS):
            part = gterm[row * cols : (row + 1) * cols, :]
            place = step * BACK_ROWS + row
            by_row = pltpu.roll(part, place, 1)
            by_col = pltpu.roll(part, 0, 1, stride=1, stride_axis=0)
            pieces.append(jnp.where(row_lanes < 64, by_row, by_col))
        glook = jnp.concatenate(pieces, 0).astype(bf16)
        gtable[...] = dot(glook, query, TN)
        gquery = scale_factor * wide[:, 0:LANES] + gatt.astype(f32) + dot(glook, table)
        gsums[0:8, :] = fold_rows(gquery * unit)
        gsums[8:16, :] = fold_rows(gquery)
        graw = norm_back(gquery * gain_scr[0:1, :], unit, scale, HEAD_DIM) * tile_mask
        gpadded[pl.ds(1 + step * BACK_ROWS, BACK_ROWS), 8 : 8 + cols, :] = graw.reshape(
            BACK_ROWS, cols, LANES
        )
        return carry

    lax.fori_loop(0, chunks, attend, 0, unroll=True)

    key_mask = head_mask(key_total)
    for member, grad in ((1, gkey[...].T * scale_factor), (2, gval[...].T)):
        unit, scale = head_norm_parts(kvraw_ref[(member - 1) * HEADS + head], key_mask)
        base = 16 if member == 1 else 24
        gsums[base : base + 8, :] += fold_rows(grad * unit)
        if member == 2:
            gsums[32:40, :] += fold_rows(grad)
        graw = norm_back(grad * gain_scr[member : member + 1, :], unit, scale, HEAD_DIM) * key_mask
        gkeypad[member - 1, 0:key_rows, 0:key_cols, :] = graw.reshape(key_rows, key_cols, LANES)

    sums_ref[...] = jnp.zeros_like(sums_ref)
    sums_ref[0:63, :] = gtable[0:63, :]
    sums_ref[63:126, :] = gtable[64:127, :]
    for place, base in enumerate((0, 16, 24, 8, 32)):
        sums_ref[126 + place : 127 + place, :] = jnp.sum(gsums[base : base + 8, :], 0, keepdims=True)


def back_weights_kernel(
    img_ref, padded, gpadded_0, gpadded_1, gkeypad_0, gkeypad_1, sums_0, sums_1, weight_ref, columns_ref, kern_scr,
    gmix_scr, mine_ref, theirs_ref,
    gmixrow, gkern, gweight, gbias, small_scr, dense_scr, block_scr,
):
    tokens, features = img_ref.shape
    cols = padded.shape[2] - 16
    rows = padded.shape[1] - 2
    tile = CHUNK_ROWS * cols
    chunks = rows // CHUNK_ROWS
    key_cols = cols // 2
    key_rows = rows // 2
    gkern[...] = jnp.zeros_like(gkern)

    def spread_queries(step, carry):
        span = pl.ds(pl.multiple_of(step * tile, tile), tile)
        around = pl.ds(step * CHUNK_ROWS, CHUNK_ROWS + 2)
        for head, gpadded in enumerate((gpadded_0, gpadded_1)):
            total = jnp.zeros((CHUNK_ROWS, cols, LANES), f32)
            own = gpadded[pl.ds(1 + step * CHUNK_ROWS, CHUNK_ROWS), 8 : 8 + cols, :]
            for side in range(3):
                window = gpadded[around, 9 - side : 9 - side + cols, :]
                cells = padded[head, around, 7 + side : 7 + side + cols, :]
                for up in range(3):
                    tap = 3 * up + side
                    total = total + window[2 - up : 2 - up + CHUNK_ROWS] * kern_scr[tap, 0:1, :]
                    gkern[tap] += fold_rows((own * cells[up : up + CHUNK_ROWS]).reshape(tile, LANES))
            flat = total.reshape(tile, LANES).astype(bf16)
            gmix_scr[span, head * LANES : (head + 1) * LANES] = flat
        return carry

    lax.fori_loop(0, chunks, spread_queries, 0, unroll=True)

    evens = pl.ds(0, key_cols, stride=2)
    odds = pl.ds(1, key_cols, stride=2)
    for place in range(2 * HEADS):
        member = 1 + place // HEADS
        taps = [kern_scr[tap, member : member + 1, :] for tap in range(9)]
        gkeypad = (gkeypad_0, gkeypad_1)[place % HEADS].at[place // HEADS]
        left = gkeypad[0 : key_rows + 1, 0:key_cols, :]
        right = gkeypad[0 : key_rows + 1, 1 : 1 + key_cols, :]
        here, below, beside, cross = left[:key_rows], left[1:], right[:key_rows], right[1:]
        gmixrow[:, 0, evens, :] = here * taps[4]
        gmixrow[:, 0, odds, :] = beside * taps[3] + here * taps[5]
        gmixrow[:, 1, evens, :] = below * taps[1] + here * taps[7]
        gmixrow[:, 1, odds, :] = (
            cross * taps[0] + below * taps[2] + beside * taps[6] + here * taps[8]
        )
        lane = (HEADS + place) * LANES
        gmix_scr[:, lane : lane + LANES] = gmixrow[...].reshape(rows * cols, LANES).astype(bf16)
        for side in range(3):
            for up, cells in enumerate(stride_windows(padded, HEADS + place, side, key_rows, key_cols)):
                gkern[9 * member + 3 * up + side] += fold_rows(
                    (here * cells).reshape(key_rows * key_cols, LANES)
                )

    def weigh(step, carry):
        span = pl.ds(pl.multiple_of(step * WEIGH_TILE, WEIGH_TILE), WEIGH_TILE)
        gmix = gmix_scr[span, :]
        unit, _ = norm_parts(img_ref[span, :].astype(f32), features)
        gweight[...] = dot(unit.astype(bf16), gmix, TN)
        gbias[...] = fold_rows(gmix.astype(f32))
        return carry

    lax.fori_loop(0, tokens // WEIGH_TILE, weigh, 0, unroll=True)

    bias_row = jnp.sum(gbias[...], 0, keepdims=True)
    weight = weight_ref[...].astype(f32)
    raw = gweight[...]
    lanes = lane_ids((features, LANES))
    norm_sums = jnp.where(
        lanes == 0,
        jnp.sum(weight * raw, 1, keepdims=True),
        jnp.where(lanes == 1, jnp.sum(weight * bias_row, 1, keepdims=True), 0.0),
    )
    norm_rows = jnp.concatenate([norm_sums, jnp.zeros((2 * LANES - features, LANES), f32)], 0).T
    gweight[...] = raw * columns_ref[0:features, 16:17] + columns_ref[0:features, 0:1] * bias_row

    for tap in range(27):
        row = 3 * (tap % 9) + tap // 9
        small_scr[row : row + 1, :] = jnp.sum(gkern[tap], 0, keepdims=True)
    small_scr[27:158, :] = sums_0[0:131, :] + sums_1[0:131, :]
    for place in range(3 * HEADS):
        small_scr[158 + place : 159 + place, :] = bias_row[:, place * LANES : (place + 1) * LANES]
    for place in range(2):
        for head in range(HEADS):
            at = 164 + HEADS * place + head
            small_scr[at : at + 1, :] = head_piece(norm_rows[place : place + 1, :], head * HEAD_DIM)
    weights = jnp.concatenate(
        [gweight[:, place * LANES : place * LANES + HEAD_DIM] for place in range(3 * HEADS)]
        + [jnp.zeros((features, 64), f32)],
        1,
    )
    block_scr[...] = jnp.zeros_like(block_scr)
    stack_blocks(weights, block_scr)
    split_owners(block_scr, mine_ref, theirs_ref, (0, 2, 4, 6))
    count = block_scr.shape[1]
    dense_scr[...] = jnp.zeros_like(dense_scr)
    dense_scr[0:126, :] = small_scr[0:126, :] * head_mask(126)
    beside = lane_ids((42, LANES)) >= HEAD_DIM
    for piece in range(3):
        moved = small_scr[126:168, :]
        moved = pltpu.roll(moved, HEAD_DIM - 32 * piece, 1)
        dense_scr[42 * piece : 42 * (piece + 1), :] += jnp.where(beside, moved, 0.0)
    small = dense_scr[...].astype(bf16)
    mine_ref[4 * count :, :] = small
    theirs_ref[4 * count :, :] = small


def back_images_kernel(img_ref, gmix_ref, gmid_ref, weight_ref, rows_ref, gimg_ref):
    tokens, features = img_ref.shape
    tile = IMAGE_TILE
    block = tokens // 4
    gain_one = rows_ref[16:17, 0:features]

    def finish(step, carry):
        span = pl.ds(pl.multiple_of(step * tile, tile), tile)
        unit, scale = norm_parts(img_ref[span, :].astype(f32), features)
        gnorm = dot(gmix_ref[span, :], weight_ref[...], NT)
        gimg = gmid_ref[span, :].astype(f32) + norm_back(gnorm * gain_one, unit, scale, features)
        for place in range(tile // block):
            gimg_ref[step * (tile // block) + place] = fold_block(
                gimg[place * block : (place + 1) * block, :]
            )
        return carry

    lax.fori_loop(0, tokens // tile, finish, 0, unroll=True)


def halve_kernel(mine_ref, got_ref, keep_ref, send_ref):
    half = keep_ref.shape[0]
    total = (mine_ref[...].astype(f32) + got_ref[...].astype(f32)).astype(bf16)
    keep_ref[...] = total[:half]
    send_ref[...] = total[half:]


def pair_kernel(shared, mine_ref, got_ref, own_ref, msg_1, msg_2, msg_3):
    total = (mine_ref[...].astype(f32) + got_ref[...].astype(f32)).astype(bf16)
    count = (total.shape[0] - shared) // 4
    for place, out in enumerate((own_ref, msg_1, msg_2, msg_3)):
        out[0:count, :] = total[place * count : (place + 1) * count]
        if shared:
            out[count:, :] = total[4 * count :]


def chips_sum(own_ref, got_1, got_2, got_3):
    return (own_ref[...].astype(f32) + got_1[...].astype(f32)) + (
        got_2[...].astype(f32) + got_3[...].astype(f32)
    )


def two_kernel(own_ref, got_ref, out_ref):
    out_ref[...] = (own_ref[...].astype(f32) + got_ref[...].astype(f32)).astype(bf16)


def four_kernel(own_ref, got_1, got_2, got_3, out_ref):
    out_ref[...] = chips_sum(own_ref, got_1, got_2, got_3).astype(bf16)


def pictures_kernel(out_0, out_1, out_2, out_3, gimg_low, out_ref, gimg_ref):
    for shift in range(4):
        gimg_ref[shift] = unfold_block(gimg_low[shift]).astype(f32)
        block = (out_0, out_1, out_2, out_3)[shift][...]
        out_ref[turned(4 - shift)] = unfold_block(block)


def finish_kernel(
    early_0, early_1, late_0, late_1,
    gqkv_ref, gproj_ref, gup_ref, gdown_ref, ggain_ref, gshift_ref, gkern_ref,
    gpgain_ref, gpshift_ref, grelh_ref, grelw_ref,
    small_scr, dense_scr,
):
    share, features = gproj_ref.shape
    hidden = gup_ref.shape[1]
    pieces = hidden // features
    early = early_0[...].astype(f32) + early_1[...].astype(f32)
    early = jnp.concatenate(
        [early[share * i : share * (i + 1), :] for i in range((2 * features + 2 * hidden) // LANES)], 1
    )
    gproj_ref[...] = early[:, 0:features]
    gup_ref[...] = early[:, features : features + hidden]
    for piece in range(pieces):
        start = features + hidden + piece * features
        gdown_ref[piece * share : (piece + 1) * share, :] = early[:, start : start + features]
    start = features + 2 * hidden
    block = early[0:8, start : start + features]
    late = late_0[...].astype(f32) + late_1[...].astype(f32)
    gqkv_ref[...] = jnp.concatenate([late[share * i : share * (i + 1), :] for i in range(5)], 1)[
        :, 0 : 3 * features
    ]
    dense = late[LATE_ROWS : LATE_ROWS + DENSE_ROWS, :]
    small_scr[0:126, :] = dense[0:126, :]
    dense_scr[...] = dense
    lanes = lane_ids((42, LANES))
    rest = jnp.zeros((42, LANES), f32)
    for piece in range(3):
        moved = pltpu.roll(dense_scr[42 * piece : 42 * (piece + 1), :], 32 + 32 * piece, 1)
        rest = jnp.where((lanes >= 32 * piece) & (lanes < 32 * piece + 32), moved, rest)
    small_scr[126:168, :] = rest
    for tap in range(9):
        gkern_ref[tap] = small_scr[3 * tap : 3 * tap + 3, 0:HEAD_DIM]
    gpgain_ref[...] = small_scr[153:156, 0:HEAD_DIM]
    gpshift_ref[...] = small_scr[156:158, 0:HEAD_DIM]
    grelh_ref[...] = small_scr[27:90, 0:HEAD_DIM]
    grelw_ref[...] = small_scr[90:153, 0:HEAD_DIM]
    ggain_ref[1:2, :] = block[0:1, :]
    gshift_ref[1:2, :] = block[1:2, :]
    for head in range(HEADS):
        lanes = slice(head * HEAD_DIM, (head + 1) * HEAD_DIM)
        ggain_ref[0:1, lanes] = small_scr[164 + head : 165 + head, 0:HEAD_DIM]
        gshift_ref[0:1, lanes] = small_scr[166 + head : 167 + head, 0:HEAD_DIM]
        for section in range(3):
            row = 158 + section * HEADS + head
            gshift_ref[2 + section : 3 + section, lanes] = small_scr[row : row + 1, 0:HEAD_DIM]
    gshift_ref[5:6, :] = block[2:3, :]
    gshift_ref[6 : 6 + pieces, :] = block[4 : 4 + pieces, :]
    gshift_ref[6 + pieces : 7 + pieces, :] = block[3:4, :]


LONG = {"back_attend_1": 2 * 10**10}


def call(kernel, name, outs, scratch, flops, limit, spaces, out_spaces, *args):
    place = {"v": pltpu.VMEM, "p": pltpu.VMEM, "h": pltpu.HBM, "a": pl.ANY}
    keep = {"p": pltpu.VMEM, "h": pltpu.HBM}
    args = [
        pltpu.with_memory_space_constraint(a, keep[c]) if c in keep else a for c, a in zip(spaces, args)
    ]
    outs = [keep[c](o.shape, o.dtype) if c in keep else o for c, o in zip(out_spaces, outs)]
    return pl.pallas_call(
        kernel,
        name=name,
        out_shape=outs,
        in_specs=[pl.BlockSpec(memory_space=place[c]) for c in spaces],
        out_specs=[pl.BlockSpec(memory_space=place[c]) for c in out_spaces],
        scratch_shapes=scratch,
        cost_estimate=pl.CostEstimate(flops=LONG.get(name, 1), bytes_accessed=LONG.get(name, 1) // 500, transcendentals=0),
        compiler_params=pltpu.CompilerParams(vmem_limit_bytes=limit * 2**20),
    )(*args)


KA_LIMIT = 36


def whole_image(
    images,
    w_qkv,
    w_proj,
    w_up,
    w_down,
    gains_main,
    shifts_main,
    pool_kernels,
    pool_gains,
    pool_shifts,
    rel_height,
    rel_width,
    cotangent,
):
    owners = lax.axis_size("batch")
    cycle = lax.axis_size("rows")
    image_count, row_count, cols, features = images.shape
    rows = row_count * cycle
    tokens = rows * cols
    hidden = w_up.shape[1]
    share = w_proj.shape[0]
    pieces = hidden // features
    key_total = tokens // 4
    early_used = (2 * features + 2 * hidden) // LANES * share
    early_rows = -(-early_used // 16) * 16
    def shaped(shape, dtype):
        return jax.ShapeDtypeStruct(shape, dtype)

    block = tokens // cycle
    folded = (block * features // LANES, LANES)
    width = 4 * features + 2 * hidden

    def send_on(pieces):
        return list(pieces[:1]) + [
            lax.ppermute(pieces[k], "rows", [(i, (i + k) % cycle) for i in range(cycle)])
            for k in range(1, cycle)
        ]

    def trade(cells, flip):
        return lax.ppermute(cells, "batch", [(i, i ^ flip) for i in range(owners)])

    img = call(
        fold_images_kernel,
        "fold_images",
        [shaped((cycle,) + folded, bf16)],
        [pltpu.VMEM((cycle, block, features), bf16), pltpu.SemaphoreType.DMA((4,))],
        1,
        4,
        "h",
        "v",
        images.reshape(cycle, block, features),
    )[0]
    img, w_qkv = lax.optimization_barrier((img, w_qkv))
    img = lax.all_to_all(img, "rows", 0, 0, tiled=True)
    packed = call(
        pack_kernel,
        "pack",
        [shaped((share, width), bf16)],
        [pltpu.VMEM(w.shape, bf16) for w in (w_qkv, w_proj, w_up, w_down)]
        + [pltpu.SemaphoreType.DMA((4,))],
        10**6,
        4,
        "hhhh",
        "v",
        w_qkv, w_proj, w_up, w_down,
    )[0]
    packed, cotangent = lax.optimization_barrier((packed, cotangent))
    cot_pieces = call(
        fold_kernel,
        "fold",
        [shaped(folded, bf16)] * cycle,
        [
            pltpu.VMEM((cycle, block, features), bf16),
            pltpu.VMEM((cycle,) + folded, bf16),
            pltpu.SemaphoreType.DMA((4,)),
            pltpu.SemaphoreType.DMA((4,)),
        ],
        10**6,
        8,
        "h",
        "a" * 4,
        cotangent.reshape(cycle, block, features),
    )
    img, cot_pieces, *shards = lax.optimization_barrier(
        (img, cot_pieces, *[trade(packed, flip) for flip in (2, 4, 6)])
    )
    own = jnp.stack([packed, *shards])
    other = trade(own, 1)
    taps = pool_kernels.transpose(1, 0, 2)
    small = (gains_main, shifts_main, taps, pool_gains, pool_shifts, rel_height, rel_width)
    wide, full_proj, full_up, full_down, biases, lines, columns, taps_wide, pool_lines, ahead, behind = call(
        functools.partial(weights_kernel, owners),
        "weights",
        [
            shaped((features, 3 * HEADS * LANES), bf16),
            shaped((HEADS * LANES, features), bf16),
            shaped((features, hidden), bf16),
            shaped((hidden, features), bf16),
            shaped((8, hidden), f32),
            shaped((24, 2 * LANES), f32),
            shaped((2 * LANES, LANES), f32),
            shaped((9, 8, LANES), f32),
            shaped((8, LANES), f32),
            shaped((LANES, LANES), bf16),
            shaped((LANES, LANES), bf16),
        ],
        [pltpu.VMEM((features, width), f32), pltpu.VMEM((hidden, features), f32)]
        + [pltpu.VMEM(a.shape, bf16) for a in small]
        + [pltpu.VMEM((LANES, LANES), f32), pltpu.SemaphoreType.DMA((7,))],
        10**6,
        12,
        "vv" + "h" * 7,
        "v" * 11,
        own, other, *small,
    )
    cot_pieces = send_on(cot_pieces)
    whole = [
        shaped((3 * HEADS, rows + 2, cols + 16, LANES), f32),
        shaped((HEADS, tokens, LANES), f32),
        shaped((HEADS, tokens, LANES), f32),
        shaped((2 * HEADS, key_total, LANES), f32),
        shaped((HEADS, tokens, key_total), bf16),
        shaped((tokens, HEADS * LANES), bf16),
    ]
    img, padded, qunit, qscale, kvraw, soft, att, keys, values = call(
        attend_kernel,
        "attend",
        [shaped((tokens, features), bf16)] + whole + [shaped((HEADS, key_total, LANES), bf16)] * 2,
        [
            pltpu.VMEM((HEADS, tokens, LANES), bf16),
            pltpu.VMEM((HEADS, key_total, 2 * LANES), bf16),
        ],
        10**10,
        KA_LIMIT,
        "v" * 7,
        "p" * 9,
        img, wide, biases, lines, taps_wide, pool_lines, ahead,
    )
    *out_pieces, normed, unit, scale, active, slope = call(
        feed_ahead_kernel,
        "feed_ahead",
        [shaped(folded, bf16)] * cycle
        + [
            shaped((tokens, features), bf16),
            shaped((tokens, features), f32),
            shaped((tokens, features), f32),
            shaped((tokens, hidden), bf16),
            shaped((tokens, hidden), f32),
        ],
        [pltpu.VMEM((cycle,) + folded, bf16), pltpu.SemaphoreType.DMA((4,))],
        1,
        36,
        "pp" + "v" * 5,
        "a" * cycle + "p" * 5,
        img, att, full_proj, full_up, full_down, biases, lines,
    )
    gmid, gatt, mine, theirs = call(
        functools.partial(feed_back_kernel, owners),
        "feed_back",
        [shaped((tokens, features), bf16), shaped((tokens, HEADS * LANES), bf16)]
        + [shaped((4 * early_rows, LANES), bf16)] * 2,
        [
            pltpu.VMEM((features, hidden), f32),
            pltpu.VMEM((features, hidden), f32),
            pltpu.VMEM((HEADS * LANES, features), f32),
            pltpu.VMEM((8, hidden), f32),
            pltpu.VMEM((32, features), f32),
            pltpu.VMEM((owners, early_rows, LANES), f32),
            pltpu.VMEM((cycle,) + folded, bf16),
            pltpu.SemaphoreType.DMA((4,)),
        ],
        1,
        36,
        "p" + "a" * 4 + "p" * 5 + "v" * 4,
        "pp" + "vv",
        att, *cot_pieces, normed, unit, scale, active, slope, full_proj, full_up, full_down, lines,
    )

    def halved(mine, got):
        return call(
            halve_kernel,
            "halve",
            [shaped((mine.shape[0] // 2, LANES), bf16)] * 2,
            [],
            10**6,
            4,
            "vv",
            "vv",
            mine, got,
        )

    got = trade(theirs, 1)

    def back_attend(head, behind):
        return call(
            functools.partial(back_attend_kernel, head),
            f"back_attend_{head}",
            [
                shaped((rows + 2, cols + 16, LANES), f32),
                shaped((2, rows // 2 + 1, cols // 2 + 8, LANES), f32),
                shaped((136, LANES), f32),
            ],
            [
                pltpu.VMEM((key_total, 2 * LANES), bf16),
                pltpu.VMEM((LANES, LANES), f32),
                pltpu.VMEM((LANES, key_total), f32),
                pltpu.VMEM((LANES, key_total), f32),
                pltpu.VMEM((40, LANES), f32),
            ],
            10**10,
            30,
            "p" * 7 + "vv",
            "ppp",
            qunit, qscale, kvraw, soft, gatt, keys, values, pool_lines, behind,
        )

    gpadded_0, gkeypad_0, sums_0 = back_attend(0, behind)
    got, gkeypad_0, behind = lax.optimization_barrier((got, gkeypad_0, behind))
    early, away = halved(mine, got)
    away = trade(away, 2)
    out_pieces = send_on(out_pieces)
    gpadded_1, gkeypad_1, sums_1 = back_attend(1, behind)
    gmix, mine, theirs = call(
        back_weights_kernel,
        "back_weights",
        [shaped((tokens, 3 * HEADS * LANES), bf16)]
        + [shaped((4 * LATE_ROWS + DENSE_ROWS, LANES), bf16)] * 2,
        [
            pltpu.VMEM((rows // 2, 2, cols, LANES), f32),
            pltpu.VMEM((27, 8, LANES), f32),
            pltpu.VMEM((features, 3 * HEADS * LANES), f32),
            pltpu.VMEM((8, 3 * HEADS * LANES), f32),
            pltpu.VMEM((SMALL_ROWS, LANES), f32),
            pltpu.VMEM((DENSE_ROWS, LANES), f32),
            pltpu.VMEM((owners, LATE_ROWS, LANES), f32),
        ],
        10**10,
        30,
        "p" + "p" * 7 + "v" * 3,
        "pvv",
        img, padded, gpadded_0, gpadded_1, gkeypad_0, gkeypad_1, sums_0, sums_1, wide, columns, taps_wide,
    )

    def summed(kernel, *pieces):
        return call(
            kernel,
            "sum_four" if len(pieces) == 4 else "sum_two",
            [shaped(pieces[0].shape, bf16)],
            [],
            1,
            4,
            "v" * len(pieces),
            "v",
            *pieces,
        )[0]

    def ring_trade(cells, flip):
        return lax.ppermute(cells, "rows", [(i, i ^ flip) for i in range(cycle)])

    away, out_pieces, gmix, mine, theirs = lax.optimization_barrier(
        (away, out_pieces, gmix, mine, theirs)
    )
    early, away = halved(early, away)
    away = trade(away, 4)
    got = trade(theirs, 1)
    gimg = call(
        back_images_kernel,
        "back_images",
        [shaped((cycle,) + folded, bf16)],
        [],
        10**10,
        24,
        "pppvv",
        "v",
        img, gmix, gmid, wide, lines,
    )[0]
    got, gimg = lax.optimization_barrier((got, gimg))
    gimg = lax.all_to_all(gimg, "rows", 0, 0, tiled=True)
    early = summed(two_kernel, early, away)
    early = summed(two_kernel, early, ring_trade(early, 1))
    away = ring_trade(early, 2)
    own, *apart = call(
        functools.partial(pair_kernel, DENSE_ROWS),
        "pair",
        [shaped((LATE_ROWS + DENSE_ROWS, LANES), bf16)] * 4,
        [],
        10**6,
        4,
        "vv",
        "vvvv",
        mine, got,
    )
    late = summed(four_kernel, own, *[trade(apart[k], 2 * k + 2) for k in range(3)])
    late = summed(two_kernel, late, ring_trade(late, 1))
    late_away = ring_trade(late, 2)
    output, grad_images = call(
        pictures_kernel,
        "pictures",
        [shaped((cycle, block, features), bf16), shaped((cycle, block, features), f32)],
        [],
        1,
        16,
        "v" * 5,
        "v" * 2,
        *out_pieces, gimg,
    )
    late, output, grad_images = lax.optimization_barrier((late, output, grad_images))
    grads = call(
        finish_kernel,
        "finish",
        [
            shaped((share, 3 * features), f32),
            shaped((share, features), f32),
            shaped((share, hidden), f32),
            shaped((share * pieces, features), f32),
            shaped(gains_main.shape, f32),
            shaped(shifts_main.shape, f32),
            shaped(taps.shape, f32),
            shaped(pool_gains.shape, f32),
            shaped(pool_shifts.shape, f32),
            shaped(rel_height.shape, f32),
            shaped(rel_width.shape, f32),
        ],
        [pltpu.VMEM((SMALL_ROWS, LANES), f32), pltpu.VMEM((DENSE_ROWS, LANES), f32)],
        10**8,
        16,
        "v" * 4,
        "v" * 11,
        early, away, late, late_away,
    )
    grads = list(grads)
    grads[6] = grads[6].transpose(1, 0, 2)
    return (output.reshape(images.shape), grad_images.reshape(images.shape), *grads)

def per_device(images, *rest):
    cycle = lax.axis_size("rows")
    image_count, row_count, cols, _ = images.shape
    fits = image_count == cycle and row_count * cycle == 32 and cols == 32
    return whole_image(images, *rest) if fits else row_sharded(images, *rest)


def solution(mesh):
    return jax.shard_map(
        per_device,
        mesh=mesh,
        in_specs=(
            P("batch", "rows", None, None),
            P("batch", None),
            P("batch", None),
            P("batch", None),
            P("batch", None),
            P(),
            P(),
            P(),
            P(),
            P(),
            P(),
            P(),
            P("batch", "rows", None, None),
        ),
        out_specs=(
            P("batch", "rows", None, None),
            P("batch", "rows", None, None),
            P("batch", None),
            P("batch", None),
            P("batch", None),
            P("batch", None),
            P(),
            P(),
            P(),
            P(),
            P(),
            P(),
            P(),
        ),
        check_vma=False,
    )
```

```python
import functools

import jax
import jax.numpy as jnp
from jax import lax
from jax.experimental import pallas as pl
from jax.experimental.pallas import tpu as pltpu
from jax.sharding import PartitionSpec as P

HEADS = 2
HEAD_DIM = 96


norm_eps = 1e-06
highest = lax.Precision.HIGHEST


def padded(cells, sides, width):
    for axis, dim in sides:
        count = lax.axis_size(axis)
        ends = count - 1
        head = lax.slice_in_dim(cells, 0, width, axis=dim)
        tail = lax.slice_in_dim(cells, cells.shape[dim] - width, cells.shape[dim], axis=dim)
        cells = jnp.concatenate(
            [
                lax.ppermute(tail, axis, [(i, (i + 1) % count) for i in range(ends)]),
                cells,
                lax.ppermute(head, axis, [((i + 1) % count, i) for i in range(ends)]),
            ],
            axis=dim,
        )
    return cells


def layer_norm(values, gains, shifts):
    centre = jnp.mean(values, -1, keepdims=True)
    centred = values - centre
    spread = jnp.mean(centred * centred, -1, keepdims=True)
    return centred * lax.rsqrt(spread + norm_eps) * gains + shifts


def gelu_tanh(values):
    return jax.nn.gelu(values, approximate=True)


def pool_section(section, kernel, stride):
    image_count, ext_rows, col_count, features = section.shape
    out_rows = (ext_rows - 2) // stride
    out_cols = col_count // stride
    col_out = jnp.arange(out_cols)[:, None] * stride
    col_in = jnp.arange(col_count)[None, :]
    shifted = []
    for offset_col in range(3):
        picker = (col_out + offset_col - 1 == col_in).astype(jnp.float32)
        shifted.append(jnp.einsum("jy,bxyc->bxjc", picker, section, precision=highest))
    summed = jnp.zeros((image_count, out_rows, out_cols, features), jnp.float32)
    for offset_row in range(3):
        for offset_col in range(3):
            window = shifted[offset_col][:, offset_row : offset_row + ext_rows - 2]
            if stride == 2:
                window = window.reshape(image_count, out_rows, 2, out_cols, features)[:, :, 0]
            summed = summed + window * kernel[3 * offset_row + offset_col]
    return summed


def pooled_local(extended_f, kernels, gains, shifts):
    features = extended_f.shape[-1]
    head_dim = kernels.shape[-1]
    head_count = features // head_dim
    results = []
    for member, stride in ((0, 1), (1, 2), (2, 2)):
        pooled = pool_section(
            extended_f[member], jnp.tile(kernels[member], (1, head_count)), stride
        )
        pooled = pooled.reshape(pooled.shape[:-1] + (head_count, head_dim))
        offset = (
            shifts[0] if member == 0 else shifts[1] if member == 2 else jnp.zeros_like(shifts[0])
        )
        results.append(layer_norm(pooled, gains[member], offset))
    return tuple(results)


def row_sharded(
    images,
    w_qkv,
    w_proj,
    w_up,
    w_down,
    gains_main,
    shifts_main,
    pool_kernels,
    pool_gains,
    pool_shifts,
    rel_height,
    rel_width,
    cotangent,
):
    image_count, row_count, col_count, features = images.shape
    head_dim = HEAD_DIM
    head_count = HEADS
    scale_factor = head_dim ** (-0.5)
    cycle_size = lax.axis_size("rows")
    key_rows_all = row_count * cycle_size // 2
    key_cols = col_count // 2
    key_total = key_rows_all * key_cols
    query_count = row_count * col_count
    key_local = row_count // 2 * key_cols
    gain_rows = gains_main.astype(jnp.float32)
    shift_rows = shifts_main.astype(jnp.float32)
    full_qkv, full_proj, full_up, full_down = (
        lax.all_gather(w_qkv, "batch", axis=0, tiled=True),
        lax.all_gather(w_proj, "batch", axis=0, tiled=True),
        lax.all_gather(w_up, "batch", axis=0, tiled=True),
        lax.all_gather(w_down, "batch", axis=0, tiled=True),
    )
    qkv_split = full_qkv.reshape(features, 3, features)
    inputs_f = images.astype(jnp.float32)
    normed_one, norm_one_pullback = jax.vjp(layer_norm, inputs_f, gain_rows[0], shift_rows[0])
    normed_low = normed_one.astype(jnp.bfloat16)
    mixed = (
        jnp.einsum("bxyd,dme->mbxye", normed_low, qkv_split, preferred_element_type=jnp.float32)
        + shift_rows[2:5][:, None, None, None, :]
    )
    mixed_low = mixed.astype(jnp.bfloat16)
    extended = padded(mixed_low, (("rows", 2),), 1)
    (queries, keys_pooled, values_pooled), pool_pullback = jax.vjp(
        pooled_local,
        extended.astype(jnp.float32),
        pool_kernels.astype(jnp.float32),
        pool_gains.astype(jnp.float32),
        pool_shifts.astype(jnp.float32),
    )
    queries_low = queries.astype(jnp.bfloat16)
    query_flat = queries_low.reshape(image_count, query_count, head_count, head_dim)
    keys_low = keys_pooled.astype(jnp.bfloat16).reshape(image_count, key_local, features)
    values_low = values_pooled.astype(jnp.bfloat16).reshape(image_count, key_local, features)
    key_value = jnp.concatenate([keys_low, values_low], -1)
    first_row = lax.axis_index("rows") * row_count

    def rel_terms(query_vals, table_height, table_width):
        row_place = first_row + jnp.arange(row_count)
        dist_height = (
            row_place[:, None] - 2 * jnp.arange(key_rows_all)[None, :] + 2 * (key_rows_all - 1)
        )
        pick_height = (
            dist_height[:, :, None] == jnp.arange(table_height.shape[0])[None, None, :]
        ).astype(jnp.float32)
        lookup_height = jnp.einsum("xjt,tc->xjc", pick_height, table_height, precision=highest)
        dist_width = (
            jnp.arange(col_count)[:, None] - 2 * jnp.arange(key_cols)[None, :] + 2 * (key_cols - 1)
        )
        pick_width = (
            dist_width[:, :, None] == jnp.arange(table_width.shape[0])[None, None, :]
        ).astype(jnp.float32)
        lookup_width = jnp.einsum("yjt,tc->yjc", pick_width, table_width, precision=highest)
        term_height = jnp.einsum("bxyhc,xjc->bhxyj", query_vals, lookup_height, precision=highest)
        term_width = jnp.einsum("bxyhc,yjc->bhxyj", query_vals, lookup_width, precision=highest)
        return (term_height, term_width)

    (term_height, term_width), rel_pullback = jax.vjp(
        rel_terms,
        queries_low.astype(jnp.float32),
        rel_height.astype(jnp.float32),
        rel_width.astype(jnp.float32),
    )
    rel_full = (term_height[..., :, None] + term_width[..., None, :]).reshape(
        image_count, head_count, query_count, key_total
    )

    def key_scores(key_piece):
        piece_rows = key_piece.shape[1]
        keys_part = key_piece[..., :features].reshape(image_count, piece_rows, head_count, head_dim)
        products = jnp.einsum(
            "bqhc,bkhc->bhqk", query_flat, keys_part, preferred_element_type=jnp.float32
        )
        return products * scale_factor + lax.slice_in_dim(rel_full, 0, piece_rows, axis=3)

    key_piece = lax.all_gather(key_value, "rows", axis=1, tiled=True)
    run_max = jnp.full((image_count, head_count, query_count), -1e30, jnp.float32)
    run_sum = jnp.zeros((image_count, head_count, query_count), jnp.float32)
    run_acc = jnp.zeros((image_count, head_count, query_count, head_dim), jnp.float32)
    piece_rows = key_piece.shape[1]
    values_part = key_piece[..., features:].reshape(image_count, piece_rows, head_count, head_dim)
    scores = key_scores(key_piece)
    new_max = jnp.maximum(run_max, jnp.max(scores, -1))
    weights_exp = jnp.exp(scores - new_max[..., None])
    factor = jnp.exp(run_max - new_max)
    run_sum = run_sum * factor + jnp.sum(weights_exp, -1)
    run_acc = run_acc * factor[..., None] + jnp.einsum(
        "bhqk,bkhc->bhqc", weights_exp, values_part.astype(jnp.float32), precision=highest
    )
    run_max, run_sum, run_acc = (new_max, run_sum, run_acc)
    log_total = run_max + jnp.log(run_sum)
    attended = (run_acc / run_sum[..., None]).transpose(0, 2, 1, 3) + query_flat.astype(jnp.float32)
    attended_low = attended.reshape(image_count, row_count, col_count, features).astype(
        jnp.bfloat16
    )
    branch = (
        jnp.einsum("bxyd,de->bxye", attended_low, full_proj, preferred_element_type=jnp.float32)
        + shift_rows[5]
    )
    middle = inputs_f + branch
    normed_two, norm_two_pullback = jax.vjp(layer_norm, middle, gain_rows[1], shift_rows[1])
    normed_two_low = normed_two.astype(jnp.bfloat16)
    hidden = jnp.einsum(
        "bxyd,df->bxyf", normed_two_low, full_up, preferred_element_type=jnp.float32
    ) + shift_rows[6:-1].reshape(-1)
    activated, gelu_pullback = jax.vjp(gelu_tanh, hidden)
    activated_low = activated.astype(jnp.bfloat16)
    output = (
        middle
        + jnp.einsum("bxyf,fd->bxyd", activated_low, full_down, preferred_element_type=jnp.float32)
        + shift_rows[-1]
    )
    output_low = output.astype(jnp.bfloat16)
    upstream = cotangent.astype(jnp.float32)
    grad_down = jnp.einsum(
        "bxyf,bxyd->fd", activated_low, cotangent, preferred_element_type=jnp.float32
    )
    grad_shift_down = jnp.sum(upstream, (0, 1, 2))
    grad_activated = jnp.einsum(
        "bxyd,fd->bxyf", cotangent, full_down, preferred_element_type=jnp.float32
    )
    (grad_hidden,) = gelu_pullback(grad_activated)
    grad_hidden_low = grad_hidden.astype(jnp.bfloat16)
    grad_up = jnp.einsum(
        "bxyd,bxyf->df", normed_two_low, grad_hidden_low, preferred_element_type=jnp.float32
    )
    grad_shift_up = jnp.sum(grad_hidden_low.astype(jnp.float32), (0, 1, 2))
    grad_normed_two = jnp.einsum(
        "bxyf,df->bxyd", grad_hidden_low, full_up, preferred_element_type=jnp.float32
    )
    grad_middle_norm, grad_gain_two, grad_shift_two = norm_two_pullback(grad_normed_two)
    grad_middle = upstream + grad_middle_norm
    grad_branch_low = grad_middle.astype(jnp.bfloat16)
    grad_proj = jnp.einsum(
        "bxyd,bxye->de", attended_low, grad_branch_low, preferred_element_type=jnp.float32
    )
    grad_shift_proj = jnp.sum(grad_branch_low.astype(jnp.float32), (0, 1, 2))
    grad_attended = jnp.einsum(
        "bxye,de->bxyd", grad_branch_low, full_proj, preferred_element_type=jnp.float32
    )
    grad_flat = grad_attended.astype(jnp.bfloat16).reshape(
        image_count, query_count, head_count, head_dim
    )
    grad_flat_f = grad_flat.astype(jnp.float32)
    key_value_all = lax.all_gather(key_value, "rows", axis=1, tiled=True)
    scores = key_scores(key_value_all)
    soft = jnp.exp(scores - log_total[..., None])
    keys_all = key_value_all[..., :features].reshape(image_count, key_total, head_count, head_dim)
    values_all = key_value_all[..., features:].reshape(image_count, key_total, head_count, head_dim)
    grad_soft = jnp.einsum(
        "bqhc,bkhc->bhqk", grad_flat, values_all, preferred_element_type=jnp.float32
    )
    row_dot = jnp.sum(soft * grad_soft, -1, keepdims=True)
    grad_scores = (soft * (grad_soft - row_dot)).astype(jnp.bfloat16)
    grad_queries = (
        scale_factor
        * jnp.einsum("bhqk,bkhc->bqhc", grad_scores, keys_all, preferred_element_type=jnp.float32)
        + grad_flat_f
    )
    grad_scores_f = grad_scores.astype(jnp.float32).reshape(
        image_count, head_count, row_count, col_count, key_rows_all, key_cols
    )
    grad_query_rel, grad_rel_h, grad_rel_w = rel_pullback(
        (jnp.sum(grad_scores_f, -1), jnp.sum(grad_scores_f, -2))
    )
    grad_queries = (
        grad_queries.reshape(image_count, row_count, col_count, head_count, head_dim)
        + grad_query_rel
    )
    key_span = key_local * lax.axis_size("rows")
    part_scores = lax.slice_in_dim(grad_scores, 0, key_span, axis=3)
    part_soft = lax.slice_in_dim(soft, 0, key_span, axis=3)
    grad_keys_part = scale_factor * jnp.einsum(
        "bhqk,bqhc->kbhc", part_scores, query_flat, preferred_element_type=jnp.float32
    )
    grad_values_part = jnp.einsum("bhqk,bqhc->kbhc", part_soft, grad_flat_f, precision=highest)
    key_grads = (
        lax.psum_scatter(
            jnp.concatenate(
                [
                    grad_keys_part.reshape(key_span, image_count, features),
                    grad_values_part.reshape(key_span, image_count, features),
                ],
                -1,
            ).astype(jnp.bfloat16),
            "rows",
            scatter_dimension=0,
            tiled=True,
        )
        .astype(jnp.float32)
        .transpose(1, 0, 2)
    )
    grad_keys = key_grads[..., :features].reshape(
        image_count, row_count // 2, key_cols, head_count, head_dim
    )
    grad_values = key_grads[..., features:].reshape(
        image_count, row_count // 2, key_cols, head_count, head_dim
    )
    grad_extended, grad_kernels, grad_pool_gain, grad_pool_shift = pool_pullback(
        (grad_queries, grad_keys, grad_values)
    )
    rims = jnp.concatenate([grad_extended[:, :, :1], grad_extended[:, :, -1:]], 2)
    rims_all = padded(rims.astype(jnp.bfloat16), (("rows", 2),), 1).astype(rims.dtype)
    grad_mixed = grad_extended[:, :, 1:-1]
    grad_mixed = grad_mixed.at[:, :, 0].add(rims_all[:, :, 0]).at[:, :, -1].add(rims_all[:, :, 3])
    grad_mixed_low = grad_mixed.astype(jnp.bfloat16)
    grad_qkv = jnp.einsum(
        "bxyd,mbxye->dme", normed_low, grad_mixed_low, preferred_element_type=jnp.float32
    ).reshape(features, 3 * features)
    grad_shift_qkv = jnp.sum(grad_mixed_low.astype(jnp.float32), (1, 2, 3))
    grad_normed_one = jnp.einsum(
        "mbxye,dme->bxyd", grad_mixed_low, qkv_split, preferred_element_type=jnp.float32
    )
    grad_inputs_norm, grad_gain_one, grad_shift_one = norm_one_pullback(grad_normed_one)
    grad_images = grad_middle + grad_inputs_norm
    grad_gains = jnp.stack([grad_gain_one, grad_gain_two])
    grad_shifts = jnp.concatenate(
        [
            grad_shift_one[None],
            grad_shift_two[None],
            grad_shift_qkv,
            grad_shift_proj[None],
            grad_shift_up.reshape(-1, features),
            grad_shift_down[None],
        ],
        0,
    )
    small_summed = lax.psum(
        (
            grad_gains,
            grad_shifts,
            grad_kernels,
            grad_pool_gain,
            grad_pool_shift,
            grad_rel_h,
            grad_rel_w,
        ),
        ("batch", "rows"),
    )
    matrix_grads = (grad_qkv, grad_proj, grad_up, grad_down)
    summed_rows = (
        lax.psum(matrix_grads[0].astype(jnp.bfloat16), "rows").astype(jnp.float32),
        lax.psum(matrix_grads[1].astype(jnp.bfloat16), "rows").astype(jnp.float32),
        lax.psum(matrix_grads[2].astype(jnp.bfloat16), "rows").astype(jnp.float32),
        lax.psum(matrix_grads[3].astype(jnp.bfloat16), "rows").astype(jnp.float32),
    )
    owned = (
        lax.psum_scatter(
            summed_rows[0].astype(jnp.bfloat16), "batch", scatter_dimension=0, tiled=True
        ).astype(jnp.float32),
        lax.psum_scatter(
            summed_rows[1].astype(jnp.bfloat16), "batch", scatter_dimension=0, tiled=True
        ).astype(jnp.float32),
        lax.psum_scatter(
            summed_rows[2].astype(jnp.bfloat16), "batch", scatter_dimension=0, tiled=True
        ).astype(jnp.float32),
        lax.psum_scatter(
            summed_rows[3].astype(jnp.bfloat16), "batch", scatter_dimension=0, tiled=True
        ).astype(jnp.float32),
    )
    return (
        output_low,
        grad_images,
        owned[0],
        owned[1],
        owned[2],
        owned[3],
        small_summed[0],
        small_summed[1],
        small_summed[2],
        small_summed[3],
        small_summed[4],
        small_summed[5],
        small_summed[6],
    )


LANES = 128
NT = (((1,), (1,)), ((), ()))
TN = (((0,), (0,)), ((), ()))
NN = (((1,), (0,)), ((), ()))
f32 = jnp.float32
bf16 = jnp.bfloat16


def dot(a, b, dims=NN):
    return lax.dot_general(a, b, dims, preferred_element_type=f32)


def lane_ids(shape):
    return lax.broadcasted_iota(jnp.int32, shape, len(shape) - 1)


def head_mask(rows):
    return (lane_ids((rows, LANES)) < HEAD_DIM).astype(f32)


def head_piece(values, start):
    base = start // LANES * LANES
    move = start - base
    if move == 0:
        piece = values[:, base : base + LANES]
    else:
        piece = pltpu.roll(values[:, base : base + 2 * LANES], 2 * LANES - move, 1)[:, :LANES]
    return piece * head_mask(values.shape[0])


def norm_parts(values, count):
    centre = jnp.sum(values, -1, keepdims=True) * (1.0 / count)
    centred = values - centre
    spread = jnp.sum(centred * centred, -1, keepdims=True) * (1.0 / count)
    scale = lax.rsqrt(spread + norm_eps)
    return centred * scale, scale


def head_norm_parts(values, mask):
    centre = jnp.sum(values, -1, keepdims=True) * (1.0 / HEAD_DIM)
    centred = (values - centre) * mask
    spread = jnp.sum(centred * centred, -1, keepdims=True) * (1.0 / HEAD_DIM)
    scale = lax.rsqrt(spread + norm_eps)
    return centred * scale, scale


def norm_back(grad, unit, scale, count):
    first = jnp.sum(grad, -1, keepdims=True) * (1.0 / count)
    second = jnp.sum(grad * unit, -1, keepdims=True) * (1.0 / count)
    return scale * (grad - first - unit * second)


def fold_rows(values):
    rows, lanes = values.shape
    return jnp.sum(values.reshape(rows // 8, 8, lanes), 0)


def fold_block(values):
    rows = values.shape[0]
    tail = values[:, LANES : LANES + 64].astype(f32)
    tail = jnp.concatenate([tail, jnp.zeros_like(tail)], 1)
    side = tail[: rows // 2] + pltpu.roll(tail[rows // 2 :], 64, 1)
    return jnp.concatenate([values[:, :LANES].astype(bf16), side.astype(bf16)], 0)


def unfold_block(folded):
    rows = folded.shape[0] * 2 // 3
    side = folded[rows:].astype(f32)
    tail = jnp.concatenate([side, pltpu.roll(side, 64, 1)], 0).astype(folded.dtype)
    return jnp.concatenate([folded[:rows], tail[:, :64]], 1)


def turned(shift):
    return lax.rem(lax.axis_index("rows") + shift, 4)


def copy_all(pairs, sems):
    copies = []
    for near, far in pairs:
        copies.append(pltpu.make_async_copy(near, far, sems.at[len(copies)]))
        copies[-1].start()
    return copies


def wait_all(copies):
    for copy in copies:
        copy.wait()


def pack_kernel(qkv_ref, proj_ref, up_ref, down_ref, packed_ref, qkv_in, proj_in, up_in, down_in, sems):
    wait_all(
        copy_all(
            [(qkv_ref, qkv_in), (proj_ref, proj_in), (up_ref, up_in), (down_ref, down_in)], sems
        )
    )
    share = qkv_in.shape[0]
    packed_ref[...] = jnp.concatenate(
        [qkv_in[...].astype(f32), proj_in[...].astype(f32), up_in[...].astype(f32)]
        + [
            down_in[...].astype(f32)[share * i : share * (i + 1)]
            for i in range(down_in.shape[0] // share)
        ],
        1,
    ).astype(bf16)


def fold_images_kernel(img_ref, out_ref, img_in, sems):
    loads = copy_all([(img_ref.at[k], img_in.at[k]) for k in range(4)], sems)
    for block in range(4):
        loads[block].wait()
        out_ref[block] = fold_block(img_in[block])


def fold_kernel(cot_ref, cot_0, cot_1, cot_2, cot_3, cot_in, cot_scr, in_sems, sems):
    loads = copy_all([(cot_ref.at[turned(k)], cot_in.at[k]) for k in range(4)], in_sems)
    copies = []
    for shift, far in enumerate((cot_0, cot_1, cot_2, cot_3)):
        loads[shift].wait()
        cot_scr[shift] = fold_block(cot_in[shift])
        copies.append(pltpu.make_async_copy(cot_scr.at[shift], far, sems.at[shift]))
        copies[-1].start()
    wait_all(copies)


def flipped(flip):
    place = lax.axis_index("batch")
    owner = place
    for bit in (1, 2, 4):
        if flip & bit:
            owner = owner + bit - 2 * bit * lax.rem(place // bit, 2)
    return owner


def gather_rows(own_ref, other_ref, first, last, full_scr):
    share = own_ref.shape[1]
    for flip in range(8):
        source = other_ref if flip & 1 else own_ref
        rows = pl.ds(pl.multiple_of(flipped(flip) * share, 8), share)
        full_scr[rows, :] = source[flip // 2, :, first:last].astype(f32)


def load_taps(kernel_ref, kernel_scr):
    kernel_scr[...] = jnp.zeros_like(kernel_scr)
    for tap in range(9):
        kernel_scr[tap, 0:3, 0:HEAD_DIM] = kernel_ref[tap].astype(f32)


def load_gains(gain_ref, shift_ref, gain_scr):
    gain_scr[...] = jnp.zeros_like(gain_scr)
    gain_scr[0:3, 0:HEAD_DIM] = gain_ref[...].astype(f32)
    gain_scr[3:5, 0:HEAD_DIM] = shift_ref[...].astype(f32)


def clear_rim(padded_scr):
    rows, cols, lanes = padded_scr.shape[-3:]
    for place in range(padded_scr.shape[0] if len(padded_scr.shape) == 4 else 1):
        cells = padded_scr.at[place] if len(padded_scr.shape) == 4 else padded_scr
        cells[0:1] = jnp.zeros((1, cols, lanes), f32)
        cells[rows - 1 : rows] = jnp.zeros((1, cols, lanes), f32)
        cells[:, 0:8, :] = jnp.zeros((rows, 8, lanes), f32)
        cells[:, cols - 8 : cols, :] = jnp.zeros((rows, 8, lanes), f32)


CHUNK_ROWS = 4
POOL_ROWS = 8
MIX_ROWS = 32
ATTEND_ROWS = 32
BACK_ROWS = 32
WEIGH_TILE = 1024
IMAGE_TILE = 1024
LOG2_E = 1.4426950408889634


def stride_windows(padded, place, side, key_rows, key_cols):
    columns = pl.ds(7 + side, key_cols, stride=2)
    even = padded[place, pl.ds(0, key_rows + 1, stride=2), columns, :]
    odd = padded[place, pl.ds(1, key_rows, stride=2), columns, :]
    return even[:key_rows], odd, even[1:]


def attend_kernel(
    stage, weight_scr, bias_ref, rows_ref, kern_scr, gain_scr, table_ref,
    img_ref, norm_out, padded, qunit_out, qscale_out, kvraw_out, soft_out, att_out, key_out, val_out,
    query_scr, keyaug_scr,
):
    cols = padded.shape[2] - 16
    rows = padded.shape[1] - 2
    tile = POOL_ROWS * cols
    chunks = rows // POOL_ROWS
    key_cols = cols // 2
    key_rows = rows // 2
    key_total = key_rows * key_cols
    features = img_ref.shape[1]
    clear_rim(padded)
    gain_one = rows_ref[16:17, 0:features]
    shift_one = rows_ref[0:1, 0:features]
    table = table_ref[...]

    mix_tile = MIX_ROWS * cols

    img_ref[...] = jnp.concatenate(
        [unfold_block(stage[place]) for place in range(4)], 0
    )

    def mix(step, carry):
        span = pl.ds(pl.multiple_of(step * mix_tile, mix_tile), mix_tile)
        unit, _ = norm_parts(img_ref[span, :].astype(f32), features)
        norm_out[span, :] = unit.astype(bf16)
        normed = (unit * gain_one + shift_one).astype(bf16)
        mixed = dot(normed, weight_scr[...]) + bias_ref[0:1, :]
        for place in range(3 * HEADS):
            low = mixed[:, place * LANES : (place + 1) * LANES].astype(bf16)
            padded[place, pl.ds(1 + step * MIX_ROWS, MIX_ROWS), 8 : 8 + cols, :] = low.astype(
                f32
            ).reshape(MIX_ROWS, cols, LANES)
        return carry

    lax.fori_loop(0, rows // MIX_ROWS, mix, 0, unroll=True)

    tile_mask = head_mask(tile)

    def pool_queries(step, carry):
        span = pl.ds(pl.multiple_of(step * tile, tile), tile)
        for head in range(HEADS):
            total = jnp.zeros((POOL_ROWS, cols, LANES), f32)
            for side in range(3):
                window = padded[
                    head, pl.ds(step * POOL_ROWS, POOL_ROWS + 2), 7 + side : 7 + side + cols, :
                ]
                for up in range(3):
                    total = total + window[up : up + POOL_ROWS] * kern_scr[3 * up + side, 0:1, :]
            unit, scale = head_norm_parts(total.reshape(tile, LANES), tile_mask)
            qunit_out[head, span, :] = unit
            qscale_out[head, span, :] = jnp.broadcast_to(scale, (tile, LANES))
            query_scr[head, span, :] = (unit * gain_scr[0:1, :] + gain_scr[3:4, :]).astype(bf16)
        return carry

    lax.fori_loop(0, chunks, pool_queries, 0, unroll=True)

    for place in range(2 * HEADS):
        member = 1 + place // HEADS
        total = jnp.zeros((key_rows, key_cols, LANES), f32)
        for side in range(3):
            for up, window in enumerate(stride_windows(padded, HEADS + place, side, key_rows, key_cols)):
                total = total + window * kern_scr[3 * up + side, member : member + 1, :]
        kvraw_out[place] = total.reshape(key_total, LANES)

    key_mask = head_mask(key_total)
    key_place = lax.broadcasted_iota(jnp.int32, (key_total, LANES), 0)
    lanes = lane_ids((key_total, LANES))
    from_row = 30 - 2 * (key_place // key_cols)
    from_col = 96 + 2 * (key_place % key_cols)
    hot = (
        (lanes == from_row)
        | (lanes == from_row + 64)
        | (lanes == from_col)
        | (lanes == from_col - 64)
    ).astype(bf16)
    for head in range(HEADS):
        unit, _ = head_norm_parts(kvraw_out[head], key_mask)
        low = (unit * gain_scr[1:2, :]).astype(bf16)
        key_out[head] = low
        keyaug_scr[head, :, 0:LANES] = low
        keyaug_scr[head, :, LANES : 2 * LANES] = hot
        unit, _ = head_norm_parts(kvraw_out[HEADS + head], key_mask)
        val_out[head] = (unit * gain_scr[2:3, :] + gain_scr[4:5, :]).astype(bf16)

    scale_factor = HEAD_DIM ** (-0.5)
    row_lanes = lane_ids((cols, LANES))
    part_tile = ATTEND_ROWS * cols
    part_lanes = lane_ids((part_tile, LANES))

    def attend(step, carry):
        span = pl.ds(pl.multiple_of(step * part_tile, part_tile), part_tile)
        for head in range(HEADS):
            query = query_scr[head, span, :]
            looked = dot(query, table, NT) * (1.0 / scale_factor)
            pieces = []
            for row in range(ATTEND_ROWS):
                part = looked[row * cols : (row + 1) * cols, :]
                place = step * ATTEND_ROWS + row
                by_row = pltpu.roll(part, LANES - place, 1)
                by_col = pltpu.roll(part, 0, 1, stride=1, stride_axis=0)
                pieces.append(jnp.where(row_lanes < 64, by_row, by_col))
            terms = jnp.concatenate(pieces, 0)
            high = terms.astype(bf16).astype(f32)
            rest = pltpu.roll(terms - high, 64, 1)
            both = jnp.where((part_lanes < 32) | (part_lanes >= 96), high, rest).astype(bf16)
            scores = dot(jnp.concatenate([query, both], 1), keyaug_scr[head], NT)
            top = jnp.max(scores, -1, keepdims=True)
            powers = jnp.exp2((scores - top) * (scale_factor * LOG2_E))
            soft = (powers * (1.0 / jnp.sum(powers, -1, keepdims=True))).astype(bf16)
            soft_out[head, span, :] = soft
            att = dot(soft, val_out[head]) + query.astype(f32)
            att_out[span, head * LANES : (head + 1) * LANES] = att.astype(bf16)
        return carry

    lax.fori_loop(0, rows // ATTEND_ROWS, attend, 0, unroll=True)


def stack_blocks(values, block_scr):
    owners = block_scr.shape[0]
    share = values.shape[0] // owners
    for block in range(values.shape[1] // LANES):
        for owner in range(owners):
            block_scr[owner, share * block : share * (block + 1), :] = values[
                share * owner : share * (owner + 1), block * LANES : (block + 1) * LANES
            ]


def split_owners(block_scr, mine_ref, theirs_ref, order):
    count = block_scr.shape[1]
    for place, flip in enumerate(order):
        span = pl.ds(place * count, count)
        mine_ref[span, :] = block_scr[flipped(flip)].astype(bf16)
        theirs_ref[span, :] = block_scr[flipped(flip + 1)].astype(bf16)


def weights_kernel(
    owners, own_ref, other_ref, gains_far, shifts_far, kern_far, pgain_far, pshift_far, relh_far, relw_far,
    wide_ref, proj_ref, up_ref, down_ref, bias_ref, rows_ref, columns_ref, taps_ref, pool_ref, ahead_ref, behind_ref,
    full_scr, down_scr, gains_in, shifts_in, kern_in, pgain_in, pshift_in, relh_in, relw_in, table_scr, sems,
):
    loads = copy_all(
        [
            (gains_far, gains_in), (shifts_far, shifts_in), (kern_far, kern_in), (pgain_far, pgain_in),
            (pshift_far, pshift_in), (relh_far, relh_in), (relw_far, relw_in),
        ],
        sems,
    )
    gather_rows(own_ref, other_ref, 0, own_ref.shape[2], full_scr)
    for place in range(3 * HEADS):
        wide_ref[:, place * LANES : (place + 1) * LANES] = head_piece(
            full_scr[:, 0 : 5 * LANES], place * HEAD_DIM
        ).astype(bf16)
    features, hidden_count = up_ref.shape
    proj = pltpu.roll(full_scr[:, 4 * LANES : 6 * LANES], 192, 1)[:, 0:features]
    gap = jnp.zeros((LANES - HEAD_DIM, features), f32)
    proj_ref[...] = jnp.concatenate(
        [proj[0:HEAD_DIM, :], gap, proj[HEAD_DIM : 2 * HEAD_DIM, :], gap], 0
    ).astype(bf16)
    up_ref[...] = full_scr[:, 4 * features : 4 * features + hidden_count].astype(bf16)
    columns = full_scr[:, 4 * features + hidden_count :]
    share = features // owners
    pieces = hidden_count // features
    for piece in range(pieces):
        start = piece * features
        base = start // LANES * LANES
        window = columns[:, base : base + 2 * LANES]
        if start != base:
            window = pltpu.roll(window, 2 * LANES - (start - base), 1)
        for owner in range(owners):
            place = owner * share * pieces + piece * share
            down_scr[place : place + share, :] = window[
                owner * share : (owner + 1) * share, 0:features
            ]
    down_ref[...] = down_scr[...].astype(bf16)
    wait_all(loads)
    rows_ref[...] = jnp.zeros_like(rows_ref)
    rows_ref[0 : shifts_in.shape[0], 0:features] = shifts_in[...].astype(f32)
    rows_ref[16:18, 0:features] = gains_in[...].astype(f32)
    columns_ref[...] = jnp.concatenate(
        [rows_ref[...], jnp.zeros((LANES - rows_ref.shape[0], 2 * LANES), f32)], 0
    ).T
    bias_ref[...] = jnp.zeros_like(bias_ref)
    for section in range(3):
        for head in range(HEADS):
            place = (section * HEADS + head) * LANES
            bias_ref[0:1, place : place + LANES] = head_piece(
                rows_ref[2 + section : 3 + section, :], head * HEAD_DIM
            )
    for piece in range(pieces):
        bias_ref[1:2, piece * features : (piece + 1) * features] = rows_ref[
            6 + piece : 7 + piece, 0:features
        ]
    load_taps(kern_in, taps_ref)
    load_gains(pgain_in, pshift_in, pool_ref)
    count = relw_in.shape[0]
    table_scr[...] = jnp.zeros_like(table_scr)
    table_scr[0:count, 0:HEAD_DIM] = relh_in[...].astype(f32)
    table_scr[64 : 64 + count, 0:HEAD_DIM] = relw_in[...].astype(f32)
    behind_ref[...] = table_scr[...].astype(bf16)
    flip = (
        lax.broadcasted_iota(jnp.int32, (64, count), 0) + lax.broadcasted_iota(jnp.int32, (64, count), 1)
        == count - 1
    ).astype(bf16)
    table_scr[64:128, 0:HEAD_DIM] = dot(flip, relw_in[...])
    ahead_ref[...] = table_scr[...].astype(bf16)


def send_turned(near, fars, sems):
    sends = []
    for shift, far in enumerate(fars):
        sends.append(pltpu.make_async_copy(near.at[turned(shift)], far, sems.at[shift]))
        sends[-1].start()
    return sends


GELU_A = 0.7978845608028654
GELU_B = 0.044715


def feed_ahead_kernel(
    img_ref, att_ref, proj_ref, up_ref, down_ref, bias_ref, rows_ref,
    out_0, out_1, out_2, out_3, normed_ref, unit_ref, scale_ref, active_ref, slope_ref,
    out_stage, turn_sems,
):
    tokens, features = img_ref.shape
    pieces = up_ref.shape[1] // features
    block = tokens // 4
    middle = img_ref[...].astype(f32) + (dot(att_ref[...], proj_ref[...]) + rows_ref[5:6, 0:features])
    unit, scale = norm_parts(middle, features)
    normed = (unit * rows_ref[17:18, 0:features] + rows_ref[1:2, 0:features]).astype(bf16)
    unit_ref[...] = unit
    scale_ref[...] = jnp.broadcast_to(scale, scale_ref.shape)
    normed_ref[...] = normed
    hidden = dot(normed, up_ref[...]) + bias_ref[1:2, :]
    square = hidden * hidden
    wave = jnp.tanh(hidden * (GELU_A + (GELU_A * GELU_B) * square))
    half = 0.5 + 0.5 * wave
    active = (hidden * half).astype(bf16)
    active_ref[...] = active
    slope_ref[...] = half * (
        1.0 + (1.0 - half) * (hidden * (2.0 * GELU_A + (6.0 * GELU_A * GELU_B) * square))
    )
    out = middle + dot(active, down_ref[...]) + rows_ref[6 + pieces : 7 + pieces, 0:features]
    for place in range(4):
        out_stage[place] = fold_block(out[place * block : (place + 1) * block, :])
    wait_all(send_turned(out_stage, (out_0, out_1, out_2, out_3), turn_sems))


def feed_back_kernel(
    owners,
    att_ref, cot_0, cot_1, cot_2, cot_3, normed_ref, unit_ref, scale_ref, active_ref, slope_ref,
    proj_ref, up_ref, down_ref, rows_ref,
    mid_ref, gatt_ref, mine_ref, theirs_ref,
    gdown, gup, gproj, gbias, gsmall, block_scr, cot_stage, cot_sems,
):
    cot_loads = copy_all(
        [(piece, cot_stage.at[turned(4 - k)]) for k, piece in enumerate((cot_0, cot_1, cot_2, cot_3))],
        cot_sems,
    )
    tokens, features = unit_ref.shape
    hidden_count = up_ref.shape[1]
    pieces = hidden_count // features
    unit = unit_ref[...]
    att = att_ref[...]
    wait_all(cot_loads)
    cot_low = jnp.concatenate([unfold_block(cot_stage[place]) for place in range(4)], 0)
    cot = cot_low.astype(f32)
    gdown[...] = dot(cot_low, active_ref[...], TN)
    gact = dot(cot_low, down_ref[...], NT)
    ghid = (gact * slope_ref[...]).astype(bf16)
    gup[...] = dot(normed_ref[...], ghid, TN)
    gbias[...] = fold_rows(ghid.astype(f32))
    gnorm = dot(ghid, up_ref[...], NT)
    gsmall[0:8, :] = fold_rows(gnorm * unit)
    gsmall[8:16, :] = fold_rows(gnorm)
    gmid = cot + norm_back(gnorm * rows_ref[17:18, 0:features], unit, scale_ref[...], features)
    gbranch = gmid.astype(bf16)
    mid_ref[...] = gbranch
    gsmall[16:24, :] = fold_rows(gbranch.astype(f32))
    gsmall[24:32, :] = fold_rows(cot)
    gproj[...] = dot(att, gbranch, TN)
    gatt_ref[...] = dot(gbranch, proj_ref[...], NT).astype(bf16)

    share = features // owners
    proj = jnp.concatenate(
        [gproj[head * LANES : head * LANES + HEAD_DIM, :] for head in range(HEADS)], 0
    )
    down = gdown[...].T
    down_pieces = []
    for piece in range(pieces):
        down_pieces.append(
            jnp.concatenate(
                [
                    down[
                        owner * share * pieces + piece * share : owner * share * pieces
                        + (piece + 1) * share,
                        :,
                    ]
                    for owner in range(owners)
                ],
                0,
            )
        )
    sums = [jnp.sum(gsmall[8 * i : 8 * i + 8, :], 0, keepdims=True) for i in range(4)]
    bias_row = jnp.sum(gbias[...], 0, keepdims=True)
    block = jnp.concatenate(
        sums + [bias_row[:, i * features : (i + 1) * features] for i in range(pieces)], 0
    )
    block = jnp.concatenate([block, jnp.zeros((share - 8, features), f32)], 0)
    small = jnp.concatenate([block] * owners, 0)
    block_scr[...] = jnp.zeros_like(block_scr)
    stack_blocks(jnp.concatenate([proj, gup[...]] + down_pieces + [small], 1), block_scr)
    split_owners(block_scr, mine_ref, theirs_ref, (0, 4, 2, 6))


SMALL_ROWS = 168
DENSE_ROWS = 128
LATE_ROWS = 128


def back_attend_kernel(
    head, qunit_ref, qscale_ref, kvraw_ref, soft_ref, gatt_ref, key_ref, val_ref,
    gain_scr, table_ref,
    gpadded, gkeypad, sums_ref,
    keyaug_scr, gtable, gkey, gval, gsums,
):
    cols = gpadded.shape[1] - 16
    rows = gpadded.shape[0] - 2
    tile = BACK_ROWS * cols
    chunks = rows // BACK_ROWS
    key_cols = cols // 2
    key_rows = rows // 2
    key_total = kvraw_ref.shape[1]
    clear_rim(gpadded)
    gkeypad[...] = jnp.zeros_like(gkeypad)
    table = table_ref[...]
    gsums[...] = jnp.zeros_like(gsums)

    key_place = lax.broadcasted_iota(jnp.int32, (key_total, LANES), 0)
    lanes = lane_ids((key_total, LANES))
    hot = (
        (lanes == 30 - 2 * (key_place // key_cols)) | (lanes == 94 - 2 * (key_place % key_cols))
    ).astype(bf16)
    keyaug_scr[:, 0:LANES] = key_ref[head]
    keyaug_scr[:, LANES : 2 * LANES] = hot

    scale_factor = HEAD_DIM ** (-0.5)
    tile_mask = head_mask(tile)
    row_lanes = lane_ids((cols, LANES))

    def attend(step, carry):
        span = pl.ds(pl.multiple_of(step * tile, tile), tile)
        unit, scale = qunit_ref[head, span, :], qscale_ref[head, span, :]
        query = (unit * gain_scr[0:1, :] + gain_scr[3:4, :]).astype(bf16)
        gatt = gatt_ref[span, head * LANES : (head + 1) * LANES]
        soft_low = soft_ref[head, span, :]
        soft = soft_low.astype(f32)
        gsoft = dot(gatt, val_ref[head], NT)
        inner = jnp.sum(soft * gsoft, -1, keepdims=True)
        gscore = (soft * (gsoft - inner)).astype(bf16)
        gkey[...] = dot(query, gscore, TN)
        gval[...] = dot(gatt, soft_low, TN)
        wide = dot(gscore, keyaug_scr[...])
        gterm = wide[:, LANES : 2 * LANES]
        pieces = []
        for row in range(BACK_ROWS):
            part = gterm[row * cols : (row + 1) * cols, :]
            place = step * BACK_ROWS + row
            by_row = pltpu.roll(part, place, 1)
            by_col = pltpu.roll(part, 0, 1, stride=1, stride_axis=0)
            pieces.append(jnp.where(row_lanes < 64, by_row, by_col))
        glook = jnp.concatenate(pieces, 0).astype(bf16)
        gtable[...] = dot(glook, query, TN)
        gquery = scale_factor * wide[:, 0:LANES] + gatt.astype(f32) + dot(glook, table)
        gsums[0:8, :] = fold_rows(gquery * unit)
        gsums[8:16, :] = fold_rows(gquery)
        graw = norm_back(gquery * gain_scr[0:1, :], unit, scale, HEAD_DIM) * tile_mask
        gpadded[pl.ds(1 + step * BACK_ROWS, BACK_ROWS), 8 : 8 + cols, :] = graw.reshape(
            BACK_ROWS, cols, LANES
        )
        return carry

    lax.fori_loop(0, chunks, attend, 0, unroll=True)

    key_mask = head_mask(key_total)
    for member, grad in ((1, gkey[...].T * scale_factor), (2, gval[...].T)):
        unit, scale = head_norm_parts(kvraw_ref[(member - 1) * HEADS + head], key_mask)
        base = 16 if member == 1 else 24
        gsums[base : base + 8, :] += fold_rows(grad * unit)
        if member == 2:
            gsums[32:40, :] += fold_rows(grad)
        graw = norm_back(grad * gain_scr[member : member + 1, :], unit, scale, HEAD_DIM) * key_mask
        gkeypad[member - 1, 0:key_rows, 0:key_cols, :] = graw.reshape(key_rows, key_cols, LANES)

    sums_ref[...] = jnp.zeros_like(sums_ref)
    sums_ref[0:63, :] = gtable[0:63, :]
    sums_ref[63:126, :] = gtable[64:127, :]
    for place, base in enumerate((0, 16, 24, 8, 32)):
        sums_ref[126 + place : 127 + place, :] = jnp.sum(gsums[base : base + 8, :], 0, keepdims=True)


def back_weights_kernel(
    norm_ref, padded, gpadded_0, gpadded_1, gkeypad_0, gkeypad_1, sums_0, sums_1, weight_ref, columns_ref, kern_scr,
    gmix_scr, mine_ref, theirs_ref,
    gmixrow, gkern, gweight, gbias, small_scr, dense_scr, block_scr,
):
    tokens, features = norm_ref.shape
    cols = padded.shape[2] - 16
    rows = padded.shape[1] - 2
    tile = CHUNK_ROWS * cols
    chunks = rows // CHUNK_ROWS
    key_cols = cols // 2
    key_rows = rows // 2
    gkern[...] = jnp.zeros_like(gkern)

    def spread_queries(step, carry):
        span = pl.ds(pl.multiple_of(step * tile, tile), tile)
        around = pl.ds(step * CHUNK_ROWS, CHUNK_ROWS + 2)
        for head, gpadded in enumerate((gpadded_0, gpadded_1)):
            total = jnp.zeros((CHUNK_ROWS, cols, LANES), f32)
            own = gpadded[pl.ds(1 + step * CHUNK_ROWS, CHUNK_ROWS), 8 : 8 + cols, :]
            for side in range(3):
                window = gpadded[around, 9 - side : 9 - side + cols, :]
                cells = padded[head, around, 7 + side : 7 + side + cols, :]
                for up in range(3):
                    tap = 3 * up + side
                    total = total + window[2 - up : 2 - up + CHUNK_ROWS] * kern_scr[tap, 0:1, :]
                    gkern[tap] += fold_rows((own * cells[up : up + CHUNK_ROWS]).reshape(tile, LANES))
            flat = total.reshape(tile, LANES).astype(bf16)
            gmix_scr[span, head * LANES : (head + 1) * LANES] = flat
        return carry

    lax.fori_loop(0, chunks, spread_queries, 0, unroll=True)

    evens = pl.ds(0, key_cols, stride=2)
    odds = pl.ds(1, key_cols, stride=2)
    for place in range(2 * HEADS):
        member = 1 + place // HEADS
        taps = [kern_scr[tap, member : member + 1, :] for tap in range(9)]
        gkeypad = (gkeypad_0, gkeypad_1)[place % HEADS].at[place // HEADS]
        left = gkeypad[0 : key_rows + 1, 0:key_cols, :]
        right = gkeypad[0 : key_rows + 1, 1 : 1 + key_cols, :]
        here, below, beside, cross = left[:key_rows], left[1:], right[:key_rows], right[1:]
        gmixrow[:, 0, evens, :] = here * taps[4]
        gmixrow[:, 0, odds, :] = beside * taps[3] + here * taps[5]
        gmixrow[:, 1, evens, :] = below * taps[1] + here * taps[7]
        gmixrow[:, 1, odds, :] = (
            cross * taps[0] + below * taps[2] + beside * taps[6] + here * taps[8]
        )
        lane = (HEADS + place) * LANES
        gmix_scr[:, lane : lane + LANES] = gmixrow[...].reshape(rows * cols, LANES).astype(bf16)
        for side in range(3):
            for up, cells in enumerate(stride_windows(padded, HEADS + place, side, key_rows, key_cols)):
                gkern[9 * member + 3 * up + side] += fold_rows(
                    (here * cells).reshape(key_rows * key_cols, LANES)
                )

    def weigh(step, carry):
        span = pl.ds(pl.multiple_of(step * WEIGH_TILE, WEIGH_TILE), WEIGH_TILE)
        gmix = gmix_scr[span, :]
        gweight[...] = dot(norm_ref[span, :], gmix, TN)
        gbias[...] = fold_rows(gmix.astype(f32))
        return carry

    lax.fori_loop(0, tokens // WEIGH_TILE, weigh, 0, unroll=True)

    bias_row = jnp.sum(gbias[...], 0, keepdims=True)
    weight = weight_ref[...].astype(f32)
    raw = gweight[...]
    lanes = lane_ids((features, LANES))
    norm_sums = jnp.where(
        lanes == 0,
        jnp.sum(weight * raw, 1, keepdims=True),
        jnp.where(lanes == 1, jnp.sum(weight * bias_row, 1, keepdims=True), 0.0),
    )
    norm_rows = jnp.concatenate([norm_sums, jnp.zeros((2 * LANES - features, LANES), f32)], 0).T
    gweight[...] = raw * columns_ref[0:features, 16:17] + columns_ref[0:features, 0:1] * bias_row

    for tap in range(27):
        row = 3 * (tap % 9) + tap // 9
        small_scr[row : row + 1, :] = jnp.sum(gkern[tap], 0, keepdims=True)
    small_scr[27:158, :] = sums_0[0:131, :] + sums_1[0:131, :]
    for place in range(3 * HEADS):
        small_scr[158 + place : 159 + place, :] = bias_row[:, place * LANES : (place + 1) * LANES]
    for place in range(2):
        for head in range(HEADS):
            at = 164 + HEADS * place + head
            small_scr[at : at + 1, :] = head_piece(norm_rows[place : place + 1, :], head * HEAD_DIM)
    weights = jnp.concatenate(
        [gweight[:, place * LANES : place * LANES + HEAD_DIM] for place in range(3 * HEADS)]
        + [jnp.zeros((features, 64), f32)],
        1,
    )
    block_scr[...] = jnp.zeros_like(block_scr)
    stack_blocks(weights, block_scr)
    split_owners(block_scr, mine_ref, theirs_ref, (0, 2, 4, 6))
    count = block_scr.shape[1]
    dense_scr[...] = jnp.zeros_like(dense_scr)
    dense_scr[0:126, :] = small_scr[0:126, :] * head_mask(126)
    beside = lane_ids((42, LANES)) >= HEAD_DIM
    for piece in range(3):
        moved = small_scr[126:168, :]
        moved = pltpu.roll(moved, HEAD_DIM - 32 * piece, 1)
        dense_scr[42 * piece : 42 * (piece + 1), :] += jnp.where(beside, moved, 0.0)
    small = dense_scr[...].astype(bf16)
    mine_ref[4 * count :, :] = small
    theirs_ref[4 * count :, :] = small


def back_images_kernel(img_ref, gmix_ref, gmid_ref, weight_ref, rows_ref, gimg_ref):
    tokens, features = img_ref.shape
    tile = IMAGE_TILE
    block = tokens // 4
    gain_one = rows_ref[16:17, 0:features]

    def finish(step, carry):
        span = pl.ds(pl.multiple_of(step * tile, tile), tile)
        unit, scale = norm_parts(img_ref[span, :].astype(f32), features)
        gnorm = dot(gmix_ref[span, :], weight_ref[...], NT)
        gimg = gmid_ref[span, :].astype(f32) + norm_back(gnorm * gain_one, unit, scale, features)
        for place in range(tile // block):
            gimg_ref[step * (tile // block) + place] = fold_block(
                gimg[place * block : (place + 1) * block, :]
            )
        return carry

    lax.fori_loop(0, tokens // tile, finish, 0, unroll=True)


def halve_kernel(mine_ref, got_ref, keep_ref, send_ref):
    half = keep_ref.shape[0]
    total = (mine_ref[...].astype(f32) + got_ref[...].astype(f32)).astype(bf16)
    keep_ref[...] = total[:half]
    send_ref[...] = total[half:]


def pair_kernel(shared, mine_ref, got_ref, own_ref, msg_1, msg_2, msg_3):
    total = (mine_ref[...].astype(f32) + got_ref[...].astype(f32)).astype(bf16)
    count = (total.shape[0] - shared) // 4
    for place, out in enumerate((own_ref, msg_1, msg_2, msg_3)):
        out[0:count, :] = total[place * count : (place + 1) * count]
        if shared:
            out[count:, :] = total[4 * count :]


def chips_sum(own_ref, got_1, got_2, got_3):
    return (own_ref[...].astype(f32) + got_1[...].astype(f32)) + (
        got_2[...].astype(f32) + got_3[...].astype(f32)
    )


def two_kernel(own_ref, got_ref, out_ref):
    out_ref[...] = (own_ref[...].astype(f32) + got_ref[...].astype(f32)).astype(bf16)


def four_kernel(own_ref, got_1, got_2, got_3, out_ref):
    out_ref[...] = chips_sum(own_ref, got_1, got_2, got_3).astype(bf16)


def pictures_kernel(out_0, out_1, out_2, out_3, gimg_low, out_ref, gimg_ref):
    for shift in range(4):
        gimg_ref[shift] = unfold_block(gimg_low[shift]).astype(f32)
        block = (out_0, out_1, out_2, out_3)[shift][...]
        out_ref[turned(4 - shift)] = unfold_block(block)


def finish_kernel(
    early_0, early_1, late_0, late_1,
    gqkv_ref, gproj_ref, gup_ref, gdown_ref, ggain_ref, gshift_ref, gkern_ref,
    gpgain_ref, gpshift_ref, grelh_ref, grelw_ref,
    small_scr, dense_scr,
):
    share, features = gproj_ref.shape
    hidden = gup_ref.shape[1]
    pieces = hidden // features
    early = early_0[...].astype(f32) + early_1[...].astype(f32)
    early = jnp.concatenate(
        [early[share * i : share * (i + 1), :] for i in range((2 * features + 2 * hidden) // LANES)], 1
    )
    gproj_ref[...] = early[:, 0:features]
    gup_ref[...] = early[:, features : features + hidden]
    for piece in range(pieces):
        start = features + hidden + piece * features
        gdown_ref[piece * share : (piece + 1) * share, :] = early[:, start : start + features]
    start = features + 2 * hidden
    block = early[0:8, start : start + features]
    late = late_0[...].astype(f32) + late_1[...].astype(f32)
    gqkv_ref[...] = jnp.concatenate([late[share * i : share * (i + 1), :] for i in range(5)], 1)[
        :, 0 : 3 * features
    ]
    dense = late[LATE_ROWS : LATE_ROWS + DENSE_ROWS, :]
    small_scr[0:126, :] = dense[0:126, :]
    dense_scr[...] = dense
    lanes = lane_ids((42, LANES))
    rest = jnp.zeros((42, LANES), f32)
    for piece in range(3):
        moved = pltpu.roll(dense_scr[42 * piece : 42 * (piece + 1), :], 32 + 32 * piece, 1)
        rest = jnp.where((lanes >= 32 * piece) & (lanes < 32 * piece + 32), moved, rest)
    small_scr[126:168, :] = rest
    for tap in range(9):
        gkern_ref[tap] = small_scr[3 * tap : 3 * tap + 3, 0:HEAD_DIM]
    gpgain_ref[...] = small_scr[153:156, 0:HEAD_DIM]
    gpshift_ref[...] = small_scr[156:158, 0:HEAD_DIM]
    grelh_ref[...] = small_scr[27:90, 0:HEAD_DIM]
    grelw_ref[...] = small_scr[90:153, 0:HEAD_DIM]
    ggain_ref[1:2, :] = block[0:1, :]
    gshift_ref[1:2, :] = block[1:2, :]
    for head in range(HEADS):
        lanes = slice(head * HEAD_DIM, (head + 1) * HEAD_DIM)
        ggain_ref[0:1, lanes] = small_scr[164 + head : 165 + head, 0:HEAD_DIM]
        gshift_ref[0:1, lanes] = small_scr[166 + head : 167 + head, 0:HEAD_DIM]
        for section in range(3):
            row = 158 + section * HEADS + head
            gshift_ref[2 + section : 3 + section, lanes] = small_scr[row : row + 1, 0:HEAD_DIM]
    gshift_ref[5:6, :] = block[2:3, :]
    gshift_ref[6 : 6 + pieces, :] = block[4 : 4 + pieces, :]
    gshift_ref[6 + pieces : 7 + pieces, :] = block[3:4, :]


LONG = {"back_attend_1": 2 * 10**10}


def call(kernel, name, outs, scratch, flops, limit, spaces, out_spaces, *args):
    place = {"v": pltpu.VMEM, "p": pltpu.VMEM, "h": pltpu.HBM, "a": pl.ANY}
    keep = {"p": pltpu.VMEM, "h": pltpu.HBM}
    args = [
        pltpu.with_memory_space_constraint(a, keep[c]) if c in keep else a for c, a in zip(spaces, args)
    ]
    outs = [keep[c](o.shape, o.dtype) if c in keep else o for c, o in zip(out_spaces, outs)]
    return pl.pallas_call(
        kernel,
        name=name,
        out_shape=outs,
        in_specs=[pl.BlockSpec(memory_space=place[c]) for c in spaces],
        out_specs=[pl.BlockSpec(memory_space=place[c]) for c in out_spaces],
        scratch_shapes=scratch,
        cost_estimate=pl.CostEstimate(flops=LONG.get(name, 1), bytes_accessed=LONG.get(name, 1) // 500, transcendentals=0),
        compiler_params=pltpu.CompilerParams(vmem_limit_bytes=limit * 2**20),
    )(*args)


KA_LIMIT = 36


def whole_image(
    images,
    w_qkv,
    w_proj,
    w_up,
    w_down,
    gains_main,
    shifts_main,
    pool_kernels,
    pool_gains,
    pool_shifts,
    rel_height,
    rel_width,
    cotangent,
):
    owners = lax.axis_size("batch")
    cycle = lax.axis_size("rows")
    image_count, row_count, cols, features = images.shape
    rows = row_count * cycle
    tokens = rows * cols
    hidden = w_up.shape[1]
    share = w_proj.shape[0]
    pieces = hidden // features
    key_total = tokens // 4
    early_used = (2 * features + 2 * hidden) // LANES * share
    early_rows = -(-early_used // 16) * 16
    def shaped(shape, dtype):
        return jax.ShapeDtypeStruct(shape, dtype)

    block = tokens // cycle
    folded = (block * features // LANES, LANES)
    width = 4 * features + 2 * hidden

    def send_on(pieces):
        return list(pieces[:1]) + [
            lax.ppermute(pieces[k], "rows", [(i, (i + k) % cycle) for i in range(cycle)])
            for k in range(1, cycle)
        ]

    def trade(cells, flip):
        return lax.ppermute(cells, "batch", [(i, i ^ flip) for i in range(owners)])

    img = call(
        fold_images_kernel,
        "fold_images",
        [shaped((cycle,) + folded, bf16)],
        [pltpu.VMEM((cycle, block, features), bf16), pltpu.SemaphoreType.DMA((4,))],
        1,
        4,
        "h",
        "v",
        images.reshape(cycle, block, features),
    )[0]
    img, w_qkv = lax.optimization_barrier((img, w_qkv))
    img = lax.all_to_all(img, "rows", 0, 0, tiled=True)
    packed = call(
        pack_kernel,
        "pack",
        [shaped((share, width), bf16)],
        [pltpu.VMEM(w.shape, bf16) for w in (w_qkv, w_proj, w_up, w_down)]
        + [pltpu.SemaphoreType.DMA((4,))],
        10**6,
        4,
        "hhhh",
        "v",
        w_qkv, w_proj, w_up, w_down,
    )[0]
    packed, cotangent = lax.optimization_barrier((packed, cotangent))
    cot_pieces = call(
        fold_kernel,
        "fold",
        [shaped(folded, bf16)] * cycle,
        [
            pltpu.VMEM((cycle, block, features), bf16),
            pltpu.VMEM((cycle,) + folded, bf16),
            pltpu.SemaphoreType.DMA((4,)),
            pltpu.SemaphoreType.DMA((4,)),
        ],
        10**6,
        8,
        "h",
        "a" * 4,
        cotangent.reshape(cycle, block, features),
    )
    img, cot_pieces, *shards = lax.optimization_barrier(
        (img, cot_pieces, *[trade(packed, flip) for flip in (2, 4, 6)])
    )
    own = jnp.stack([packed, *shards])
    other = trade(own, 1)
    taps = pool_kernels.transpose(1, 0, 2)
    small = (gains_main, shifts_main, taps, pool_gains, pool_shifts, rel_height, rel_width)
    wide, full_proj, full_up, full_down, biases, lines, columns, taps_wide, pool_lines, ahead, behind = call(
        functools.partial(weights_kernel, owners),
        "weights",
        [
            shaped((features, 3 * HEADS * LANES), bf16),
            shaped((HEADS * LANES, features), bf16),
            shaped((features, hidden), bf16),
            shaped((hidden, features), bf16),
            shaped((8, hidden), f32),
            shaped((24, 2 * LANES), f32),
            shaped((2 * LANES, LANES), f32),
            shaped((9, 8, LANES), f32),
            shaped((8, LANES), f32),
            shaped((LANES, LANES), bf16),
            shaped((LANES, LANES), bf16),
        ],
        [pltpu.VMEM((features, width), f32), pltpu.VMEM((hidden, features), f32)]
        + [pltpu.VMEM(a.shape, bf16) for a in small]
        + [pltpu.VMEM((LANES, LANES), f32), pltpu.SemaphoreType.DMA((7,))],
        10**6,
        12,
        "vv" + "h" * 7,
        "v" * 11,
        own, other, *small,
    )
    cot_pieces = send_on(cot_pieces)
    whole = [
        shaped((3 * HEADS, rows + 2, cols + 16, LANES), f32),
        shaped((HEADS, tokens, LANES), f32),
        shaped((HEADS, tokens, LANES), f32),
        shaped((2 * HEADS, key_total, LANES), f32),
        shaped((HEADS, tokens, key_total), bf16),
        shaped((tokens, HEADS * LANES), bf16),
    ]
    img, norm_one, padded, qunit, qscale, kvraw, soft, att, keys, values = call(
        attend_kernel,
        "attend",
        [shaped((tokens, features), bf16)] * 2 + whole + [shaped((HEADS, key_total, LANES), bf16)] * 2,
        [
            pltpu.VMEM((HEADS, tokens, LANES), bf16),
            pltpu.VMEM((HEADS, key_total, 2 * LANES), bf16),
        ],
        10**10,
        KA_LIMIT,
        "v" * 7,
        "p" * 10,
        img, wide, biases, lines, taps_wide, pool_lines, ahead,
    )
    *out_pieces, normed, unit, scale, active, slope = call(
        feed_ahead_kernel,
        "feed_ahead",
        [shaped(folded, bf16)] * cycle
        + [
            shaped((tokens, features), bf16),
            shaped((tokens, features), f32),
            shaped((tokens, features), f32),
            shaped((tokens, hidden), bf16),
            shaped((tokens, hidden), f32),
        ],
        [pltpu.VMEM((cycle,) + folded, bf16), pltpu.SemaphoreType.DMA((4,))],
        1,
        36,
        "pp" + "v" * 5,
        "a" * cycle + "p" * 5,
        img, att, full_proj, full_up, full_down, biases, lines,
    )
    gmid, gatt, mine, theirs = call(
        functools.partial(feed_back_kernel, owners),
        "feed_back",
        [shaped((tokens, features), bf16), shaped((tokens, HEADS * LANES), bf16)]
        + [shaped((4 * early_rows, LANES), bf16)] * 2,
        [
            pltpu.VMEM((features, hidden), f32),
            pltpu.VMEM((features, hidden), f32),
            pltpu.VMEM((HEADS * LANES, features), f32),
            pltpu.VMEM((8, hidden), f32),
            pltpu.VMEM((32, features), f32),
            pltpu.VMEM((owners, early_rows, LANES), f32),
            pltpu.VMEM((cycle,) + folded, bf16),
            pltpu.SemaphoreType.DMA((4,)),
        ],
        1,
        36,
        "p" + "a" * 4 + "p" * 5 + "v" * 4,
        "pp" + "vv",
        att, *cot_pieces, normed, unit, scale, active, slope, full_proj, full_up, full_down, lines,
    )

    def halved(mine, got):
        return call(
            halve_kernel,
            "halve",
            [shaped((mine.shape[0] // 2, LANES), bf16)] * 2,
            [],
            10**6,
            4,
            "vv",
            "vv",
            mine, got,
        )

    got = trade(theirs, 1)

    def back_attend(head, behind):
        return call(
            functools.partial(back_attend_kernel, head),
            f"back_attend_{head}",
            [
                shaped((rows + 2, cols + 16, LANES), f32),
                shaped((2, rows // 2 + 1, cols // 2 + 8, LANES), f32),
                shaped((136, LANES), f32),
            ],
            [
                pltpu.VMEM((key_total, 2 * LANES), bf16),
                pltpu.VMEM((LANES, LANES), f32),
                pltpu.VMEM((LANES, key_total), f32),
                pltpu.VMEM((LANES, key_total), f32),
                pltpu.VMEM((40, LANES), f32),
            ],
            10**10,
            30,
            "p" * 7 + "vv",
            "ppp",
            qunit, qscale, kvraw, soft, gatt, keys, values, pool_lines, behind,
        )

    gpadded_0, gkeypad_0, sums_0 = back_attend(0, behind)
    got, gkeypad_0, behind = lax.optimization_barrier((got, gkeypad_0, behind))
    early, away = halved(mine, got)
    away = trade(away, 2)
    out_pieces = send_on(out_pieces)
    gpadded_1, gkeypad_1, sums_1 = back_attend(1, behind)
    gmix, mine, theirs = call(
        back_weights_kernel,
        "back_weights",
        [shaped((tokens, 3 * HEADS * LANES), bf16)]
        + [shaped((4 * LATE_ROWS + DENSE_ROWS, LANES), bf16)] * 2,
        [
            pltpu.VMEM((rows // 2, 2, cols, LANES), f32),
            pltpu.VMEM((27, 8, LANES), f32),
            pltpu.VMEM((features, 3 * HEADS * LANES), f32),
            pltpu.VMEM((8, 3 * HEADS * LANES), f32),
            pltpu.VMEM((SMALL_ROWS, LANES), f32),
            pltpu.VMEM((DENSE_ROWS, LANES), f32),
            pltpu.VMEM((owners, LATE_ROWS, LANES), f32),
        ],
        10**10,
        30,
        "p" + "p" * 7 + "v" * 3,
        "pvv",
        norm_one, padded, gpadded_0, gpadded_1, gkeypad_0, gkeypad_1, sums_0, sums_1, wide, columns, taps_wide,
    )

    def summed(kernel, *pieces):
        return call(
            kernel,
            "sum_four" if len(pieces) == 4 else "sum_two",
            [shaped(pieces[0].shape, bf16)],
            [],
            1,
            4,
            "v" * len(pieces),
            "v",
            *pieces,
        )[0]

    def ring_trade(cells, flip):
        return lax.ppermute(cells, "rows", [(i, i ^ flip) for i in range(cycle)])

    away, out_pieces, gmix, mine, theirs = lax.optimization_barrier(
        (away, out_pieces, gmix, mine, theirs)
    )
    early, away = halved(early, away)
    away = trade(away, 4)
    got = trade(theirs, 1)
    gimg = call(
        back_images_kernel,
        "back_images",
        [shaped((cycle,) + folded, bf16)],
        [],
        10**10,
        24,
        "pppvv",
        "v",
        img, gmix, gmid, wide, lines,
    )[0]
    got, gimg = lax.optimization_barrier((got, gimg))
    gimg = lax.all_to_all(gimg, "rows", 0, 0, tiled=True)
    early = summed(two_kernel, early, away)
    early = summed(two_kernel, early, ring_trade(early, 1))
    away = ring_trade(early, 2)
    own, *apart = call(
        functools.partial(pair_kernel, DENSE_ROWS),
        "pair",
        [shaped((LATE_ROWS + DENSE_ROWS, LANES), bf16)] * 4,
        [],
        10**6,
        4,
        "vv",
        "vvvv",
        mine, got,
    )
    late = summed(four_kernel, own, *[trade(apart[k], 2 * k + 2) for k in range(3)])
    late = summed(two_kernel, late, ring_trade(late, 1))
    late_away = ring_trade(late, 2)
    output, grad_images = call(
        pictures_kernel,
        "pictures",
        [shaped((cycle, block, features), bf16), shaped((cycle, block, features), f32)],
        [],
        1,
        16,
        "v" * 5,
        "v" * 2,
        *out_pieces, gimg,
    )
    late, output, grad_images = lax.optimization_barrier((late, output, grad_images))
    grads = call(
        finish_kernel,
        "finish",
        [
            shaped((share, 3 * features), f32),
            shaped((share, features), f32),
            shaped((share, hidden), f32),
            shaped((share * pieces, features), f32),
            shaped(gains_main.shape, f32),
            shaped(shifts_main.shape, f32),
            shaped(taps.shape, f32),
            shaped(pool_gains.shape, f32),
            shaped(pool_shifts.shape, f32),
            shaped(rel_height.shape, f32),
            shaped(rel_width.shape, f32),
        ],
        [pltpu.VMEM((SMALL_ROWS, LANES), f32), pltpu.VMEM((DENSE_ROWS, LANES), f32)],
        10**8,
        16,
        "v" * 4,
        "v" * 11,
        early, away, late, late_away,
    )
    grads = list(grads)
    grads[6] = grads[6].transpose(1, 0, 2)
    return (output.reshape(images.shape), grad_images.reshape(images.shape), *grads)

def per_device(images, *rest):
    cycle = lax.axis_size("rows")
    image_count, row_count, cols, _ = images.shape
    fits = image_count == cycle and row_count * cycle == 32 and cols == 32
    return whole_image(images, *rest) if fits else row_sharded(images, *rest)


def solution(mesh):
    return jax.shard_map(
        per_device,
        mesh=mesh,
        in_specs=(
            P("batch", "rows", None, None),
            P("batch", None),
            P("batch", None),
            P("batch", None),
            P("batch", None),
            P(),
            P(),
            P(),
            P(),
            P(),
            P(),
            P(),
            P("batch", "rows", None, None),
        ),
        out_specs=(
            P("batch", "rows", None, None),
            P("batch", "rows", None, None),
            P("batch", None),
            P("batch", None),
            P("batch", None),
            P("batch", None),
            P(),
            P(),
            P(),
            P(),
            P(),
            P(),
            P(),
        ),
        check_vma=False,
    )
```
